32 devices in a mesh: tok: 8 (over z, x), head: 4 (over y, core).
Axes of the slice: x: 2, y: 2, z: 4, core: 2. Of those that a mesh axis runs over, the one named last changes fastest.
Arguments:
- tokens: bfloat16 [2048, 2880], P(('tok', 'head')), may hold values from -6 to 6
- lengths: int32 [4], replicated, may hold values from 1 to 1024, 1920 in all
- norm_gain_attn: float32 [2880], replicated, may hold values from 0.1 to 1.9
- query_key_value_weight: bfloat16 [2880, 5120], P(None, 'head'), may hold values from -0.109375 to 0.109375
- sinks: float32 [64], P('head'), may hold values from 1 to 6
- w_out_attn: bfloat16 [4096, 2880], P('head'), may hold values from -0.09375 to 0.09375
- norm_gain_moe: float32 [2880], replicated, may hold values from 0.1 to 1.9
- routes: int32 [2048, 4], P(('tok', 'head')), may hold values from 0 to 31, all different within a row; in each aligned block of 64 rows (0 to 63, 64 to 127, ...) at most 10 rows name the same one
- gates: float32 [2048, 4], P(('tok', 'head')), may hold values from 0.1 to 1
- w_in: bfloat16 [32, 2880, 5760], P(('tok', 'head')), may hold values from -0.109375 to 0.109375
- w_down: bfloat16 [32, 2880, 2880], P(('tok', 'head')), may hold values from -0.109375 to 0.109375
- page_table: int32 [128], replicated, may hold values from 0 to 127, as said below
Outputs:
- hidden_out: bfloat16 [2048, 2880], P(('tok', 'head'))
- kv_cache: bfloat16 [8, 128, 16, 128], P('head', 'tok')
The draws below stay inside these ranges and needn't reach their ends.
Inputs may be any that keep to these rules, and one draw needn't show every extreme that they name: `routes`: every row names 4 different experts. In each aligned block of 64 rows no expert is named by more than 10 rows, and in every draw some block has an expert named by exactly 10 rows. `lengths`: they sum to 1920, and the longest is exactly 1024. `page_table`: A permutation. Of the 16 logical pages in each aligned block of 16, exactly 2 map into each aligned block of 16 physical pages.
All inputs are finite; a program needn't handle non-finite values.
Results may differ from the reference program's by a relative error of at most 0.018.
Values may be sent and summed in bfloat16 or wider, within the bound.
No kernel may reach another device: no remote copies, remote signals or barrier semaphores. Data moves between devices by JAX's collectives and lax.ppermute only.
A program may use at most 128 MiB of HBM per device.

```python
import math
import jax
import jax.numpy as jnp
import numpy as np
from jax import lax

MODEL_WIDTH = 2880
NQ = 64
KEY_VALUE_HEADS = 8
HEAD_SIZE = 64
EXPERTS = 32
TOPK = 4
FF = 2880
ATTEND_WINDOW = 128
NSEQ = 4
PAGE_TOKENS = 16
QUERY_PER_KEY = 8
SPLIT = 1
FFS = 2880
PACKED_TOKENS = 2048
ROWS = 64
VALID = 1920
LONGEST = 1024
CAP = 10
CACHE_PAGES = 128
PAGES_DEV = 16
PAGE_SHARE = 2


def shuffle(subkey):
    return jax.random.permutation(subkey, PAGES_DEV)


def draw_page_table(key, part):
    blocks = CACHE_PAGES // PAGES_DEV
    source_keys = jax.random.split(jax.random.fold_in(key, 11), blocks)
    target_keys = jax.random.split(jax.random.fold_in(key, 12), blocks)
    spread = jax.vmap(shuffle)(source_keys).astype(jnp.int32)
    landing = jax.vmap(shuffle)(target_keys).astype(jnp.int32)
    target = spread // PAGE_SHARE
    within = spread % PAGE_SHARE
    anchor = jnp.arange(blocks, dtype=jnp.int32)[:, None]
    placed_slot = landing[target, anchor * PAGE_SHARE + within]
    return (target * PAGES_DEV + placed_slot).reshape(-1).astype(jnp.int32)


def block_scale(key, dims, shards, least, high):
    gain, own = 1.0, jax.random.fold_in(key, 6)
    for dim, blocks in shards:
        heights = jnp.exp(jax.random.uniform(jax.random.fold_in(own, dim), (blocks,), jnp.float32, least / len(shards), high / len(shards)))
        gain = gain * jnp.repeat(heights, dims[dim] // blocks).reshape([-1 if axis == dim else 1 for axis in range(len(dims))])
    return gain


def length_profile(count, total, bound, lean):
    weights = [(1 << 20) // math.isqrt(grade ** lean) + 1 for grade in range(2, count + 1)]
    rest, holding = total - bound - (count - 1), [1] * (count - 1)
    while rest > 0:
        movable = [i for i in range(count - 1) if holding[i] < bound]
        mass, left = sum([weights[i] for i in movable]), rest
        for i in movable:
            addition = min(bound - holding[i], max(1, left * weights[i] // mass), rest)
            holding[i] = holding[i] + addition
            rest = rest - addition
    return np.array([bound] + holding)


def ragged_sizes(rng, amount, total, limit, slope):
    if amount == 2:
        one = jax.random.randint(rng, (), max(1, total - limit), min(limit, total - 1) + 1)
        return jnp.stack([one, total - one])
    tallies = jnp.asarray(length_profile(amount, total, limit, slope), jnp.int32)
    couples = (amount - 1) // 2
    giver, taker = tallies[1:1 + 2 * couples:2], tallies[2:2 + 2 * couples:2]
    slack = jnp.minimum(giver - 1, limit - taker)
    moved = jax.random.randint(jax.random.fold_in(rng, 1), (couples,), 0, 1 << 20) % (slack + 1)
    tallies = tallies.at[1:1 + 2 * couples:2].set(giver - moved).at[2:2 + 2 * couples:2].set(taker + moved)
    return tallies[jax.random.permutation(jax.random.fold_in(rng, 2), amount)]


def deal_out(key, own, number, rows, number_of, top, limit, skew):
    order = jax.random.permutation(key, number_of)
    crowded, common = load_shares(number_of, rows * top, limit, skew, True), load_shares(number_of, rows * top, limit, skew, False)
    places = jnp.arange(number_of)

    def named(sizes, offset_by):
        used = int((sizes > 0).sum())
        fixed = max(1, used // 4)
        moved = fixed + (places - fixed + offset_by * (used - fixed)) % max(1, number_of - fixed)
        return jnp.zeros((number_of,), jnp.int32).at[order[jnp.where(places < fixed, places, moved)]].set(jnp.asarray(sizes, jnp.int32))

    sizes = jnp.where(number % 4 == 0, named(crowded, number // 4), named(common, number - number // 4 - 1))
    mixed = jax.random.permutation(jax.random.fold_in(own, 3), number_of)
    giver, receiver = mixed[0:number_of // 2 * 2:2], mixed[1:number_of // 2 * 2:2]
    slack = jnp.minimum(sizes[giver] - 1, limit - sizes[receiver]) // 2
    slack = jnp.where((giver == order[0]) | (receiver == order[0]) | (sizes[receiver] == 0), 0, jnp.maximum(slack, 0))
    moved = jax.random.randint(jax.random.fold_in(own, 4), (number_of // 2,), 0, 1 << 20) % (slack + 1)
    sizes = sizes.at[giver].add(-moved).at[receiver].add(moved)
    items = jnp.searchsorted(jnp.cumsum(sizes), jnp.arange(rows * top), side="right").astype(jnp.int32)
    grid = items.reshape(top, rows).T
    grid = grid[jax.random.permutation(jax.random.fold_in(own, 1), rows)]
    offset_by = jax.random.randint(jax.random.fold_in(own, 2), (rows, 1), 0, top)
    return jnp.take_along_axis(grid, (jnp.arange(top)[None, :] + offset_by) % top, axis=1)


def load_shares(count, total, limit, lean, full):
    portions = [(1 << 20) // math.isqrt(standing ** lean) + 1 for standing in range(1, count + 1)]
    largest = limit if full else min(limit, max(-(-total // count), total * portions[0] // sum(portions)))
    least = 1 if total - largest >= count - 1 else 0
    holding, surplus = [largest] + [least] * (count - 1), total - largest - least * (count - 1)
    while surplus > 0:
        movable = [i for i in range(1, count) if holding[i] < largest] or [i for i in range(1, count) if holding[i] < limit]
        mass, left = sum([portions[i] for i in movable]), surplus
        for i in movable:
            addition = min(limit - holding[i], max(1, left * portions[i] // mass), surplus)
            holding[i] = holding[i] + addition
            surplus = surplus - addition
    return np.array(holding)


def normal_values(own_key, extent, width, reach, cuts=(), kind=jnp.bfloat16):
    array = jax.random.normal(own_key, extent, jnp.float32) * width
    if len(cuts) > 0:
        array = block_scale(own_key, extent, cuts, -0.22, 0.18) * array
    return jnp.clip(array, min=-reach, max=reach).astype(kind)


def setup_inputs(seed: int = 0) -> dict:
    seeds = jax.random.split(jax.random.key(seed), 13)
    tokens = normal_values(seeds[0], (PACKED_TOKENS, MODEL_WIDTH), 1.0, 6.0, ((0, 32),))
    lengths = ragged_sizes(seeds[1], NSEQ, VALID, LONGEST, 2).astype(jnp.int32)
    norm_gain_attn = jnp.clip(1.0 + 0.18 * jax.random.normal(seeds[2], (MODEL_WIDTH,), jnp.float32), 0.1, 1.9)
    query_key_value_weight = normal_values(seeds[3], (MODEL_WIDTH, KEY_VALUE_HEADS * (QUERY_PER_KEY + 2) * HEAD_SIZE), MODEL_WIDTH ** -0.5, 0.109375, ((1, 4),))
    sinks = jnp.clip(1.0 + 5.0 * jax.random.uniform(seeds[4], (NQ,), jnp.float32) ** block_scale(seeds[4], (NQ,), ((0, 4),), -0.2, 0.2), 1.0, 6.0)
    w_out_attn = normal_values(seeds[5], (NQ * HEAD_SIZE, MODEL_WIDTH), (NQ * HEAD_SIZE) ** -0.5, 0.09375, ((0, 4),))
    norm_gain_moe = jnp.clip(1.0 + 0.18 * jax.random.normal(seeds[6], (MODEL_WIDTH,), jnp.float32), 0.1, 1.9)
    routes_keys = jax.random.split(jax.random.fold_in(seeds[7], 1), PACKED_TOKENS // ROWS)
    routes_turns = jax.random.permutation(jax.random.fold_in(seeds[7], 3), PACKED_TOKENS // ROWS)
    routes = jax.vmap(lambda own, number: deal_out(jax.random.fold_in(seeds[7], 2), own, number, ROWS, EXPERTS, TOPK, CAP, 1))(routes_keys, routes_turns).reshape((PACKED_TOKENS, TOPK))
    gates = jnp.clip(0.1 + 0.9 * jax.random.uniform(seeds[8], (PACKED_TOKENS, TOPK), jnp.float32) ** block_scale(seeds[8], (PACKED_TOKENS, TOPK), ((0, 32),), -0.2, 0.2), 0.1, 1.0)
    w_in = normal_values(seeds[9], (EXPERTS * SPLIT, MODEL_WIDTH, 2 * FFS), MODEL_WIDTH ** -0.5, 0.109375, ((0, 32),))
    w_down = normal_values(seeds[10], (EXPERTS * SPLIT, FFS, MODEL_WIDTH), FF ** -0.5, 0.109375, ((0, 32),))
    page_table = draw_page_table(jax.random.fold_in(seeds[12], 71), 0)
    return dict(tokens=tokens, lengths=lengths, norm_gain_attn=norm_gain_attn, query_key_value_weight=query_key_value_weight, sinks=sinks, w_out_attn=w_out_attn, norm_gain_moe=norm_gain_moe, routes=routes, gates=gates, w_in=w_in, w_down=w_down, page_table=page_table)


EPSILON = 1e-05
ROPE_BASE = 150000.0
GLU_ALPHA = 1.702

def to_wide(values):
    return lax.optimization_barrier(values).astype(jnp.float32)

def normalize(values, gain_vec):
    wide = values.astype(jnp.float32)
    inv_rms = lax.rsqrt(lax.optimization_barrier(jnp.mean(wide * wide, axis=-1, keepdims=True)) + EPSILON)
    return wide * inv_rms * gain_vec

def segment_table(lengths, row_index):
    seq_ends = jnp.cumsum(lengths).astype(jnp.int32)
    starts = jnp.concatenate([jnp.zeros((1,), jnp.int32), seq_ends])
    segment = lax.optimization_barrier(jnp.sum((row_index[:, None] >= seq_ends[None, :]).astype(jnp.int32), axis=1)).astype(jnp.int32)
    onehot = segment[:, None] == jnp.arange(starts.shape[0], dtype=jnp.int32)[None, :]
    seg_start = lax.optimization_barrier(jnp.sum(jnp.where(onehot, starts[None, :], 0), axis=1)).astype(jnp.int32)
    return (segment, (row_index - seg_start).astype(jnp.int32))

def rotate(values, positions):
    half_dim = values.shape[-1] // 2
    inv_freq = jnp.exp(jnp.arange(half_dim, dtype=jnp.float32) * (-2.0 * math.log(ROPE_BASE) / values.shape[-1]))
    angles = positions.astype(jnp.float32)[:, None] * inv_freq[None, :]
    view_shape = (angles.shape[0],) + (1,) * (values.ndim - 2) + (half_dim,)
    cos_table = jnp.cos(angles).reshape(view_shape)
    sin_table = jnp.sin(angles).reshape(view_shape)
    lower_half = values[..., :half_dim]
    upper_half = values[..., half_dim:]
    return jnp.concatenate([lower_half * cos_table - upper_half * sin_table, upper_half * cos_table + lower_half * sin_table], axis=-1)

def band_mask(query_index, key_index, query_segs, key_segs, window):
    nblocks = query_index.shape[0] // window
    query_pos = query_index.reshape(nblocks, window)
    query_seg = query_segs.reshape(nblocks, window)
    key_grid = key_index.reshape(nblocks + 1, window)
    seg_grid = key_segs.reshape(nblocks + 1, window)
    key_pos = jnp.concatenate([key_grid[:-1], key_grid[1:]], axis=1)
    key_seg = jnp.concatenate([seg_grid[:-1], seg_grid[1:]], axis=1)
    distance = query_pos[:, :, None] - key_pos[:, None, :]
    allowed = (query_seg[:, :, None] == key_seg[:, None, :]) & (query_seg < NSEQ)[:, :, None]
    allowed = allowed & (key_pos >= 0)[:, None, :] & (distance >= 0) & (distance < window)
    return allowed

def reference(tokens, lengths, norm_gain_attn, query_key_value_weight, sinks, w_out_attn, norm_gain_moe, routes, gates, w_in, w_down, page_table):
    row_index = jnp.arange(PACKED_TOKENS, dtype=jnp.int32)
    segment, positions = segment_table(lengths, row_index)
    normed_input = normalize(tokens, norm_gain_attn).astype(jnp.bfloat16)
    projected_rows = jnp.dot(normed_input, query_key_value_weight, preferred_element_type=jnp.float32).reshape(PACKED_TOKENS, KEY_VALUE_HEADS, QUERY_PER_KEY + 2, HEAD_SIZE)
    query_rows = (rotate(projected_rows[:, :, :QUERY_PER_KEY], positions) * HEAD_SIZE ** (-0.5)).astype(jnp.bfloat16)
    key_rot = rotate(projected_rows[:, :, QUERY_PER_KEY], positions)
    key_value_pairs = jnp.concatenate([key_rot, projected_rows[:, :, QUERY_PER_KEY + 1]], axis=-1).astype(jnp.bfloat16)
    padded_rows = jnp.concatenate([jnp.zeros((ATTEND_WINDOW, KEY_VALUE_HEADS, 2 * HEAD_SIZE), jnp.bfloat16), key_value_pairs], axis=0)
    key_index = jnp.arange(PACKED_TOKENS + ATTEND_WINDOW, dtype=jnp.int32) - ATTEND_WINDOW
    key_segs, _ = segment_table(lengths, key_index)
    nblocks = PACKED_TOKENS // ATTEND_WINDOW
    allowed = band_mask(row_index, key_index, segment, key_segs, ATTEND_WINDOW)

    def single_group(operands):
        group_queries, group_pairs, group_sinks = operands
        query_blocks = to_wide(group_queries).reshape(nblocks, ATTEND_WINDOW, QUERY_PER_KEY, HEAD_SIZE)
        pair_grid = to_wide(group_pairs).reshape(nblocks + 1, ATTEND_WINDOW, 2 * HEAD_SIZE)
        key_band = jnp.concatenate([pair_grid[:-1], pair_grid[1:]], axis=1)
        scores = jnp.einsum('bqnh,bkh->bnqk', query_blocks, key_band[..., :HEAD_SIZE])
        weights = jnp.where(allowed[:, None], jnp.exp(scores), 0.0)
        totals = lax.optimization_barrier(jnp.sum(weights, axis=-1, keepdims=True)) + jnp.exp(group_sinks)[None, :, None, None]
        probs_bf = (weights / totals).astype(jnp.bfloat16)
        outputs = jnp.einsum('bnqk,bkh->bqnh', to_wide(probs_bf), key_band[..., HEAD_SIZE:])
        return outputs.astype(jnp.bfloat16).reshape(PACKED_TOKENS, QUERY_PER_KEY * HEAD_SIZE)
    group_split = lax.map(single_group, (jnp.transpose(query_rows, (1, 0, 2, 3)), jnp.transpose(padded_rows, (1, 0, 2)), sinks.reshape(KEY_VALUE_HEADS, QUERY_PER_KEY)))
    attended = jnp.transpose(group_split, (1, 0, 2)).reshape(PACKED_TOKENS, NQ * HEAD_SIZE)
    resid = tokens.astype(jnp.float32) + jnp.dot(attended, w_out_attn, preferred_element_type=jnp.float32)
    moe_in = normalize(resid, norm_gain_moe).astype(jnp.bfloat16)
    is_live = segment < NSEQ
    expert_ids = jnp.arange(EXPERTS, dtype=jnp.int32)
    naming = routes[:, :, None] == expert_ids[None, None, :]
    routed = (jnp.any(naming, axis=1) & is_live[:, None]).astype(jnp.int32)
    sources = PACKED_TOKENS // ROWS
    slot_rank = (jnp.cumsum(routed.reshape(sources, ROWS, EXPERTS), axis=1).astype(jnp.int32) - 1).reshape(PACKED_TOKENS, EXPERTS)
    slot_ids = jnp.arange(CAP, dtype=jnp.int32)
    placed = ((routed == 1)[:, :, None] & (slot_rank[:, :, None] == slot_ids[None, None, :])).reshape(sources, ROWS, EXPERTS, CAP)
    local_ids = jnp.arange(ROWS, dtype=jnp.int32)
    local_row = lax.optimization_barrier(jnp.sum(jnp.where(placed, local_ids[None, :, None, None], 0), axis=1)).astype(jnp.int32)
    global_row = (local_row + (jnp.arange(sources, dtype=jnp.int32) * ROWS)[:, None, None]).astype(jnp.int32)
    filled = jnp.any(placed, axis=1)
    weighted = jnp.where(is_live[:, None], gates, 0.0)
    expert_gate = lax.optimization_barrier(jnp.sum(jnp.where(naming, weighted[:, :, None], 0.0), axis=1))

    def one_expert(carry, operands):
        expert_in, expert_down, rows_here, filled_here, gate_here = operands
        rows_flat = rows_here.reshape(-1)
        mask_flat = filled_here.reshape(-1)
        inputs = jnp.where(mask_flat[:, None], moe_in[rows_flat], jnp.zeros((), jnp.bfloat16))
        combined = jnp.zeros((rows_flat.shape[0], MODEL_WIDTH), jnp.float32)
        for shard in range(SPLIT):
            gate_up = jnp.dot(inputs, expert_in[shard], preferred_element_type=jnp.float32)
            gate_part = gate_up[:, :FFS]
            up_part = gate_up[:, FFS:]
            activated = ((up_part + 1.0) * gate_part * jax.nn.sigmoid(GLU_ALPHA * gate_part)).astype(jnp.bfloat16)
            partial_out = jnp.dot(activated, expert_down[shard], preferred_element_type=jnp.float32).astype(jnp.bfloat16)
            combined = combined + to_wide(partial_out)
        scale_rows = jnp.where(mask_flat, gate_here[rows_flat], 0.0)
        return (carry.at[rows_flat].add(scale_rows[:, None] * combined), None)
    expert_sum, _ = lax.scan(one_expert, jnp.zeros((PACKED_TOKENS, MODEL_WIDTH), jnp.float32), (w_in.reshape(EXPERTS, SPLIT, MODEL_WIDTH, 2 * FFS), w_down.reshape(EXPERTS, SPLIT, FFS, MODEL_WIDTH), jnp.transpose(global_row, (1, 0, 2)), jnp.transpose(filled, (1, 0, 2)), jnp.transpose(expert_gate)))
    hidden_out = (resid + expert_sum).astype(jnp.bfloat16)
    page_row_slots = key_value_pairs.reshape(CACHE_PAGES, PAGE_TOKENS, KEY_VALUE_HEADS, 2 * HEAD_SIZE)
    cache = jnp.zeros_like(page_row_slots).at[page_table].set(page_row_slots)
    kv_cache = jnp.transpose(cache, (2, 0, 1, 3))
    return (hidden_out, kv_cache)
```

```python
import functools
import math

import jax
import jax.numpy as jnp
from jax import lax
from jax.experimental import pallas as pl
from jax.experimental.pallas import tpu as pltpu
from jax.sharding import PartitionSpec as P

MODEL_WIDTH = 2880
HEAD_SIZE = 64
EXPERTS = 32
ATTEND_WINDOW = 128
NSEQ = 4
PAGE_TOKENS = 16
QUERY_PER_KEY = 8


EPSILON = 1e-05
ROPE_BASE = 150000.0
GLU_ALPHA = 1.702

LANES = 128
MAIN_SLOTS = 8
PIECE = 768
PIECES = 4
EXTRA_AT = 2944
IN_TILE = 1152
MIB = 1 << 20


def passed_along(array, axis, by):
    peers = lax.axis_size(axis)
    pairs = [(i, i + by) for i in range(peers) if 0 <= i + by < peers]
    return lax.ppermute(array, axis, pairs)


def segment_ends(lengths_ref):
    ends, end = [], 0
    for k in range(NSEQ):
        end = end + lengths_ref[k]
        ends.append(end)
    return ends


def segment_of(index, ends):
    segment = jnp.zeros_like(index)
    for end in ends:
        segment = segment + jnp.where(index >= end, 1, 0)
    return segment


def rope_tables(index, ends):
    start = jnp.zeros_like(index)
    for end in ends:
        start = jnp.where(index >= end, end, start)
    half = HEAD_SIZE // 2
    lane = lax.broadcasted_iota(jnp.int32, index.shape, 1)
    inv_freq = jnp.exp(
        (lane % half).astype(jnp.float32) * (-2.0 * math.log(ROPE_BASE) / HEAD_SIZE)
    )
    angles = (index - start).astype(jnp.float32) * inv_freq
    low = lane % HEAD_SIZE < half
    sin = jnp.sin(angles)
    return jnp.cos(angles), jnp.where(low, -sin, sin), low, lane


def qkv_kernel(step, chips, ids_ref, lengths_ref, own_ref, other_ref, gain_ref, w_ref, *refs):
    q_ref, kv_ref, xn_ref, cos_ref, sin_ref = refs[-5:]
    rows = own_ref.shape[0]
    core, chip, shard = ids_ref[0], (ids_ref[1] + chips - step) % chips, ids_ref[2]

    @pl.when(pl.program_id(0) == 0)
    def _():
        for at, ref in ((core, own_ref), (1 - core, other_ref)):
            wide = ref[...].astype(jnp.float32)
            inv_rms = lax.rsqrt(jnp.mean(wide * wide, axis=-1, keepdims=True) + EPSILON)
            normed = (wide * inv_rms * gain_ref[...][None]).astype(jnp.bfloat16)
            xn_ref[pl.ds(pl.multiple_of(at * rows, 16), rows), :] = normed
        first = (shard * chips + chip) * 2 * rows
        index = first + lax.broadcasted_iota(jnp.int32, cos_ref.shape, 0)
        cos, sin, _, _ = rope_tables(index, segment_ends(lengths_ref))
        cos_ref[...] = cos
        sin_ref[...] = sin

    projected = jnp.dot(xn_ref[...], w_ref[...], preferred_element_type=jnp.float32)
    cos, sin = cos_ref[...], sin_ref[...]
    lane = lax.broadcasted_iota(jnp.int32, cos.shape, 1)
    low = lane % HEAD_SIZE < HEAD_SIZE // 2

    def turned(u):
        return jnp.where(low, pltpu.roll(u, LANES - 32, 1), pltpu.roll(u, 32, 1))

    for b in range(QUERY_PER_KEY // 2):
        u = projected[:, b * LANES : (b + 1) * LANES]
        q_ref[:, b * LANES : (b + 1) * LANES] = (
            (u * cos + turned(u) * sin) * HEAD_SIZE ** (-0.5)
        ).astype(jnp.bfloat16)
    u = projected[:, QUERY_PER_KEY * HEAD_SIZE :]
    rotated = u * cos + turned(u) * sin
    kv_ref[...] = jnp.where(lane < HEAD_SIZE, rotated, u).astype(jnp.bfloat16)


def project(ids, lengths, step, chips, own, other, gain, weight, earlier):
    rows, width = own.shape
    columns = weight.shape[1]
    group = (QUERY_PER_KEY + 2) * HEAD_SIZE
    qs, kvs = QUERY_PER_KEY * HEAD_SIZE, 2 * HEAD_SIZE
    groups = columns // group
    whole = lambda g, ids: (0, 0)
    by_group = lambda g, ids: ((ids[1] + chips - step) % chips, g)
    return pl.pallas_call(
        functools.partial(qkv_kernel, step, chips),
        grid_spec=pltpu.PrefetchScalarGridSpec(
            num_scalar_prefetch=1,
            grid=(groups,),
            in_specs=[
                pl.BlockSpec(memory_space=pltpu.SMEM),
                pl.BlockSpec((rows, width), whole),
                pl.BlockSpec((rows, width), whole),
                pl.BlockSpec((width,), lambda g, ids: (0,)),
                pl.BlockSpec((width, group), lambda g, ids: (0, g)),
            ]
            + [pl.BlockSpec(memory_space=pl.ANY)] * len(earlier),
            out_specs=[
                pl.BlockSpec((2 * rows, qs), by_group),
                pl.BlockSpec((2 * rows, kvs), by_group),
            ],
            scratch_shapes=[
                pltpu.VMEM((2 * rows, width), jnp.bfloat16),
                pltpu.VMEM((2 * rows, LANES), jnp.float32),
                pltpu.VMEM((2 * rows, LANES), jnp.float32),
            ],
        ),
        out_shape=[
            jax.ShapeDtypeStruct((2 * rows * chips, groups * qs), jnp.bfloat16),
            jax.ShapeDtypeStruct((2 * rows * chips, groups * kvs), jnp.bfloat16),
        ],
        input_output_aliases={6: 0, 7: 1} if earlier else {},
        compiler_params=pltpu.CompilerParams(vmem_limit_bytes=60 * MIB),
        cost_estimate=pl.CostEstimate(
            flops=4 * rows * width * columns, bytes_accessed=2 * width * columns, transcendentals=0
        ),
        name="project",
    )(ids, lengths, own, other, gain, weight, *earlier)


def pack_rows(values_ref, pick_ref, packed_ref):
    packed_ref[:, :EXTRA_AT] = jnp.dot(
        pick_ref[0], values_ref[:, :EXTRA_AT], preferred_element_type=jnp.float32
    ).astype(jnp.bfloat16)
    pieces = jnp.zeros((packed_ref.shape[0], packed_ref.shape[1] - EXTRA_AT), jnp.float32)
    for p in range(pick_ref.shape[0] - 1):
        pieces = pieces + jnp.dot(
            pick_ref[1 + p],
            values_ref[:, p * PIECE : (p + 1) * PIECE],
            preferred_element_type=jnp.float32,
        )
    packed_ref[:, EXTRA_AT:] = pieces.astype(jnp.bfloat16)


def resid_kernel(tokens_ref, own_ref, others_ref, gain_ref, resid_ref, moe_ref):
    resid = tokens_ref[...].astype(jnp.float32) + own_ref[...].astype(jnp.float32)
    for k in range(others_ref.shape[0]):
        resid = resid + others_ref[k].astype(jnp.float32)
    resid_ref[...] = resid
    inv_rms = lax.rsqrt(jnp.mean(resid * resid, axis=-1, keepdims=True) + EPSILON)
    moe_ref[...] = (resid * inv_rms * gain_ref[...][None]).astype(jnp.bfloat16)


def pack_kernel(moe_ref, pick_ref, packed_ref, values_ref):
    width = moe_ref.shape[1]
    values_ref[:, width:] = jnp.zeros_like(values_ref[:, width:])
    values_ref[:, :width] = moe_ref[...]
    pack_rows(values_ref, pick_ref, packed_ref)


def packed_width(extras):
    return EXTRA_AT + PIECE if extras else PIECES * PIECE


def finish_attention(tokens, own, others, gain):
    rows, width = tokens.shape
    return pl.pallas_call(
        resid_kernel,
        out_shape=[
            jax.ShapeDtypeStruct((rows, width), jnp.float32),
            jax.ShapeDtypeStruct((rows, width), jnp.bfloat16),
        ],
        compiler_params=pltpu.CompilerParams(vmem_limit_bytes=32 * MIB),
        name="finish_attention",
    )(tokens, own, others, gain)


def pack(moe_in, picks, beside):
    rows, width = moe_in.shape
    kinds, slots, _ = picks.shape
    return pl.pallas_call(
        pack_kernel,
        out_shape=jax.ShapeDtypeStruct((slots, packed_width(kinds > 1)), jnp.bfloat16),
        scratch_shapes=[pltpu.VMEM((rows, PIECES * PIECE), jnp.bfloat16)],
        compiler_params=pltpu.CompilerParams(vmem_limit_bytes=32 * MIB),
        cost_estimate=pl.CostEstimate(
            flops=2 * slots * rows * 2 * width, bytes_accessed=beside, transcendentals=0
        ),
        name="pack",
    )(moe_in, picks)


def piece_of(count, slots, piece):
    t = lax.broadcasted_iota(jnp.int32, (count, slots), 0)
    r = lax.broadcasted_iota(jnp.int32, (count, slots), 1)
    return jnp.where(r == PIECES * t + piece, 1.0, 0.0).astype(jnp.bfloat16)


def fill_rows(packed_ref, x_ref, extras):
    slots, width = packed_ref.shape[0], x_ref.shape[1]
    x_ref[:slots, :] = packed_ref[:, :width]
    if extras:
        further = slots // PIECES
        for p in range(PIECES):
            extent = min(PIECE, width - p * PIECE)
            x_ref[slots:, p * PIECE : p * PIECE + extent] = jnp.dot(
                piece_of(further, slots, p),
                packed_ref[:, EXTRA_AT : EXTRA_AT + extent],
                preferred_element_type=jnp.float32,
            ).astype(jnp.bfloat16)


def activate(gate_up_ref, act_ref):
    rows, ffs = act_ref.shape
    base = ffs // LANES * LANES
    chunk = 32
    for r in range(0, rows, chunk):
        gate = gate_up_ref[r : r + chunk, :ffs]
        up = gate_up_ref[r : r + chunk, base:]
        if ffs > base:
            up = pltpu.roll(up, up.shape[1] - (ffs - base), 1)
        up = up[:, :ffs]
        act_ref[r : r + chunk, :] = (
            (up + 1.0) * gate * jax.nn.sigmoid(GLU_ALPHA * gate)
        ).astype(jnp.bfloat16)


def put_piece(piece, act_ref, w_down_ref, out_ref, width, piece_ref):
    slots = out_ref.shape[0]
    made = jnp.dot(act_ref[...], w_down_ref[0], preferred_element_type=jnp.float32)
    column = lax.broadcasted_iota(jnp.int32, made.shape, 1) + piece * PIECE
    made = jnp.where(column < width, made, 0.0).astype(jnp.bfloat16)
    out_ref[:, pl.ds(pl.multiple_of(piece * PIECE, LANES), PIECE)] = made[:slots]
    if piece_ref is not None:
        further = slots // PIECES
        t = lax.broadcasted_iota(jnp.int32, (slots, further), 1)
        r = lax.broadcasted_iota(jnp.int32, (slots, further), 0)
        spread = jnp.where(r == PIECES * t + piece, 1.0, 0.0).astype(jnp.bfloat16)
        part = jnp.dot(spread, made[slots:], preferred_element_type=jnp.float32).astype(
            jnp.bfloat16
        )

        @pl.when(piece == 0)
        def _():
            piece_ref[...] = part

        @pl.when(piece > 0)
        def _():
            piece_ref[...] = piece_ref[...] + part

        @pl.when(piece == PIECES - 1)
        def _():
            out_ref[:, EXTRA_AT:] = piece_ref[...]


def expert_kernel(extras, in_tiles, down, *refs):
    packed_ref, w_in_ref = refs[:2]
    scratch = refs[4:] if down else refs[3:]
    x_ref, gate_up_ref = scratch[:2]
    act_ref = scratch[2] if down else refs[2]
    step = pl.program_id(0)

    @pl.when(step == 0)
    def _():
        fill_rows(packed_ref, x_ref, extras)

    @pl.when(step < in_tiles)
    def _():
        gate_up_ref[:, pl.ds(pl.multiple_of(step * IN_TILE, LANES), IN_TILE)] = jnp.dot(
            x_ref[...], w_in_ref[0], preferred_element_type=jnp.float32
        )

    @pl.when(step == (in_tiles if down else in_tiles - 1))
    def _():
        activate(gate_up_ref, act_ref)

    if down:
        w_down_ref, out_ref = refs[2:4]

        @pl.when(step >= in_tiles)
        def _():
            piece_ref = scratch[3] if extras else None
            put_piece(step - in_tiles, act_ref, w_down_ref, out_ref, x_ref.shape[1], piece_ref)


def down_kernel(extras, width, act_ref, w_down_ref, out_ref, *scratch):
    put_piece(
        pl.program_id(0), act_ref, w_down_ref, out_ref, width, scratch[0] if extras else None
    )


def expert(packed, w_in, w_down, extras, down=True):
    slots, held = packed.shape
    width = w_in.shape[1]
    ffs = w_down.shape[1]
    rows = slots + (slots // PIECES if extras else 0)
    in_tiles = pl.cdiv(2 * ffs, IN_TILE)
    whole = lambda i: (0, 0)
    in_specs = [
        pl.BlockSpec((slots, held), whole),
        pl.BlockSpec((1, width, IN_TILE), lambda i: (0, 0, jnp.minimum(i, in_tiles - 1))),
    ]
    scratch = [
        pltpu.VMEM((rows, width), jnp.bfloat16),
        pltpu.VMEM((rows, in_tiles * IN_TILE), jnp.float32),
    ]
    args = (packed, w_in)
    out = (rows, ffs)
    if down:
        in_specs += [
            pl.BlockSpec((1, ffs, PIECE), lambda i: (0, 0, jnp.maximum(i - in_tiles, 0)))
        ]
        scratch += [pltpu.VMEM((rows, ffs), jnp.bfloat16)]
        scratch += [pltpu.VMEM((slots, PIECE), jnp.bfloat16)] if extras else []
        args += (w_down,)
        out = (slots, held)
    parts = 6 if down else 4
    return pl.pallas_call(
        functools.partial(expert_kernel, extras, in_tiles, down),
        grid=(in_tiles + (PIECES if down else 0),),
        in_specs=in_specs,
        out_specs=pl.BlockSpec(out, whole),
        out_shape=jax.ShapeDtypeStruct(out, jnp.bfloat16),
        scratch_shapes=scratch,
        compiler_params=pltpu.CompilerParams(vmem_limit_bytes=56 * MIB),
        cost_estimate=pl.CostEstimate(
            flops=parts * rows * width * ffs,
            bytes_accessed=parts * width * ffs,
            transcendentals=rows * ffs,
        ),
        name="expert" if down else "expert_up",
    )(*args)


def expert_down(act, w_down, slots, held, extras):
    rows, ffs = act.shape
    width = w_down.shape[2]
    whole = lambda i: (0, 0)
    return pl.pallas_call(
        functools.partial(down_kernel, extras, width),
        grid=(PIECES,),
        in_specs=[
            pl.BlockSpec((rows, ffs), whole),
            pl.BlockSpec((1, ffs, PIECE), lambda i: (0, 0, i)),
        ],
        out_specs=pl.BlockSpec((slots, held), whole),
        out_shape=jax.ShapeDtypeStruct((slots, held), jnp.bfloat16),
        scratch_shapes=[pltpu.VMEM((slots, PIECE), jnp.bfloat16)] if extras else [],
        compiler_params=pltpu.CompilerParams(vmem_limit_bytes=56 * MIB),
        cost_estimate=pl.CostEstimate(
            flops=2 * rows * width * ffs, bytes_accessed=2 * width * ffs, transcendentals=0
        ),
        name="expert_down",
    )(act, w_down)


def weighted_sum(made_ref, weight_ref, total_ref):
    width = total_ref.shape[1]
    for term in range(2):
        made = jnp.dot(
            weight_ref[term, 0], made_ref[:, :width], preferred_element_type=jnp.float32
        )
        total_ref[...] = made if term == 0 else total_ref[...] + made
        for p in range(weight_ref.shape[1] - 1):
            extent = min(PIECE, width - p * PIECE)
            at = slice(p * PIECE, p * PIECE + extent)
            total_ref[:, at] = total_ref[:, at] + jnp.dot(
                weight_ref[term, 1 + p],
                made_ref[:, EXTRA_AT : EXTRA_AT + extent],
                preferred_element_type=jnp.float32,
            )


def partial_kernel(made_ref, weight_ref, out_ref, total_ref):
    weighted_sum(made_ref, weight_ref, total_ref)
    out_ref[...] = total_ref[...].astype(jnp.bfloat16)


def total_kernel(made_ref, weight_ref, resid_ref, far_ref, out_ref, total_ref):
    weighted_sum(made_ref, weight_ref, total_ref)
    out_ref[...] = (
        resid_ref[...] + (total_ref[...] + far_ref[...].astype(jnp.float32))
    ).astype(jnp.bfloat16)


def combine(made, weights, resid=None, far=None):
    rows = weights.shape[2]
    kernel, more = (partial_kernel, ()) if resid is None else (total_kernel, (resid, far))
    return pl.pallas_call(
        kernel,
        out_shape=jax.ShapeDtypeStruct((rows, MODEL_WIDTH), jnp.bfloat16),
        scratch_shapes=[pltpu.VMEM((rows, MODEL_WIDTH), jnp.float32)],
        compiler_params=pltpu.CompilerParams(vmem_limit_bytes=32 * MIB),
        name="combine",
    )(made, weights, *more)


def slots_kernel(extras, far, half, experts, shards, topk, ids_ref, lengths_ref, choice_ref, *out_refs):
    pick_ref, weight_ref = out_refs
    device = ids_ref[3]
    first_expert = device // half * experts
    _, slots, rows = pick_ref.shape
    source = (device + half) % (2 * half) if far else device
    r = lax.broadcasted_iota(jnp.int32, (slots, rows), 0)
    index = source * rows + lax.broadcasted_iota(jnp.int32, (slots, rows), 1)
    slot = r % MAIN_SLOTS
    own_expert = (first_expert + r // (MAIN_SLOTS * shards)).astype(jnp.float32)
    named = jnp.zeros((slots, rows), jnp.float32)
    gate = jnp.zeros((slots, rows), jnp.float32)
    for k in range(topk):
        here = choice_ref[k : k + 1, :] == own_expert
        named = jnp.where(here, 1.0, named)
        gate = gate + jnp.where(here, choice_ref[topk + k : topk + k + 1, :], 0.0)
    named = jnp.where(index < segment_ends(lengths_ref)[-1], named, 0.0)
    i = lax.broadcasted_iota(jnp.int32, (rows, rows), 0)
    j = lax.broadcasted_iota(jnp.int32, (rows, rows), 1)
    earlier = jnp.where(i < j, 1.0, 0.0).astype(jnp.bfloat16)
    same = jnp.where(i == j, 1.0, 0.0).astype(jnp.bfloat16)
    rank = jnp.dot(named.astype(jnp.bfloat16), earlier, preferred_element_type=jnp.float32)
    rank = jnp.where(named > 0.0, rank, -1.0).astype(jnp.int32)
    high = gate.astype(jnp.bfloat16).astype(jnp.float32)

    def put(hit, pick_at, high_at, low_at):
        pick_at[...] = jnp.where(hit, 1.0, 0.0).astype(jnp.bfloat16)
        for values, at in ((high, high_at), (gate - high, low_at)):
            kept = jnp.where(hit, values, 0.0).astype(jnp.bfloat16)
            at[...] = lax.dot_general(
                same, kept, (((1,), (1,)), ((), ())), preferred_element_type=jnp.float32
            ).astype(jnp.bfloat16)

    put(rank == slot, pick_ref.at[0], weight_ref.at[0, 0], weight_ref.at[1, 0])
    if extras:
        for p in range(PIECES):
            hit = jnp.where(slot % PIECES == p, rank, -2) == MAIN_SLOTS + slot // PIECES
            put(hit, pick_ref.at[1 + p], weight_ref.at[0, 1 + p], weight_ref.at[1, 1 + p])


def slot_tables(ids, lengths, choice, far, half, experts, shards, extras):
    topk, rows = choice.shape[0] // 2, choice.shape[1]
    slots = experts * shards * MAIN_SLOTS
    kinds = 1 + PIECES if extras else 1
    shapes = [(kinds, slots, rows), (2, kinds, rows, slots)]
    smem = pl.BlockSpec(memory_space=pltpu.SMEM)
    return pl.pallas_call(
        functools.partial(slots_kernel, extras, far, half, experts, shards, topk),
        in_specs=[smem, smem, pl.BlockSpec(memory_space=pltpu.VMEM)],
        out_shape=[jax.ShapeDtypeStruct(shape, jnp.bfloat16) for shape in shapes],
        compiler_params=pltpu.CompilerParams(vmem_limit_bytes=32 * MIB),
        name="slots",
    )(ids, lengths, choice)


def attend_kernel(row_count, chips, ids_ref, lengths_ref, q_ref, rim_ref, pair_ref, sink_ref, w_ref, kept_ref, sent_ref, attended_ref):
    def attend_block(block):
        window = rim_ref.shape[0]
        rows = slice(block * window, (block + 1) * window)
        groups = pair_ref.shape[1] // LANES
        core = ids_ref[0]
        ends = segment_ends(lengths_ref)
        first = ids_ref[2] * (chips * 2 * row_count) + block * window
        query = first + lax.broadcasted_iota(jnp.int32, (window, 2 * window), 0)
        key = first - window + lax.broadcasted_iota(jnp.int32, (window, 2 * window), 1)
        query_segment = segment_of(query, ends)
        seen = (query_segment == segment_of(key, ends)) & (query_segment < NSEQ)
        seen = seen & (key >= 0) & (query >= key) & (query - key < window)
        lane = lax.broadcasted_iota(jnp.int32, (2 * window, LANES), 1)
        twos = QUERY_PER_KEY // 2
        for g in range(groups):
            at = slice(g * LANES, (g + 1) * LANES)
            before = pair_ref[(block - 1) * window : block * window, at] if block else rim_ref[:, at]
            pairs = jnp.concatenate([before, pair_ref[rows, at]], axis=0).astype(jnp.float32)
            keys = jnp.where(lane < HEAD_SIZE, pairs, 0.0)
            values = jnp.where(lane < HEAD_SIZE, 0.0, pairs)
            keys = [x.astype(jnp.bfloat16) for x in (keys, pltpu.roll(keys, HEAD_SIZE, 1))]
            values = [x.astype(jnp.bfloat16) for x in (pltpu.roll(values, HEAD_SIZE, 1), values)]
            start = g * twos * LANES
            queries = jnp.concatenate(
                [q_ref[rows, start + two * LANES : start + (two + 1) * LANES] for two in range(twos)],
                axis=0,
            )
            made = jnp.zeros((twos * window, LANES), jnp.float32)
            for side in range(2):
                scores = lax.dot_general(
                    queries, keys[side], (((1,), (1,)), ((), ())), preferred_element_type=jnp.float32
                )
                probs = []
                for two in range(twos):
                    sink = sink_ref[g * QUERY_PER_KEY + 2 * two + side]
                    weights = jnp.where(
                        seen, jnp.exp(scores[two * window : (two + 1) * window]), 0.0
                    )
                    totals = jnp.sum(weights, axis=-1, keepdims=True)
                    totals = totals + jnp.exp(jnp.full_like(totals, sink))
                    probs.append((weights * (1.0 / totals)).astype(jnp.bfloat16))
                made = made + jnp.dot(
                    jnp.concatenate(probs, axis=0), values[side], preferred_element_type=jnp.float32
                )
            made = made.astype(jnp.bfloat16)
            for two in range(twos):
                columns = slice(start + two * LANES, start + (two + 1) * LANES)
                for part in range(window // row_count):
                    head = block * (window // row_count) + part
                    place = (head % 2 + core) % 2 * chips + head // 2
                    row = two * window + part * row_count
                    attended_ref[
                        pl.ds(pl.multiple_of(place * row_count, 16), row_count), columns
                    ] = made[row : row + row_count]

    @pl.when(pl.program_id(0) == 0)
    def _():
        window = rim_ref.shape[0]
        for block in range(q_ref.shape[0] // window):
            attend_block(block)

    product = lax.dot_general(
        attended_ref[...],
        w_ref[...],
        (((1,), (1,)), ((), ())),
        preferred_element_type=jnp.float32,
    )
    for chip in range(chips):
        at, then = chip * row_count, (chips + chip) * row_count
        kept_ref[chip] = product[at : at + row_count]
        sent_ref[chip] = product[then : then + row_count].astype(jnp.bfloat16)


def attend(ids, lengths, queries, rim, pairs, sinks, w_out, row_count):
    total, columns = queries.shape
    width = w_out.shape[0]
    chips = total // (2 * row_count)
    tile = PIECE
    whole = lambda i, ids: (0, 0)
    smem = pl.BlockSpec(memory_space=pltpu.SMEM)
    return pl.pallas_call(
        functools.partial(attend_kernel, row_count, chips),
        grid_spec=pltpu.PrefetchScalarGridSpec(
            num_scalar_prefetch=1,
            grid=(pl.cdiv(width, tile),),
            in_specs=[
                smem,
                pl.BlockSpec(queries.shape, whole),
                pl.BlockSpec(rim.shape, whole),
                pl.BlockSpec(pairs.shape, whole),
                smem,
                pl.BlockSpec((tile, columns), lambda i, ids: (i, 0)),
            ],
            out_specs=[pl.BlockSpec((chips, row_count, tile), lambda i, ids: (0, 0, i))] * 2,
            scratch_shapes=[pltpu.VMEM(queries.shape, jnp.bfloat16)],
        ),
        out_shape=[
            jax.ShapeDtypeStruct((chips, row_count, width), jnp.float32),
            jax.ShapeDtypeStruct((chips, row_count, width), jnp.bfloat16),
        ],
        compiler_params=pltpu.CompilerParams(vmem_limit_bytes=60 * MIB),
        cost_estimate=pl.CostEstimate(
            flops=2 * total * columns * width, bytes_accessed=2 * columns * width, transcendentals=0
        ),
        name="attend",
    )(ids, lengths, queries, rim, pairs, sinks, w_out)


def page_order(page_table, n_tok, pages_dev):
    page_grid = page_table.reshape(n_tok, pages_dev)
    target = page_grid // pages_dev
    page_ids = jnp.arange(pages_dev, dtype=jnp.int32)
    earlier = page_ids[:, None] > page_ids[None, :]
    same_dest = target[:, :, None] == target[:, None, :]
    order_rank = jnp.sum((same_dest & earlier[None]).astype(jnp.int32), axis=2)
    return (target, order_rank, page_grid % pages_dev)


def exchanged_pages(pairs, page_table, tok_id, n_tok):
    rows = pairs.shape[0]
    groups = pairs.shape[1] // (2 * HEAD_SIZE)
    pages_dev = rows // PAGE_TOKENS
    share_count = pages_dev // n_tok
    paged = pairs.reshape(pages_dev, PAGE_TOKENS, groups, 2 * HEAD_SIZE).transpose(0, 2, 1, 3)
    target, order_rank, _ = page_order(page_table, n_tok, pages_dev)
    dest_ids = jnp.arange(n_tok, dtype=jnp.int32)
    share_ids = jnp.arange(share_count, dtype=jnp.int32)
    page_ids = jnp.arange(pages_dev, dtype=jnp.int32)
    matched = (target[tok_id][:, None, None] == dest_ids[None, :, None]) & (
        order_rank[tok_id][:, None, None] == share_ids[None, None, :]
    )
    pick_page = jnp.sum(jnp.where(matched, page_ids[:, None, None], 0), axis=0).reshape(-1)
    sent = paged[pick_page].reshape(n_tok, share_count * groups * PAGE_TOKENS, 2 * HEAD_SIZE)
    return lax.all_to_all(sent, "tok", split_axis=0, concat_axis=0, tiled=True)


def landed_pages(arrived, page_table, tok_id, n_tok, groups):
    share_count = arrived.shape[1] // (groups * PAGE_TOKENS)
    pages_dev = n_tok * share_count
    arrived = arrived.reshape(pages_dev, groups, PAGE_TOKENS, 2 * HEAD_SIZE)
    target, order_rank, slot_grid = page_order(page_table, n_tok, pages_dev)
    share_ids = jnp.arange(share_count, dtype=jnp.int32)
    page_ids = jnp.arange(pages_dev, dtype=jnp.int32)
    to_here = (target == tok_id)[:, :, None] & (order_rank[:, :, None] == share_ids[None, None, :])
    landing = jnp.sum(jnp.where(to_here, slot_grid[:, :, None], 0), axis=1).reshape(-1)
    source = jnp.sum(
        jnp.where(landing[None, :] == page_ids[:, None], page_ids[None, :], 0), axis=1
    )
    return arrived[source].transpose(1, 0, 2, 3)


def per_device(
    tokens,
    lengths,
    norm_gain_attn,
    query_key_value_weight,
    sinks,
    w_out_attn,
    norm_gain_moe,
    routes,
    gates,
    w_in,
    w_down,
    page_table,
):
    n_tok = lax.axis_size("tok")
    n_head = lax.axis_size("head")
    tok_id = lax.axis_index("tok")
    head_id = lax.axis_index("head")
    row_count, width = tokens.shape
    tok_dev = row_count * n_head
    groups = sinks.shape[0] // QUERY_PER_KEY
    n_y = n_head // 2
    y_id, core = head_id // 2, head_id % 2

    def to_core(array):
        return lax.ppermute(array, "head", [(h, h ^ 1) for h in range(n_head)])

    def along_y(array, by):
        return lax.ppermute(
            array, "head", [(h, (h // 2 + by) % n_y * 2 + h % 2) for h in range(n_head)]
        )

    n_dev = n_tok * n_head
    half = n_dev // 2

    def across(array):
        return lax.ppermute(array, ("tok", "head"), [(d, d ^ half) for d in range(n_dev)])

    def in_half(array):
        return lax.all_to_all(
            array,
            ("tok", "head"),
            split_axis=0,
            concat_axis=0,
            tiled=True,
            axis_index_groups=[list(range(half)), list(range(half, n_dev))],
        )

    flat_id = tok_id * n_head + head_id
    ids = jnp.stack([core, y_id, tok_id, flat_id]).astype(jnp.int32)
    choice = jnp.concatenate([routes.T.astype(jnp.float32), gates.T], axis=0)
    far_choice = across(choice)

    capacity = row_count // 8 + 2
    shards = n_dev // EXPERTS
    extras = capacity > MAIN_SLOTS
    tables = functools.partial(slot_tables, ids, lengths)
    sizes = (half, EXPERTS // 2, shards, extras)
    slots = tables(choice, False, *sizes), tables(far_choice, True, *sizes)

    placed, block = [], tokens
    for k in range(n_y):
        if k:
            block, slots = lax.optimization_barrier((along_y(tokens, k), slots))
        placed = project(
            ids,
            lengths,
            k,
            n_y,
            block,
            to_core(block),
            norm_gain_attn,
            query_key_value_weight,
            placed,
        )
    (own_picks, own_weights), (far_picks, far_weights) = slots
    query_rows, key_value_pairs = placed
    rim_rows = passed_along(key_value_pairs[tok_dev - ATTEND_WINDOW :], "tok", 1)
    kept, sent = attend(
        ids, lengths, query_rows, rim_rows, key_value_pairs, sinks, w_out_attn.T, row_count
    )
    sent = to_core(sent)

    def chip_sum(chip):
        here = lax.dynamic_index_in_dim(kept, chip, 0, keepdims=False)
        there = lax.dynamic_index_in_dim(sent, chip, 0, keepdims=False)
        return here + there.astype(jnp.float32)

    own_sum = chip_sum(y_id)
    leaving = [chip_sum((y_id + k) % n_y).astype(jnp.bfloat16) for k in range(1, n_y)]
    leaving, key_value_pairs = lax.optimization_barrier((leaving, key_value_pairs))
    other_sums = jnp.stack([along_y(part, k + 1) for k, part in enumerate(leaving)])
    pages = exchanged_pages(key_value_pairs, page_table, tok_id, n_tok)
    other_sums, pages = lax.optimization_barrier((other_sums, pages))

    resid, moe_in = finish_attention(
        tokens, own_sum, other_sums, norm_gain_moe
    )
    far_moe_in = across(moe_in)
    own_packed = pack(moe_in, own_picks, 64 * MIB)

    def exchanged(packed):
        slots, held = packed.shape
        return in_half(packed.reshape(half, MAIN_SLOTS, held)).reshape(slots, held)

    far_packed = pack(far_moe_in, far_picks, MIB)
    far_arrived = exchanged(far_packed)
    far_arrived, own_packed = lax.optimization_barrier((far_arrived, own_packed))
    own_arrived = exchanged(own_packed)
    far_made = expert(far_arrived, w_in, w_down, extras)
    far_made, own_arrived = lax.optimization_barrier((far_made, own_arrived))
    far_returned = exchanged(far_made)
    own_act = expert(own_arrived, w_in, w_down, extras, down=False)
    far_returned, own_act = lax.optimization_barrier((far_returned, own_act))
    far_part, own_act = lax.optimization_barrier((combine(far_returned, far_weights), own_act))
    far_sum = across(far_part)
    own_returned = lax.fori_loop(
        0,
        jnp.minimum(lengths[0], 1),
        lambda _, held: exchanged(expert_down(own_act, w_down, *held.shape, extras)),
        own_packed,
    )
    hidden_out = combine(own_returned, own_weights, resid, far_sum)
    kv_cache = landed_pages(pages, page_table, tok_id, n_tok, groups)
    return (hidden_out, kv_cache)


def solution(mesh):
    return jax.shard_map(
        per_device,
        mesh=mesh,
        in_specs=(
            P(("tok", "head"), None),
            P(),
            P(),
            P(None, "head"),
            P("head"),
            P("head", None),
            P(),
            P(("tok", "head"), None),
            P(("tok", "head"), None),
            P(("tok", "head"), None, None),
            P(("tok", "head"), None, None),
            P(),
        ),
        out_specs=(P(("tok", "head"), None), P("head", "tok", None, None)),
        check_vma=False,
    )
```

```python
import functools
import math

import jax
import jax.numpy as jnp
from jax import lax
from jax.experimental import pallas as pl
from jax.experimental.pallas import tpu as pltpu
from jax.sharding import PartitionSpec as P

MODEL_WIDTH = 2880
HEAD_SIZE = 64
EXPERTS = 32
ATTEND_WINDOW = 128
NSEQ = 4
PAGE_TOKENS = 16
QUERY_PER_KEY = 8


EPSILON = 1e-05
ROPE_BASE = 150000.0
GLU_ALPHA = 1.702

LANES = 128
MAIN_SLOTS = 8
PIECE = 768
PIECES = 4
EXTRA_AT = 2944
IN_TILE = 1152
MIB = 1 << 20


def passed_along(array, axis, by):
    peers = lax.axis_size(axis)
    pairs = [(i, i + by) for i in range(peers) if 0 <= i + by < peers]
    return lax.ppermute(array, axis, pairs)


def segment_ends(lengths_ref):
    ends, end = [], 0
    for k in range(NSEQ):
        end = end + lengths_ref[k]
        ends.append(end)
    return ends


def segment_of(index, ends):
    segment = jnp.zeros_like(index)
    for end in ends:
        segment = segment + jnp.where(index >= end, 1, 0)
    return segment


def rope_tables(index, ends):
    start = jnp.zeros_like(index)
    for end in ends:
        start = jnp.where(index >= end, end, start)
    half = HEAD_SIZE // 2
    lane = lax.broadcasted_iota(jnp.int32, index.shape, 1)
    inv_freq = jnp.exp(
        (lane % half).astype(jnp.float32) * (-2.0 * math.log(ROPE_BASE) / HEAD_SIZE)
    )
    angles = (index - start).astype(jnp.float32) * inv_freq
    low = lane % HEAD_SIZE < half
    sin = jnp.sin(angles)
    return jnp.cos(angles), jnp.where(low, -sin, sin), low, lane


def qkv_kernel(step, chips, ids_ref, lengths_ref, own_ref, other_ref, gain_ref, w_ref, *refs):
    q_ref, kv_ref, xn_ref, cos_ref, sin_ref = refs[-5:]
    rows = own_ref.shape[0]
    core, chip, shard = ids_ref[0], (ids_ref[1] + chips - step) % chips, ids_ref[2]

    @pl.when(pl.program_id(0) == 0)
    def _():
        for at, ref in ((core, own_ref), (1 - core, other_ref)):
            wide = ref[...].astype(jnp.float32)
            inv_rms = lax.rsqrt(jnp.mean(wide * wide, axis=-1, keepdims=True) + EPSILON)
            normed = (wide * inv_rms * gain_ref[...][None]).astype(jnp.bfloat16)
            xn_ref[pl.ds(pl.multiple_of(at * rows, 16), rows), :] = normed
        first = (shard * chips + chip) * 2 * rows
        index = first + lax.broadcasted_iota(jnp.int32, cos_ref.shape, 0)
        cos, sin, _, _ = rope_tables(index, segment_ends(lengths_ref))
        cos_ref[...] = cos
        sin_ref[...] = sin

    projected = jnp.dot(xn_ref[...], w_ref[...], preferred_element_type=jnp.float32)
    cos, sin = cos_ref[...], sin_ref[...]
    lane = lax.broadcasted_iota(jnp.int32, cos.shape, 1)
    low = lane % HEAD_SIZE < HEAD_SIZE // 2

    def turned(u):
        return jnp.where(low, pltpu.roll(u, LANES - 32, 1), pltpu.roll(u, 32, 1))

    for b in range(QUERY_PER_KEY // 2):
        u = projected[:, b * LANES : (b + 1) * LANES]
        q_ref[:, b * LANES : (b + 1) * LANES] = (
            (u * cos + turned(u) * sin) * HEAD_SIZE ** (-0.5)
        ).astype(jnp.bfloat16)
    u = projected[:, QUERY_PER_KEY * HEAD_SIZE :]
    rotated = u * cos + turned(u) * sin
    kv_ref[...] = jnp.where(lane < HEAD_SIZE, rotated, u).astype(jnp.bfloat16)


def project(ids, lengths, step, chips, own, other, gain, weight, earlier):
    rows, width = own.shape
    columns = weight.shape[1]
    group = (QUERY_PER_KEY + 2) * HEAD_SIZE
    qs, kvs = QUERY_PER_KEY * HEAD_SIZE, 2 * HEAD_SIZE
    groups = columns // group
    whole = lambda g, ids: (0, 0)
    by_group = lambda g, ids: ((ids[1] + chips - step) % chips, g)
    return pl.pallas_call(
        functools.partial(qkv_kernel, step, chips),
        grid_spec=pltpu.PrefetchScalarGridSpec(
            num_scalar_prefetch=1,
            grid=(groups,),
            in_specs=[
                pl.BlockSpec(memory_space=pltpu.SMEM),
                pl.BlockSpec((rows, width), whole),
                pl.BlockSpec((rows, width), whole),
                pl.BlockSpec((width,), lambda g, ids: (0,)),
                pl.BlockSpec((width, group), lambda g, ids: (0, g)),
            ]
            + [pl.BlockSpec(memory_space=pl.ANY)] * len(earlier),
            out_specs=[
                pl.BlockSpec((2 * rows, qs), by_group),
                pl.BlockSpec((2 * rows, kvs), by_group),
            ],
            scratch_shapes=[
                pltpu.VMEM((2 * rows, width), jnp.bfloat16),
                pltpu.VMEM((2 * rows, LANES), jnp.float32),
                pltpu.VMEM((2 * rows, LANES), jnp.float32),
            ],
        ),
        out_shape=[
            jax.ShapeDtypeStruct((2 * rows * chips, groups * qs), jnp.bfloat16),
            jax.ShapeDtypeStruct((2 * rows * chips, groups * kvs), jnp.bfloat16),
        ],
        input_output_aliases={6: 0, 7: 1} if earlier else {},
        compiler_params=pltpu.CompilerParams(vmem_limit_bytes=60 * MIB),
        cost_estimate=pl.CostEstimate(
            flops=4 * rows * width * columns, bytes_accessed=2 * width * columns, transcendentals=0
        ),
        name="project",
    )(ids, lengths, own, other, gain, weight, *earlier)


def pack_rows(values_ref, pick_ref, packed_ref):
    packed_ref[:, :EXTRA_AT] = jnp.dot(
        pick_ref[0], values_ref[:, :EXTRA_AT], preferred_element_type=jnp.float32
    ).astype(jnp.bfloat16)
    pieces = jnp.zeros((packed_ref.shape[0], packed_ref.shape[1] - EXTRA_AT), jnp.float32)
    for p in range(pick_ref.shape[0] - 1):
        pieces = pieces + jnp.dot(
            pick_ref[1 + p],
            values_ref[:, p * PIECE : (p + 1) * PIECE],
            preferred_element_type=jnp.float32,
        )
    packed_ref[:, EXTRA_AT:] = pieces.astype(jnp.bfloat16)


def resid_kernel(tokens_ref, own_ref, others_ref, gain_ref, resid_ref, moe_ref):
    resid = tokens_ref[...].astype(jnp.float32) + own_ref[...].astype(jnp.float32)
    for k in range(others_ref.shape[0]):
        resid = resid + others_ref[k].astype(jnp.float32)
    resid_ref[...] = resid
    inv_rms = lax.rsqrt(jnp.mean(resid * resid, axis=-1, keepdims=True) + EPSILON)
    moe_ref[...] = (resid * inv_rms * gain_ref[...][None]).astype(jnp.bfloat16)


def pack_kernel(moe_ref, pick_ref, packed_ref, values_ref):
    width = moe_ref.shape[1]
    values_ref[:, width:] = jnp.zeros_like(values_ref[:, width:])
    values_ref[:, :width] = moe_ref[...]
    pack_rows(values_ref, pick_ref, packed_ref)


def packed_width(extras):
    return EXTRA_AT + PIECE if extras else PIECES * PIECE


def finish_attention(tokens, own, others, gain):
    rows, width = tokens.shape
    return pl.pallas_call(
        resid_kernel,
        out_shape=[
            jax.ShapeDtypeStruct((rows, width), jnp.float32),
            jax.ShapeDtypeStruct((rows, width), jnp.bfloat16),
        ],
        compiler_params=pltpu.CompilerParams(vmem_limit_bytes=32 * MIB),
        name="finish_attention",
    )(tokens, own, others, gain)


def pack(moe_in, picks, beside):
    rows, width = moe_in.shape
    kinds, slots, _ = picks.shape
    return pl.pallas_call(
        pack_kernel,
        out_shape=jax.ShapeDtypeStruct((slots, packed_width(kinds > 1)), jnp.bfloat16),
        scratch_shapes=[pltpu.VMEM((rows, PIECES * PIECE), jnp.bfloat16)],
        compiler_params=pltpu.CompilerParams(vmem_limit_bytes=32 * MIB),
        cost_estimate=pl.CostEstimate(
            flops=2 * slots * rows * 2 * width, bytes_accessed=beside, transcendentals=0
        ),
        name="pack",
    )(moe_in, picks)


def piece_of(count, slots, piece):
    t = lax.broadcasted_iota(jnp.int32, (count, slots), 0)
    r = lax.broadcasted_iota(jnp.int32, (count, slots), 1)
    return jnp.where(r == PIECES * t + piece, 1.0, 0.0).astype(jnp.bfloat16)


def fill_rows(packed_ref, x_ref, extras):
    slots, width = packed_ref.shape[0], x_ref.shape[1]
    x_ref[:slots, :] = packed_ref[:, :width]
    if extras:
        further = slots // PIECES
        for p in range(PIECES):
            extent = min(PIECE, width - p * PIECE)
            x_ref[slots:, p * PIECE : p * PIECE + extent] = jnp.dot(
                piece_of(further, slots, p),
                packed_ref[:, EXTRA_AT : EXTRA_AT + extent],
                preferred_element_type=jnp.float32,
            ).astype(jnp.bfloat16)


def activate(gate_up_ref, act_ref):
    rows, ffs = act_ref.shape
    base = ffs // LANES * LANES
    chunk = 32
    for r in range(0, rows, chunk):
        gate = gate_up_ref[r : r + chunk, :ffs]
        up = gate_up_ref[r : r + chunk, base:]
        if ffs > base:
            up = pltpu.roll(up, up.shape[1] - (ffs - base), 1)
        up = up[:, :ffs]
        act_ref[r : r + chunk, :] = (
            (up + 1.0) * gate * jax.nn.sigmoid(GLU_ALPHA * gate)
        ).astype(jnp.bfloat16)


def put_piece(piece, act_ref, w_down_ref, out_ref, width, piece_ref):
    slots = out_ref.shape[0]
    made = jnp.dot(act_ref[...], w_down_ref[0], preferred_element_type=jnp.float32)
    column = lax.broadcasted_iota(jnp.int32, made.shape, 1) + piece * PIECE
    made = jnp.where(column < width, made, 0.0).astype(jnp.bfloat16)
    out_ref[:, pl.ds(pl.multiple_of(piece * PIECE, LANES), PIECE)] = made[:slots]
    if piece_ref is not None:
        further = slots // PIECES
        t = lax.broadcasted_iota(jnp.int32, (slots, further), 1)
        r = lax.broadcasted_iota(jnp.int32, (slots, further), 0)
        spread = jnp.where(r == PIECES * t + piece, 1.0, 0.0).astype(jnp.bfloat16)
        part = jnp.dot(spread, made[slots:], preferred_element_type=jnp.float32).astype(
            jnp.bfloat16
        )

        @pl.when(piece == 0)
        def _():
            piece_ref[...] = part

        @pl.when(piece > 0)
        def _():
            piece_ref[...] = piece_ref[...] + part

        @pl.when(piece == PIECES - 1)
        def _():
            out_ref[:, EXTRA_AT:] = piece_ref[...]


def expert_kernel(extras, in_tiles, down, *refs):
    packed_ref, w_in_ref = refs[:2]
    scratch = refs[4:] if down else refs[3:]
    x_ref, gate_up_ref = scratch[:2]
    act_ref = scratch[2] if down else refs[2]
    step = pl.program_id(0)

    @pl.when(step == 0)
    def _():
        fill_rows(packed_ref, x_ref, extras)

    @pl.when(step < in_tiles)
    def _():
        gate_up_ref[:, pl.ds(pl.multiple_of(step * IN_TILE, LANES), IN_TILE)] = jnp.dot(
            x_ref[...], w_in_ref[0], preferred_element_type=jnp.float32
        )

    @pl.when(step == (in_tiles if down else in_tiles - 1))
    def _():
        activate(gate_up_ref, act_ref)

    if down:
        w_down_ref, out_ref = refs[2:4]

        @pl.when(step >= in_tiles)
        def _():
            piece_ref = scratch[3] if extras else None
            put_piece(step - in_tiles, act_ref, w_down_ref, out_ref, x_ref.shape[1], piece_ref)


def down_kernel(extras, width, act_ref, w_down_ref, out_ref, *scratch):
    put_piece(
        pl.program_id(0), act_ref, w_down_ref, out_ref, width, scratch[0] if extras else None
    )


def expert(packed, w_in, w_down, extras, down=True):
    slots, held = packed.shape
    width = w_in.shape[1]
    ffs = w_down.shape[1]
    rows = slots + (slots // PIECES if extras else 0)
    in_tiles = pl.cdiv(2 * ffs, IN_TILE)
    whole = lambda i: (0, 0)
    in_specs = [
        pl.BlockSpec((slots, held), whole),
        pl.BlockSpec((1, width, IN_TILE), lambda i: (0, 0, jnp.minimum(i, in_tiles - 1))),
    ]
    scratch = [
        pltpu.VMEM((rows, width), jnp.bfloat16),
        pltpu.VMEM((rows, in_tiles * IN_TILE), jnp.float32),
    ]
    args = (packed, w_in)
    out = (rows, ffs)
    if down:
        in_specs += [
            pl.BlockSpec((1, ffs, PIECE), lambda i: (0, 0, jnp.maximum(i - in_tiles, 0)))
        ]
        scratch += [pltpu.VMEM((rows, ffs), jnp.bfloat16)]
        scratch += [pltpu.VMEM((slots, PIECE), jnp.bfloat16)] if extras else []
        args += (w_down,)
        out = (slots, held)
    parts = 6 if down else 4
    return pl.pallas_call(
        functools.partial(expert_kernel, extras, in_tiles, down),
        grid=(in_tiles + (PIECES if down else 0),),
        in_specs=in_specs,
        out_specs=pl.BlockSpec(out, whole),
        out_shape=jax.ShapeDtypeStruct(out, jnp.bfloat16),
        scratch_shapes=scratch,
        compiler_params=pltpu.CompilerParams(vmem_limit_bytes=56 * MIB),
        cost_estimate=pl.CostEstimate(
            flops=parts * rows * width * ffs,
            bytes_accessed=parts * width * ffs,
            transcendentals=rows * ffs,
        ),
        name="expert" if down else "expert_up",
    )(*args)


def expert_down(act, w_down, slots, held, extras):
    rows, ffs = act.shape
    width = w_down.shape[2]
    whole = lambda i: (0, 0)
    return pl.pallas_call(
        functools.partial(down_kernel, extras, width),
        grid=(PIECES,),
        in_specs=[
            pl.BlockSpec((rows, ffs), whole),
            pl.BlockSpec((1, ffs, PIECE), lambda i: (0, 0, i)),
        ],
        out_specs=pl.BlockSpec((slots, held), whole),
        out_shape=jax.ShapeDtypeStruct((slots, held), jnp.bfloat16),
        scratch_shapes=[pltpu.VMEM((slots, PIECE), jnp.bfloat16)] if extras else [],
        compiler_params=pltpu.CompilerParams(vmem_limit_bytes=56 * MIB),
        cost_estimate=pl.CostEstimate(
            flops=2 * rows * width * ffs, bytes_accessed=2 * width * ffs, transcendentals=0
        ),
        name="expert_down",
    )(act, w_down)


def weighted_sum(made_ref, weight_ref, total_ref):
    width = total_ref.shape[1]
    for term in range(2):
        made = jnp.dot(
            weight_ref[term, 0], made_ref[:, :width], preferred_element_type=jnp.float32
        )
        total_ref[...] = made if term == 0 else total_ref[...] + made
        for p in range(weight_ref.shape[1] - 1):
            extent = min(PIECE, width - p * PIECE)
            at = slice(p * PIECE, p * PIECE + extent)
            total_ref[:, at] = total_ref[:, at] + jnp.dot(
                weight_ref[term, 1 + p],
                made_ref[:, EXTRA_AT : EXTRA_AT + extent],
                preferred_element_type=jnp.float32,
            )


def partial_kernel(made_ref, weight_ref, out_ref, total_ref):
    weighted_sum(made_ref, weight_ref, total_ref)
    out_ref[...] = total_ref[...].astype(jnp.bfloat16)


def total_kernel(made_ref, weight_ref, resid_ref, far_ref, out_ref, total_ref):
    weighted_sum(made_ref, weight_ref, total_ref)
    out_ref[...] = (
        resid_ref[...] + (total_ref[...] + far_ref[...].astype(jnp.float32))
    ).astype(jnp.bfloat16)


def combine(made, weights, resid=None, far=None):
    rows = weights.shape[2]
    kernel, more = (partial_kernel, ()) if resid is None else (total_kernel, (resid, far))
    return pl.pallas_call(
        kernel,
        out_shape=jax.ShapeDtypeStruct((rows, MODEL_WIDTH), jnp.bfloat16),
        scratch_shapes=[pltpu.VMEM((rows, MODEL_WIDTH), jnp.float32)],
        compiler_params=pltpu.CompilerParams(vmem_limit_bytes=32 * MIB),
        name="combine",
    )(made, weights, *more)


def slots_kernel(extras, far, half, experts, shards, topk, ids_ref, lengths_ref, choice_ref, *out_refs):
    pick_ref, weight_ref = out_refs
    device = ids_ref[3]
    first_expert = device // half * experts
    _, slots, rows = pick_ref.shape
    source = (device + half) % (2 * half) if far else device
    r = lax.broadcasted_iota(jnp.int32, (slots, rows), 0)
    index = source * rows + lax.broadcasted_iota(jnp.int32, (slots, rows), 1)
    slot = r % MAIN_SLOTS
    own_expert = (first_expert + r // (MAIN_SLOTS * shards)).astype(jnp.float32)
    named = jnp.zeros((slots, rows), jnp.float32)
    gate = jnp.zeros((slots, rows), jnp.float32)
    for k in range(topk):
        here = choice_ref[k : k + 1, :] == own_expert
        named = jnp.where(here, 1.0, named)
        gate = gate + jnp.where(here, choice_ref[topk + k : topk + k + 1, :], 0.0)
    named = jnp.where(index < segment_ends(lengths_ref)[-1], named, 0.0)
    i = lax.broadcasted_iota(jnp.int32, (rows, rows), 0)
    j = lax.broadcasted_iota(jnp.int32, (rows, rows), 1)
    earlier = jnp.where(i < j, 1.0, 0.0).astype(jnp.bfloat16)
    same = jnp.where(i == j, 1.0, 0.0).astype(jnp.bfloat16)
    rank = jnp.dot(named.astype(jnp.bfloat16), earlier, preferred_element_type=jnp.float32)
    rank = jnp.where(named > 0.0, rank, -1.0).astype(jnp.int32)
    high = gate.astype(jnp.bfloat16).astype(jnp.float32)

    def put(hit, pick_at, high_at, low_at):
        pick_at[...] = jnp.where(hit, 1.0, 0.0).astype(jnp.bfloat16)
        for values, at in ((high, high_at), (gate - high, low_at)):
            kept = jnp.where(hit, values, 0.0).astype(jnp.bfloat16)
            at[...] = lax.dot_general(
                same, kept, (((1,), (1,)), ((), ())), preferred_element_type=jnp.float32
            ).astype(jnp.bfloat16)

    put(rank == slot, pick_ref.at[0], weight_ref.at[0, 0], weight_ref.at[1, 0])
    if extras:
        for p in range(PIECES):
            hit = jnp.where(slot % PIECES == p, rank, -2) == MAIN_SLOTS + slot // PIECES
            put(hit, pick_ref.at[1 + p], weight_ref.at[0, 1 + p], weight_ref.at[1, 1 + p])


def slot_tables(ids, lengths, choice, far, half, experts, shards, extras):
    topk, rows = choice.shape[0] // 2, choice.shape[1]
    slots = experts * shards * MAIN_SLOTS
    kinds = 1 + PIECES if extras else 1
    shapes = [(kinds, slots, rows), (2, kinds, rows, slots)]
    smem = pl.BlockSpec(memory_space=pltpu.SMEM)
    return pl.pallas_call(
        functools.partial(slots_kernel, extras, far, half, experts, shards, topk),
        in_specs=[smem, smem, pl.BlockSpec(memory_space=pltpu.VMEM)],
        out_shape=[jax.ShapeDtypeStruct(shape, jnp.bfloat16) for shape in shapes],
        compiler_params=pltpu.CompilerParams(vmem_limit_bytes=32 * MIB),
        name="slots",
    )(ids, lengths, choice)


def attend_kernel(row_count, chips, ids_ref, lengths_ref, q_ref, rim_ref, pair_ref, sink_ref, w_ref, kept_ref, sent_ref, attended_ref):
    def attend_block(block):
        window = rim_ref.shape[0]
        rows = slice(block * window, (block + 1) * window)
        groups = pair_ref.shape[1] // LANES
        core = ids_ref[0]
        ends = segment_ends(lengths_ref)
        first = ids_ref[2] * (chips * 2 * row_count) + block * window
        query = first + lax.broadcasted_iota(jnp.int32, (window, 2 * window), 0)
        key = first - window + lax.broadcasted_iota(jnp.int32, (window, 2 * window), 1)
        query_segment = segment_of(query, ends)
        seen = (query_segment == segment_of(key, ends)) & (query_segment < NSEQ)
        seen = seen & (key >= 0) & (query >= key) & (query - key < window)
        lane = lax.broadcasted_iota(jnp.int32, (2 * window, LANES), 1)
        twos = QUERY_PER_KEY // 2
        for g in range(groups):
            at = slice(g * LANES, (g + 1) * LANES)
            before = pair_ref[(block - 1) * window : block * window, at] if block else rim_ref[:, at]
            pairs = jnp.concatenate([before, pair_ref[rows, at]], axis=0).astype(jnp.float32)
            keys = jnp.where(lane < HEAD_SIZE, pairs, 0.0)
            values = jnp.where(lane < HEAD_SIZE, 0.0, pairs)
            keys = [x.astype(jnp.bfloat16) for x in (keys, pltpu.roll(keys, HEAD_SIZE, 1))]
            values = [x.astype(jnp.bfloat16) for x in (pltpu.roll(values, HEAD_SIZE, 1), values)]
            start = g * twos * LANES
            queries = jnp.concatenate(
                [q_ref[rows, start + two * LANES : start + (two + 1) * LANES] for two in range(twos)],
                axis=0,
            )
            made = jnp.zeros((twos * window, LANES), jnp.float32)
            for side in range(2):
                scores = lax.dot_general(
                    queries, keys[side], (((1,), (1,)), ((), ())), preferred_element_type=jnp.float32
                )
                probs = []
                for two in range(twos):
                    sink = sink_ref[g * QUERY_PER_KEY + 2 * two + side]
                    weights = jnp.where(
                        seen, jnp.exp(scores[two * window : (two + 1) * window]), 0.0
                    )
                    totals = jnp.sum(weights, axis=-1, keepdims=True)
                    totals = totals + jnp.exp(jnp.full_like(totals, sink))
                    probs.append((weights * (1.0 / totals)).astype(jnp.bfloat16))
                made = made + jnp.dot(
                    jnp.concatenate(probs, axis=0), values[side], preferred_element_type=jnp.float32
                )
            made = made.astype(jnp.bfloat16)
            for two in range(twos):
                columns = slice(start + two * LANES, start + (two + 1) * LANES)
                for part in range(window // row_count):
                    head = block * (window // row_count) + part
                    place = (head % 2 + core) % 2 * chips + head // 2
                    row = two * window + part * row_count
                    attended_ref[
                        pl.ds(pl.multiple_of(place * row_count, 16), row_count), columns
                    ] = made[row : row + row_count]

    @pl.when(pl.program_id(0) == 0)
    def _():
        window = rim_ref.shape[0]
        for block in range(q_ref.shape[0] // window):
            attend_block(block)

    product = lax.dot_general(
        attended_ref[...],
        w_ref[...],
        (((1,), (1,)), ((), ())),
        preferred_element_type=jnp.float32,
    )
    for chip in range(chips):
        at, then = chip * row_count, (chips + chip) * row_count
        kept_ref[chip] = product[at : at + row_count]
        sent_ref[chip] = product[then : then + row_count].astype(jnp.bfloat16)


def attend(ids, lengths, queries, rim, pairs, sinks, w_out, row_count):
    total, columns = queries.shape
    width = w_out.shape[0]
    chips = total // (2 * row_count)
    tile = PIECE
    whole = lambda i, ids: (0, 0)
    smem = pl.BlockSpec(memory_space=pltpu.SMEM)
    return pl.pallas_call(
        functools.partial(attend_kernel, row_count, chips),
        grid_spec=pltpu.PrefetchScalarGridSpec(
            num_scalar_prefetch=1,
            grid=(pl.cdiv(width, tile),),
            in_specs=[
                smem,
                pl.BlockSpec(queries.shape, whole),
                pl.BlockSpec(rim.shape, whole),
                pl.BlockSpec(pairs.shape, whole),
                smem,
                pl.BlockSpec((tile, columns), lambda i, ids: (i, 0)),
            ],
            out_specs=[pl.BlockSpec((chips, row_count, tile), lambda i, ids: (0, 0, i))] * 2,
            scratch_shapes=[pltpu.VMEM(queries.shape, jnp.bfloat16)],
        ),
        out_shape=[
            jax.ShapeDtypeStruct((chips, row_count, width), jnp.float32),
            jax.ShapeDtypeStruct((chips, row_count, width), jnp.bfloat16),
        ],
        compiler_params=pltpu.CompilerParams(vmem_limit_bytes=60 * MIB),
        cost_estimate=pl.CostEstimate(
            flops=2 * total * columns * width, bytes_accessed=2 * columns * width, transcendentals=0
        ),
        name="attend",
    )(ids, lengths, queries, rim, pairs, sinks, w_out)


def page_order(page_table, n_tok, pages_dev):
    page_grid = page_table.reshape(n_tok, pages_dev)
    target = page_grid // pages_dev
    page_ids = jnp.arange(pages_dev, dtype=jnp.int32)
    earlier = page_ids[:, None] > page_ids[None, :]
    same_dest = target[:, :, None] == target[:, None, :]
    order_rank = jnp.sum((same_dest & earlier[None]).astype(jnp.int32), axis=2)
    return (target, order_rank, page_grid % pages_dev)


def exchanged_pages(pairs, page_table, tok_id, n_tok):
    rows = pairs.shape[0]
    groups = pairs.shape[1] // (2 * HEAD_SIZE)
    pages_dev = rows // PAGE_TOKENS
    share_count = pages_dev // n_tok
    paged = pairs.reshape(pages_dev, PAGE_TOKENS, groups, 2 * HEAD_SIZE).transpose(0, 2, 1, 3)
    target, order_rank, _ = page_order(page_table, n_tok, pages_dev)
    dest_ids = jnp.arange(n_tok, dtype=jnp.int32)
    share_ids = jnp.arange(share_count, dtype=jnp.int32)
    page_ids = jnp.arange(pages_dev, dtype=jnp.int32)
    matched = (target[tok_id][:, None, None] == dest_ids[None, :, None]) & (
        order_rank[tok_id][:, None, None] == share_ids[None, None, :]
    )
    pick_page = jnp.sum(jnp.where(matched, page_ids[:, None, None], 0), axis=0).reshape(-1)
    sent = paged[pick_page].reshape(n_tok, share_count * groups * PAGE_TOKENS, 2 * HEAD_SIZE)
    return lax.all_to_all(sent, "tok", split_axis=0, concat_axis=0, tiled=True)


def landed_pages(arrived, page_table, tok_id, n_tok, groups):
    share_count = arrived.shape[1] // (groups * PAGE_TOKENS)
    pages_dev = n_tok * share_count
    arrived = arrived.reshape(pages_dev, groups, PAGE_TOKENS, 2 * HEAD_SIZE)
    target, order_rank, slot_grid = page_order(page_table, n_tok, pages_dev)
    share_ids = jnp.arange(share_count, dtype=jnp.int32)
    page_ids = jnp.arange(pages_dev, dtype=jnp.int32)
    to_here = (target == tok_id)[:, :, None] & (order_rank[:, :, None] == share_ids[None, None, :])
    landing = jnp.sum(jnp.where(to_here, slot_grid[:, :, None], 0), axis=1).reshape(-1)
    source = jnp.sum(
        jnp.where(landing[None, :] == page_ids[:, None], page_ids[None, :], 0), axis=1
    )
    return arrived[source].transpose(1, 0, 2, 3)


def per_device(
    tokens,
    lengths,
    norm_gain_attn,
    query_key_value_weight,
    sinks,
    w_out_attn,
    norm_gain_moe,
    routes,
    gates,
    w_in,
    w_down,
    page_table,
):
    n_tok = lax.axis_size("tok")
    n_head = lax.axis_size("head")
    tok_id = lax.axis_index("tok")
    head_id = lax.axis_index("head")
    row_count, width = tokens.shape
    tok_dev = row_count * n_head
    groups = sinks.shape[0] // QUERY_PER_KEY
    n_y = n_head // 2
    y_id, core = head_id // 2, head_id % 2

    def to_core(array):
        return lax.ppermute(array, "head", [(h, h ^ 1) for h in range(n_head)])

    def along_y(array, by):
        return lax.ppermute(
            array, "head", [(h, (h // 2 + by) % n_y * 2 + h % 2) for h in range(n_head)]
        )

    n_dev = n_tok * n_head
    half = n_dev // 2

    def across(array):
        return lax.ppermute(array, ("tok", "head"), [(d, d ^ half) for d in range(n_dev)])

    def in_half(array):
        return lax.all_to_all(
            array,
            ("tok", "head"),
            split_axis=0,
            concat_axis=0,
            tiled=True,
            axis_index_groups=[list(range(half)), list(range(half, n_dev))],
        )

    flat_id = tok_id * n_head + head_id
    ids = jnp.stack([core, y_id, tok_id, flat_id]).astype(jnp.int32)
    choice = jnp.concatenate([routes.T.astype(jnp.float32), gates.T], axis=0)
    far_choice = across(choice)

    capacity = row_count // 8 + 2
    shards = n_dev // EXPERTS
    extras = capacity > MAIN_SLOTS
    tables = functools.partial(slot_tables, ids, lengths)
    sizes = (half, EXPERTS // 2, shards, extras)
    placed, block = [], tokens
    for k in range(n_y):
        if k:
            block, placed = lax.optimization_barrier((along_y(tokens, k), placed))
        placed = project(
            ids,
            lengths,
            k,
            n_y,
            block,
            to_core(block),
            norm_gain_attn,
            query_key_value_weight,
            placed,
        )
    placed, choice, far_choice = lax.optimization_barrier((placed, choice, far_choice))
    query_rows, key_value_pairs = placed
    rim_rows = passed_along(key_value_pairs[tok_dev - ATTEND_WINDOW :], "tok", 1)
    slots = tables(choice, False, *sizes), tables(far_choice, True, *sizes)
    rim_rows, slots = lax.optimization_barrier((rim_rows, slots))
    (own_picks, own_weights), (far_picks, far_weights) = slots
    kept, sent = attend(
        ids, lengths, query_rows, rim_rows, key_value_pairs, sinks, w_out_attn.T, row_count
    )
    sent = to_core(sent)

    def chip_sum(chip):
        here = lax.dynamic_index_in_dim(kept, chip, 0, keepdims=False)
        there = lax.dynamic_index_in_dim(sent, chip, 0, keepdims=False)
        return here + there.astype(jnp.float32)

    own_sum = chip_sum(y_id)
    leaving = [chip_sum((y_id + k) % n_y).astype(jnp.bfloat16) for k in range(1, n_y)]
    leaving, key_value_pairs = lax.optimization_barrier((leaving, key_value_pairs))
    other_sums = jnp.stack([along_y(part, k + 1) for k, part in enumerate(leaving)])
    pages = exchanged_pages(key_value_pairs, page_table, tok_id, n_tok)
    other_sums, pages = lax.optimization_barrier((other_sums, pages))

    resid, moe_in = finish_attention(
        tokens, own_sum, other_sums, norm_gain_moe
    )
    far_moe_in = across(moe_in)
    own_packed = pack(moe_in, own_picks, 64 * MIB)

    def exchanged(packed):
        slots, held = packed.shape
        return in_half(packed.reshape(half, MAIN_SLOTS, held)).reshape(slots, held)

    def exchanged_beside(packed):
        return lax.cond(lengths[0] > 0, exchanged, jnp.zeros_like, packed)

    own_arrived = exchanged_beside(own_packed)
    far_moe_in, own_arrived = lax.optimization_barrier((far_moe_in, own_arrived))
    far_arrived = exchanged(pack(far_moe_in, far_picks, MIB))
    own_act = expert(own_arrived, w_in, w_down, extras, down=False)
    far_arrived, own_act = lax.optimization_barrier((far_arrived, own_act))
    far_made = expert(far_arrived, w_in, w_down, extras)
    far_made, own_act = lax.optimization_barrier((far_made, own_act))
    far_returned = exchanged(far_made)
    own_made = expert_down(own_act, w_down, *own_packed.shape, extras)
    far_returned, own_made = lax.optimization_barrier((far_returned, own_made))
    far_part, own_made = lax.optimization_barrier((combine(far_returned, far_weights), own_made))
    far_sum = across(far_part)
    own_returned = exchanged_beside(own_made)
    hidden_out = combine(own_returned, own_weights, resid, far_sum)
    kv_cache = landed_pages(pages, page_table, tok_id, n_tok, groups)
    return (hidden_out, kv_cache)


def solution(mesh):
    return jax.shard_map(
        per_device,
        mesh=mesh,
        in_specs=(
            P(("tok", "head"), None),
            P(),
            P(),
            P(None, "head"),
            P("head"),
            P("head", None),
            P(),
            P(("tok", "head"), None),
            P(("tok", "head"), None),
            P(("tok", "head"), None, None),
            P(("tok", "head"), None, None),
            P(),
        ),
        out_specs=(P(("tok", "head"), None), P("head", "tok", None, None)),
        check_vma=False,
    )
```

```python
import functools
import math

import jax
import jax.numpy as jnp
from jax import lax
from jax.experimental import pallas as pl
from jax.experimental.pallas import tpu as pltpu
from jax.sharding import PartitionSpec as P

MODEL_WIDTH = 2880
HEAD_SIZE = 64
EXPERTS = 32
ATTEND_WINDOW = 128
NSEQ = 4
PAGE_TOKENS = 16
QUERY_PER_KEY = 8


EPSILON = 1e-05
ROPE_BASE = 150000.0
GLU_ALPHA = 1.702

LANES = 128
MAIN_SLOTS = 8
PIECE = 768
PIECES = 4
EXTRA_AT = 2944
IN_TILE = 1920
FIRST_COPY = 1
DOWN_COPIES = 4
MIB = 1 << 20


def passed_along(array, axis, by):
    peers = lax.axis_size(axis)
    pairs = [(i, i + by) for i in range(peers) if 0 <= i + by < peers]
    return lax.ppermute(array, axis, pairs)


def segment_ends(lengths_ref):
    ends, end = [], 0
    for k in range(NSEQ):
        end = end + lengths_ref[k]
        ends.append(end)
    return ends


def segment_of(index, ends):
    segment = jnp.zeros_like(index)
    for end in ends:
        segment = segment + jnp.where(index >= end, 1, 0)
    return segment


def rope_tables(index, ends):
    start = jnp.zeros_like(index)
    for end in ends:
        start = jnp.where(index >= end, end, start)
    half = HEAD_SIZE // 2
    lane = lax.broadcasted_iota(jnp.int32, index.shape, 1)
    inv_freq = jnp.exp(
        (lane % half).astype(jnp.float32) * (-2.0 * math.log(ROPE_BASE) / HEAD_SIZE)
    )
    angles = (index - start).astype(jnp.float32) * inv_freq
    low = lane % HEAD_SIZE < half
    sin = jnp.sin(angles)
    return jnp.cos(angles), jnp.where(low, -sin, sin), low, lane


def qkv_kernel(step, chips, ids_ref, lengths_ref, own_ref, other_ref, gain_ref, w_ref, *refs):
    q_ref, kv_ref, xn_ref, cos_ref, sin_ref = refs[-5:]
    rows = own_ref.shape[0]
    core, chip, shard = ids_ref[0], (ids_ref[1] + chips - step) % chips, ids_ref[2]

    @pl.when(pl.program_id(0) == 0)
    def _():
        for at, ref in ((core, own_ref), (1 - core, other_ref)):
            wide = ref[...].astype(jnp.float32)
            inv_rms = lax.rsqrt(jnp.mean(wide * wide, axis=-1, keepdims=True) + EPSILON)
            normed = (wide * inv_rms * gain_ref[...][None]).astype(jnp.bfloat16)
            xn_ref[pl.ds(pl.multiple_of(at * rows, 16), rows), :] = normed
        first = (shard * chips + chip) * 2 * rows
        index = first + lax.broadcasted_iota(jnp.int32, cos_ref.shape, 0)
        cos, sin, _, _ = rope_tables(index, segment_ends(lengths_ref))
        cos_ref[...] = cos
        sin_ref[...] = sin

    projected = jnp.dot(xn_ref[...], w_ref[...], preferred_element_type=jnp.float32)
    cos, sin = cos_ref[...], sin_ref[...]
    lane = lax.broadcasted_iota(jnp.int32, cos.shape, 1)
    low = lane % HEAD_SIZE < HEAD_SIZE // 2

    def turned(u):
        return jnp.where(low, pltpu.roll(u, LANES - 32, 1), pltpu.roll(u, 32, 1))

    for b in range(QUERY_PER_KEY // 2):
        u = projected[:, b * LANES : (b + 1) * LANES]
        q_ref[:, b * LANES : (b + 1) * LANES] = (
            (u * cos + turned(u) * sin) * HEAD_SIZE ** (-0.5)
        ).astype(jnp.bfloat16)
    u = projected[:, QUERY_PER_KEY * HEAD_SIZE :]
    rotated = u * cos + turned(u) * sin
    kv_ref[...] = jnp.where(lane < HEAD_SIZE, rotated, u).astype(jnp.bfloat16)


def project(ids, lengths, step, chips, own, other, gain, weight, earlier):
    rows, width = own.shape
    columns = weight.shape[1]
    group = (QUERY_PER_KEY + 2) * HEAD_SIZE
    qs, kvs = QUERY_PER_KEY * HEAD_SIZE, 2 * HEAD_SIZE
    groups = columns // group
    whole = lambda g, ids: (0, 0)
    by_group = lambda g, ids: ((ids[1] + chips - step) % chips, g)
    return pl.pallas_call(
        functools.partial(qkv_kernel, step, chips),
        grid_spec=pltpu.PrefetchScalarGridSpec(
            num_scalar_prefetch=1,
            grid=(groups,),
            in_specs=[
                pl.BlockSpec(memory_space=pltpu.SMEM),
                pl.BlockSpec((rows, width), whole),
                pl.BlockSpec((rows, width), whole),
                pl.BlockSpec((width,), lambda g, ids: (0,)),
                pl.BlockSpec((width, group), lambda g, ids: (0, g)),
            ]
            + [pl.BlockSpec(memory_space=pl.ANY)] * len(earlier),
            out_specs=[
                pl.BlockSpec((2 * rows, qs), by_group),
                pl.BlockSpec((2 * rows, kvs), by_group),
            ],
            scratch_shapes=[
                pltpu.VMEM((2 * rows, width), jnp.bfloat16),
                pltpu.VMEM((2 * rows, LANES), jnp.float32),
                pltpu.VMEM((2 * rows, LANES), jnp.float32),
            ],
        ),
        out_shape=[
            jax.ShapeDtypeStruct((2 * rows * chips, groups * qs), jnp.bfloat16),
            jax.ShapeDtypeStruct((2 * rows * chips, groups * kvs), jnp.bfloat16),
        ],
        input_output_aliases={6: 0, 7: 1} if earlier else {},
        compiler_params=pltpu.CompilerParams(vmem_limit_bytes=60 * MIB),
        cost_estimate=pl.CostEstimate(
            flops=4 * rows * width * columns, bytes_accessed=2 * width * columns, transcendentals=0
        ),
        name="project",
    )(ids, lengths, own, other, gain, weight, *earlier)


def pack_rows(values_ref, pick_ref, packed_ref):
    packed_ref[:, :EXTRA_AT] = jnp.dot(
        pick_ref[0], values_ref[:, :EXTRA_AT], preferred_element_type=jnp.float32
    ).astype(jnp.bfloat16)
    pieces = jnp.zeros((packed_ref.shape[0], packed_ref.shape[1] - EXTRA_AT), jnp.float32)
    for p in range(pick_ref.shape[0] - 1):
        pieces = pieces + jnp.dot(
            pick_ref[1 + p],
            values_ref[:, p * PIECE : (p + 1) * PIECE],
            preferred_element_type=jnp.float32,
        )
    packed_ref[:, EXTRA_AT:] = pieces.astype(jnp.bfloat16)


def resid_kernel(tokens_ref, own_ref, others_ref, gain_ref, resid_ref, moe_ref):
    resid = tokens_ref[...].astype(jnp.float32) + own_ref[...].astype(jnp.float32)
    for k in range(others_ref.shape[0]):
        resid = resid + others_ref[k].astype(jnp.float32)
    resid_ref[...] = resid
    inv_rms = lax.rsqrt(jnp.mean(resid * resid, axis=-1, keepdims=True) + EPSILON)
    moe_ref[...] = (resid * inv_rms * gain_ref[...][None]).astype(jnp.bfloat16)


def pack_kernel(moe_ref, pick_ref, packed_ref, values_ref):
    width = moe_ref.shape[1]
    values_ref[:, width:] = jnp.zeros_like(values_ref[:, width:])
    values_ref[:, :width] = moe_ref[...]
    pack_rows(values_ref, pick_ref, packed_ref)


def packed_width(extras):
    return EXTRA_AT + PIECE if extras else PIECES * PIECE


def finish_attention(tokens, own, others, gain):
    rows, width = tokens.shape
    return pl.pallas_call(
        resid_kernel,
        out_shape=[
            jax.ShapeDtypeStruct((rows, width), jnp.float32),
            jax.ShapeDtypeStruct((rows, width), jnp.bfloat16),
        ],
        compiler_params=pltpu.CompilerParams(vmem_limit_bytes=32 * MIB),
        name="finish_attention",
    )(tokens, own, others, gain)


def pack(moe_in, picks, beside):
    rows, width = moe_in.shape
    kinds, slots, _ = picks.shape
    return pl.pallas_call(
        pack_kernel,
        out_shape=jax.ShapeDtypeStruct((slots, packed_width(kinds > 1)), jnp.bfloat16),
        scratch_shapes=[pltpu.VMEM((rows, PIECES * PIECE), jnp.bfloat16)],
        compiler_params=pltpu.CompilerParams(vmem_limit_bytes=32 * MIB),
        cost_estimate=pl.CostEstimate(
            flops=2 * slots * rows * 2 * width, bytes_accessed=beside, transcendentals=0
        ),
        name="pack",
    )(moe_in, picks)


def piece_of(count, slots, piece):
    t = lax.broadcasted_iota(jnp.int32, (count, slots), 0)
    r = lax.broadcasted_iota(jnp.int32, (count, slots), 1)
    return jnp.where(r == PIECES * t + piece, 1.0, 0.0).astype(jnp.bfloat16)


def fill_rows(packed_ref, x_ref, extras):
    slots, width = packed_ref.shape[0], x_ref.shape[1]
    x_ref[:slots, :] = packed_ref[:, :width]
    if extras:
        further = slots // PIECES
        for p in range(PIECES):
            extent = min(PIECE, width - p * PIECE)
            x_ref[slots:, p * PIECE : p * PIECE + extent] = jnp.dot(
                piece_of(further, slots, p),
                packed_ref[:, EXTRA_AT : EXTRA_AT + extent],
                preferred_element_type=jnp.float32,
            ).astype(jnp.bfloat16)


def activate(gate_up_ref, act_ref):
    rows, ffs = act_ref.shape
    base = ffs // LANES * LANES
    chunk = 32
    for r in range(0, rows, chunk):
        gate = gate_up_ref[r : r + chunk, :ffs]
        up = gate_up_ref[r : r + chunk, base:]
        if ffs > base:
            up = pltpu.roll(up, up.shape[1] - (ffs - base), 1)
        up = up[:, :ffs]
        act_ref[r : r + chunk, :] = (
            (up + 1.0) * gate * jax.nn.sigmoid(GLU_ALPHA * gate)
        ).astype(jnp.bfloat16)


def put_piece(piece, made, out_ref, width, piece_ref):
    slots = out_ref.shape[0]
    extent = made.shape[1]
    if extent < PIECE:
        out_ref[:, piece * PIECE + extent : (piece + 1) * PIECE] = jnp.zeros(
            (slots, PIECE - extent), jnp.bfloat16
        )
        out_ref[:, piece * PIECE : piece * PIECE + extent] = made[:slots]
    else:
        start = piece * PIECE
        start = start if isinstance(piece, int) else pl.multiple_of(start, LANES)
        out_ref[:, pl.ds(start, extent)] = made[:slots]
    if piece_ref is not None:
        further = slots // PIECES
        t = lax.broadcasted_iota(jnp.int32, (slots, further), 1)
        r = lax.broadcasted_iota(jnp.int32, (slots, further), 0)
        spread = jnp.where(r == PIECES * t + piece, 1.0, 0.0).astype(jnp.bfloat16)
        part = jnp.dot(spread, made[slots:], preferred_element_type=jnp.float32).astype(
            jnp.bfloat16
        )
        if isinstance(piece, int):
            if piece == 0:
                piece_ref[...] = part
            else:
                piece_ref[:, :extent] = piece_ref[:, :extent] + part
            if piece == PIECES - 1:
                out_ref[:, EXTRA_AT:] = piece_ref[...]
            return

        @pl.when(piece == 0)
        def _():
            piece_ref[...] = part

        @pl.when(piece > 0)
        def _():
            piece_ref[...] = piece_ref[...] + part

        @pl.when(piece == PIECES - 1)
        def _():
            out_ref[:, EXTRA_AT:] = piece_ref[...]


def expert_kernel(extras, in_tiles, down, *refs):
    packed_ref, w_in_ref = refs[:2]
    scratch = refs[4:] if down else refs[3:]
    x_ref, gate_up_ref = scratch[:2]
    act_ref = scratch[2] if down else refs[2]
    step = pl.program_id(0)
    copies = []
    if down:
        w_down_ref, out_ref = refs[2:4]
        held_ref, total_ref, sems = scratch[3:6]
        piece_ref = scratch[6] if extras else None
        ffs = held_ref.shape[0]
        rows = pl.cdiv(ffs, DOWN_COPIES * LANES) * LANES
        for c in range(pl.cdiv(ffs, rows)):
            part = pl.ds(c * rows, min(rows, ffs - c * rows))
            copies.append(
                pltpu.make_async_copy(w_down_ref.at[0, part], held_ref.at[part], sems.at[c])
            )

    @pl.when(step == 0)
    def _():
        fill_rows(packed_ref, x_ref, extras)

    for c, copy in enumerate(copies):
        pl.when(step == min(c + FIRST_COPY, in_tiles - 1))(copy.start)

    tile = w_in_ref.shape[2]
    made = jnp.dot(x_ref[...], w_in_ref[0], preferred_element_type=jnp.float32)
    if in_tiles == 1:
        gate_up_ref[...] = made
    else:
        gate_up_ref[:, pl.ds(pl.multiple_of(step * tile, LANES), tile)] = made

    @pl.when(step == in_tiles - 1)
    def _():
        activate(gate_up_ref, act_ref)
        if down:
            width = x_ref.shape[1]
            for c, copy in enumerate(copies):
                copy.wait()
                part = slice(c * rows, min((c + 1) * rows, ffs))
                term = jnp.dot(
                    act_ref[:, part], held_ref[part, :], preferred_element_type=jnp.float32
                )
                total_ref[...] = term if c == 0 else total_ref[...] + term
            for piece in range(PIECES):
                extent = min(PIECE, width - piece * PIECE)
                made = total_ref[:, piece * PIECE : piece * PIECE + extent].astype(jnp.bfloat16)
                put_piece(piece, made, out_ref, width, piece_ref)


def down_kernel(extras, width, act_ref, w_down_ref, out_ref, *scratch):
    piece = pl.program_id(0)
    made = jnp.dot(act_ref[...], w_down_ref[0], preferred_element_type=jnp.float32)
    column = lax.broadcasted_iota(jnp.int32, made.shape, 1) + piece * PIECE
    made = jnp.where(column < width, made, 0.0).astype(jnp.bfloat16)
    put_piece(piece, made, out_ref, width, scratch[0] if extras else None)


def expert(packed, w_in, w_down, extras, down=True):
    slots, held = packed.shape
    width = w_in.shape[1]
    ffs = w_down.shape[1]
    rows = slots + (slots // PIECES if extras else 0)
    tile = min(IN_TILE, 2 * ffs)
    in_tiles = pl.cdiv(2 * ffs, tile)
    whole = lambda i: (0, 0)
    in_specs = [
        pl.BlockSpec((slots, held), whole),
        pl.BlockSpec((1, width, tile), lambda i: (0, 0, i)),
    ]
    scratch = [
        pltpu.VMEM((rows, width), jnp.bfloat16),
        pltpu.VMEM((rows, in_tiles * tile), jnp.float32),
    ]
    args = (packed, w_in)
    out = (rows, ffs)
    if down:
        in_specs += [pl.BlockSpec(memory_space=pl.ANY)]
        scratch += [
            pltpu.VMEM((rows, ffs), jnp.bfloat16),
            pltpu.VMEM((ffs, width), jnp.bfloat16),
            pltpu.VMEM((rows, width), jnp.float32),
            pltpu.SemaphoreType.DMA((DOWN_COPIES,)),
        ]
        scratch += [pltpu.VMEM((slots, PIECE), jnp.bfloat16)] if extras else []
        args += (w_down,)
        out = (slots, held)
    parts = 6 if down else 4
    return pl.pallas_call(
        functools.partial(expert_kernel, extras, in_tiles, down),
        grid=(in_tiles,),
        in_specs=in_specs,
        out_specs=pl.BlockSpec(out, whole),
        out_shape=jax.ShapeDtypeStruct(out, jnp.bfloat16),
        scratch_shapes=scratch,
        compiler_params=pltpu.CompilerParams(vmem_limit_bytes=56 * MIB),
        cost_estimate=pl.CostEstimate(
            flops=parts * rows * width * ffs,
            bytes_accessed=parts * width * ffs,
            transcendentals=rows * ffs,
        ),
        name="expert" if down else "expert_up",
    )(*args)


def expert_down(act, w_down, slots, held, extras):
    rows, ffs = act.shape
    width = w_down.shape[2]
    whole = lambda i: (0, 0)
    return pl.pallas_call(
        functools.partial(down_kernel, extras, width),
        grid=(PIECES,),
        in_specs=[
            pl.BlockSpec((rows, ffs), whole),
            pl.BlockSpec((1, ffs, PIECE), lambda i: (0, 0, i)),
        ],
        out_specs=pl.BlockSpec((slots, held), whole),
        out_shape=jax.ShapeDtypeStruct((slots, held), jnp.bfloat16),
        scratch_shapes=[pltpu.VMEM((slots, PIECE), jnp.bfloat16)] if extras else [],
        compiler_params=pltpu.CompilerParams(vmem_limit_bytes=56 * MIB),
        cost_estimate=pl.CostEstimate(
            flops=2 * rows * width * ffs, bytes_accessed=2 * width * ffs, transcendentals=0
        ),
        name="expert_down",
    )(act, w_down)


def weighted_sum(made_ref, weight_ref, total_ref):
    width = total_ref.shape[1]
    for term in range(2):
        made = jnp.dot(
            weight_ref[term, 0], made_ref[:, :width], preferred_element_type=jnp.float32
        )
        total_ref[...] = made if term == 0 else total_ref[...] + made
        for p in range(weight_ref.shape[1] - 1):
            extent = min(PIECE, width - p * PIECE)
            at = slice(p * PIECE, p * PIECE + extent)
            total_ref[:, at] = total_ref[:, at] + jnp.dot(
                weight_ref[term, 1 + p],
                made_ref[:, EXTRA_AT : EXTRA_AT + extent],
                preferred_element_type=jnp.float32,
            )


def partial_kernel(made_ref, weight_ref, out_ref, total_ref):
    weighted_sum(made_ref, weight_ref, total_ref)
    out_ref[...] = total_ref[...].astype(jnp.bfloat16)


def total_kernel(made_ref, weight_ref, resid_ref, far_ref, out_ref, total_ref):
    weighted_sum(made_ref, weight_ref, total_ref)
    out_ref[...] = (
        resid_ref[...] + (total_ref[...] + far_ref[...].astype(jnp.float32))
    ).astype(jnp.bfloat16)


def combine(made, weights, resid=None, far=None):
    rows = weights.shape[2]
    kernel, more = (partial_kernel, ()) if resid is None else (total_kernel, (resid, far))
    return pl.pallas_call(
        kernel,
        out_shape=jax.ShapeDtypeStruct((rows, MODEL_WIDTH), jnp.bfloat16),
        scratch_shapes=[pltpu.VMEM((rows, MODEL_WIDTH), jnp.float32)],
        compiler_params=pltpu.CompilerParams(vmem_limit_bytes=32 * MIB),
        name="combine",
    )(made, weights, *more)


def slots_kernel(extras, far, half, experts, shards, topk, ids_ref, lengths_ref, choice_ref, *out_refs):
    pick_ref, weight_ref = out_refs
    device = ids_ref[3]
    first_expert = device // half * experts
    _, slots, rows = pick_ref.shape
    source = (device + half) % (2 * half) if far else device
    r = lax.broadcasted_iota(jnp.int32, (slots, rows), 0)
    index = source * rows + lax.broadcasted_iota(jnp.int32, (slots, rows), 1)
    slot = r % MAIN_SLOTS
    own_expert = (first_expert + r // (MAIN_SLOTS * shards)).astype(jnp.float32)
    named = jnp.zeros((slots, rows), jnp.float32)
    gate = jnp.zeros((slots, rows), jnp.float32)
    for k in range(topk):
        here = choice_ref[k : k + 1, :] == own_expert
        named = jnp.where(here, 1.0, named)
        gate = gate + jnp.where(here, choice_ref[topk + k : topk + k + 1, :], 0.0)
    named = jnp.where(index < segment_ends(lengths_ref)[-1], named, 0.0)
    i = lax.broadcasted_iota(jnp.int32, (rows, rows), 0)
    j = lax.broadcasted_iota(jnp.int32, (rows, rows), 1)
    earlier = jnp.where(i < j, 1.0, 0.0).astype(jnp.bfloat16)
    same = jnp.where(i == j, 1.0, 0.0).astype(jnp.bfloat16)
    rank = jnp.dot(named.astype(jnp.bfloat16), earlier, preferred_element_type=jnp.float32)
    rank = jnp.where(named > 0.0, rank, -1.0).astype(jnp.int32)
    high = gate.astype(jnp.bfloat16).astype(jnp.float32)

    def put(hit, pick_at, high_at, low_at):
        pick_at[...] = jnp.where(hit, 1.0, 0.0).astype(jnp.bfloat16)
        for values, at in ((high, high_at), (gate - high, low_at)):
            kept = jnp.where(hit, values, 0.0).astype(jnp.bfloat16)
            at[...] = lax.dot_general(
                same, kept, (((1,), (1,)), ((), ())), preferred_element_type=jnp.float32
            ).astype(jnp.bfloat16)

    put(rank == slot, pick_ref.at[0], weight_ref.at[0, 0], weight_ref.at[1, 0])
    if extras:
        for p in range(PIECES):
            hit = jnp.where(slot % PIECES == p, rank, -2) == MAIN_SLOTS + slot // PIECES
            put(hit, pick_ref.at[1 + p], weight_ref.at[0, 1 + p], weight_ref.at[1, 1 + p])


def slot_tables(ids, lengths, choice, far, half, experts, shards, extras):
    topk, rows = choice.shape[0] // 2, choice.shape[1]
    slots = experts * shards * MAIN_SLOTS
    kinds = 1 + PIECES if extras else 1
    shapes = [(kinds, slots, rows), (2, kinds, rows, slots)]
    smem = pl.BlockSpec(memory_space=pltpu.SMEM)
    return pl.pallas_call(
        functools.partial(slots_kernel, extras, far, half, experts, shards, topk),
        in_specs=[smem, smem, pl.BlockSpec(memory_space=pltpu.VMEM)],
        out_shape=[jax.ShapeDtypeStruct(shape, jnp.bfloat16) for shape in shapes],
        compiler_params=pltpu.CompilerParams(vmem_limit_bytes=32 * MIB),
        name="slots",
    )(ids, lengths, choice)


def attend_kernel(row_count, chips, ids_ref, lengths_ref, q_ref, rim_ref, pair_ref, sink_ref, w_ref, kept_ref, sent_ref, attended_ref):
    def attend_block(block):
        window = rim_ref.shape[0]
        rows = slice(block * window, (block + 1) * window)
        groups = pair_ref.shape[1] // LANES
        core = ids_ref[0]
        ends = segment_ends(lengths_ref)
        first = ids_ref[2] * (chips * 2 * row_count) + block * window
        query = first + lax.broadcasted_iota(jnp.int32, (window, 2 * window), 0)
        key = first - window + lax.broadcasted_iota(jnp.int32, (window, 2 * window), 1)
        query_segment = segment_of(query, ends)
        seen = (query_segment == segment_of(key, ends)) & (query_segment < NSEQ)
        seen = seen & (key >= 0) & (query >= key) & (query - key < window)
        lane = lax.broadcasted_iota(jnp.int32, (2 * window, LANES), 1)
        twos = QUERY_PER_KEY // 2
        for g in range(groups):
            at = slice(g * LANES, (g + 1) * LANES)
            before = pair_ref[(block - 1) * window : block * window, at] if block else rim_ref[:, at]
            pairs = jnp.concatenate([before, pair_ref[rows, at]], axis=0).astype(jnp.float32)
            keys = jnp.where(lane < HEAD_SIZE, pairs, 0.0)
            values = jnp.where(lane < HEAD_SIZE, 0.0, pairs)
            keys = [x.astype(jnp.bfloat16) for x in (keys, pltpu.roll(keys, HEAD_SIZE, 1))]
            values = [x.astype(jnp.bfloat16) for x in (pltpu.roll(values, HEAD_SIZE, 1), values)]
            start = g * twos * LANES
            queries = jnp.concatenate(
                [q_ref[rows, start + two * LANES : start + (two + 1) * LANES] for two in range(twos)],
                axis=0,
            )
            made = jnp.zeros((twos * window, LANES), jnp.float32)
            for side in range(2):
                scores = lax.dot_general(
                    queries, keys[side], (((1,), (1,)), ((), ())), preferred_element_type=jnp.float32
                )
                probs = []
                for two in range(twos):
                    sink = sink_ref[g * QUERY_PER_KEY + 2 * two + side]
                    weights = jnp.where(
                        seen, jnp.exp(scores[two * window : (two + 1) * window]), 0.0
                    )
                    totals = jnp.sum(weights, axis=-1, keepdims=True)
                    totals = totals + jnp.exp(jnp.full_like(totals, sink))
                    probs.append((weights * (1.0 / totals)).astype(jnp.bfloat16))
                made = made + jnp.dot(
                    jnp.concatenate(probs, axis=0), values[side], preferred_element_type=jnp.float32
                )
            made = made.astype(jnp.bfloat16)
            for two in range(twos):
                columns = slice(start + two * LANES, start + (two + 1) * LANES)
                for part in range(window // row_count):
                    head = block * (window // row_count) + part
                    place = (head % 2 + core) % 2 * chips + head // 2
                    row = two * window + part * row_count
                    attended_ref[
                        pl.ds(pl.multiple_of(place * row_count, 16), row_count), columns
                    ] = made[row : row + row_count]

    @pl.when(pl.program_id(0) == 0)
    def _():
        window = rim_ref.shape[0]
        for block in range(q_ref.shape[0] // window):
            attend_block(block)

    product = lax.dot_general(
        attended_ref[...],
        w_ref[...],
        (((1,), (1,)), ((), ())),
        preferred_element_type=jnp.float32,
    )
    for chip in range(chips):
        at, then = chip * row_count, (chips + chip) * row_count
        kept_ref[chip] = product[at : at + row_count]
        sent_ref[chip] = product[then : then + row_count].astype(jnp.bfloat16)


def attend(ids, lengths, queries, rim, pairs, sinks, w_out, row_count):
    total, columns = queries.shape
    width = w_out.shape[0]
    chips = total // (2 * row_count)
    tile = PIECE
    whole = lambda i, ids: (0, 0)
    smem = pl.BlockSpec(memory_space=pltpu.SMEM)
    return pl.pallas_call(
        functools.partial(attend_kernel, row_count, chips),
        grid_spec=pltpu.PrefetchScalarGridSpec(
            num_scalar_prefetch=1,
            grid=(pl.cdiv(width, tile),),
            in_specs=[
                smem,
                pl.BlockSpec(queries.shape, whole),
                pl.BlockSpec(rim.shape, whole),
                pl.BlockSpec(pairs.shape, whole),
                smem,
                pl.BlockSpec((tile, columns), lambda i, ids: (i, 0)),
            ],
            out_specs=[pl.BlockSpec((chips, row_count, tile), lambda i, ids: (0, 0, i))] * 2,
            scratch_shapes=[pltpu.VMEM(queries.shape, jnp.bfloat16)],
        ),
        out_shape=[
            jax.ShapeDtypeStruct((chips, row_count, width), jnp.float32),
            jax.ShapeDtypeStruct((chips, row_count, width), jnp.bfloat16),
        ],
        compiler_params=pltpu.CompilerParams(vmem_limit_bytes=60 * MIB),
        cost_estimate=pl.CostEstimate(
            flops=2 * total * columns * width, bytes_accessed=2 * columns * width, transcendentals=0
        ),
        name="attend",
    )(ids, lengths, queries, rim, pairs, sinks, w_out)


def page_order(page_table, n_tok, pages_dev):
    page_grid = page_table.reshape(n_tok, pages_dev)
    target = page_grid // pages_dev
    page_ids = jnp.arange(pages_dev, dtype=jnp.int32)
    earlier = page_ids[:, None] > page_ids[None, :]
    same_dest = target[:, :, None] == target[:, None, :]
    order_rank = jnp.sum((same_dest & earlier[None]).astype(jnp.int32), axis=2)
    return (target, order_rank, page_grid % pages_dev)


def exchanged_pages(pairs, page_table, tok_id, n_tok):
    rows = pairs.shape[0]
    groups = pairs.shape[1] // (2 * HEAD_SIZE)
    pages_dev = rows // PAGE_TOKENS
    share_count = pages_dev // n_tok
    paged = pairs.reshape(pages_dev, PAGE_TOKENS, groups, 2 * HEAD_SIZE).transpose(0, 2, 1, 3)
    target, order_rank, _ = page_order(page_table, n_tok, pages_dev)
    dest_ids = jnp.arange(n_tok, dtype=jnp.int32)
    share_ids = jnp.arange(share_count, dtype=jnp.int32)
    page_ids = jnp.arange(pages_dev, dtype=jnp.int32)
    matched = (target[tok_id][:, None, None] == dest_ids[None, :, None]) & (
        order_rank[tok_id][:, None, None] == share_ids[None, None, :]
    )
    pick_page = jnp.sum(jnp.where(matched, page_ids[:, None, None], 0), axis=0).reshape(-1)
    sent = paged[pick_page].reshape(n_tok, share_count * groups * PAGE_TOKENS, 2 * HEAD_SIZE)
    return lax.all_to_all(sent, "tok", split_axis=0, concat_axis=0, tiled=True)


def landed_pages(arrived, page_table, tok_id, n_tok, groups):
    share_count = arrived.shape[1] // (groups * PAGE_TOKENS)
    pages_dev = n_tok * share_count
    arrived = arrived.reshape(pages_dev, groups, PAGE_TOKENS, 2 * HEAD_SIZE)
    target, order_rank, slot_grid = page_order(page_table, n_tok, pages_dev)
    share_ids = jnp.arange(share_count, dtype=jnp.int32)
    page_ids = jnp.arange(pages_dev, dtype=jnp.int32)
    to_here = (target == tok_id)[:, :, None] & (order_rank[:, :, None] == share_ids[None, None, :])
    landing = jnp.sum(jnp.where(to_here, slot_grid[:, :, None], 0), axis=1).reshape(-1)
    source = jnp.sum(
        jnp.where(landing[None, :] == page_ids[:, None], page_ids[None, :], 0), axis=1
    )
    return arrived[source].transpose(1, 0, 2, 3)


def per_device(
    tokens,
    lengths,
    norm_gain_attn,
    query_key_value_weight,
    sinks,
    w_out_attn,
    norm_gain_moe,
    routes,
    gates,
    w_in,
    w_down,
    page_table,
):
    n_tok = lax.axis_size("tok")
    n_head = lax.axis_size("head")
    tok_id = lax.axis_index("tok")
    head_id = lax.axis_index("head")
    row_count, width = tokens.shape
    tok_dev = row_count * n_head
    groups = sinks.shape[0] // QUERY_PER_KEY
    n_y = n_head // 2
    y_id, core = head_id // 2, head_id % 2

    def to_core(array):
        return lax.ppermute(array, "head", [(h, h ^ 1) for h in range(n_head)])

    def along_y(array, by):
        return lax.ppermute(
            array, "head", [(h, (h // 2 + by) % n_y * 2 + h % 2) for h in range(n_head)]
        )

    n_dev = n_tok * n_head
    half = n_dev // 2

    def across(array):
        return lax.ppermute(array, ("tok", "head"), [(d, d ^ half) for d in range(n_dev)])

    def in_half(array):
        return lax.all_to_all(
            array,
            ("tok", "head"),
            split_axis=0,
            concat_axis=0,
            tiled=True,
            axis_index_groups=[list(range(half)), list(range(half, n_dev))],
        )

    flat_id = tok_id * n_head + head_id
    ids = jnp.stack([core, y_id, tok_id, flat_id]).astype(jnp.int32)
    choice = jnp.concatenate([routes.T.astype(jnp.float32), gates.T], axis=0)

    capacity = row_count // 8 + 2
    shards = n_dev // EXPERTS
    extras = capacity > MAIN_SLOTS
    tables = functools.partial(slot_tables, ids, lengths)
    sizes = (half, EXPERTS // 2, shards, extras)
    placed, block = [], tokens
    for k in range(n_y):
        if k:
            block, placed, choice = lax.optimization_barrier((along_y(tokens, k), placed, choice))
        placed = project(
            ids,
            lengths,
            k,
            n_y,
            block,
            to_core(block),
            norm_gain_attn,
            query_key_value_weight,
            placed,
        )
    far_choice = across(choice)
    placed, choice, far_choice = lax.optimization_barrier((placed, choice, far_choice))
    query_rows, key_value_pairs = placed
    rim_rows = passed_along(key_value_pairs[tok_dev - ATTEND_WINDOW :], "tok", 1)
    slots = tables(choice, False, *sizes), tables(far_choice, True, *sizes)
    rim_rows, slots = lax.optimization_barrier((rim_rows, slots))
    (own_picks, own_weights), (far_picks, far_weights) = slots
    kept, sent = attend(
        ids, lengths, query_rows, rim_rows, key_value_pairs, sinks, w_out_attn.T, row_count
    )
    sent = to_core(sent)

    def chip_sum(chip):
        here = lax.dynamic_index_in_dim(kept, chip, 0, keepdims=False)
        there = lax.dynamic_index_in_dim(sent, chip, 0, keepdims=False)
        return here + there.astype(jnp.float32)

    own_sum = chip_sum(y_id)
    leaving = [chip_sum((y_id + k) % n_y).astype(jnp.bfloat16) for k in range(1, n_y)]
    leaving, key_value_pairs = lax.optimization_barrier((leaving, key_value_pairs))
    other_sums = jnp.stack([along_y(part, k + 1) for k, part in enumerate(leaving)])
    pages = exchanged_pages(key_value_pairs, page_table, tok_id, n_tok)
    other_sums, pages = lax.optimization_barrier((other_sums, pages))

    resid, moe_in = finish_attention(
        tokens, own_sum, other_sums, norm_gain_moe
    )
    far_moe_in = across(moe_in)
    own_packed = pack(moe_in, own_picks, 64 * MIB)

    def exchanged(packed):
        slots, held = packed.shape
        return in_half(packed.reshape(half, MAIN_SLOTS, held)).reshape(slots, held)

    def exchanged_beside(packed):
        return lax.cond(lengths[0] > 0, exchanged, jnp.zeros_like, packed)

    own_arrived = exchanged_beside(own_packed)
    far_moe_in, own_arrived = lax.optimization_barrier((far_moe_in, own_arrived))
    far_arrived = exchanged(pack(far_moe_in, far_picks, MIB))
    own_act = expert(own_arrived, w_in, w_down, extras, down=False)
    far_arrived, own_act = lax.optimization_barrier((far_arrived, own_act))
    far_made = expert(far_arrived, w_in, w_down, extras)
    far_made, own_act = lax.optimization_barrier((far_made, own_act))
    far_returned = exchanged(far_made)
    own_made = expert_down(own_act, w_down, *own_packed.shape, extras)
    far_returned, own_made = lax.optimization_barrier((far_returned, own_made))
    far_part, own_made = lax.optimization_barrier((combine(far_returned, far_weights), own_made))
    far_sum = across(far_part)
    own_returned = exchanged_beside(own_made)
    hidden_out = combine(own_returned, own_weights, resid, far_sum)
    kv_cache = landed_pages(pages, page_table, tok_id, n_tok, groups)
    return (hidden_out, kv_cache)


def solution(mesh):
    return jax.shard_map(
        per_device,
        mesh=mesh,
        in_specs=(
            P(("tok", "head"), None),
            P(),
            P(),
            P(None, "head"),
            P("head"),
            P("head", None),
            P(),
            P(("tok", "head"), None),
            P(("tok", "head"), None),
            P(("tok", "head"), None, None),
            P(("tok", "head"), None, None),
            P(),
        ),
        out_specs=(P(("tok", "head"), None), P("head", "tok", None, None)),
        check_vma=False,
    )
```

```python
import functools
import math

import jax
import jax.numpy as jnp
from jax import lax
from jax.experimental import pallas as pl
from jax.experimental.pallas import tpu as pltpu
from jax.sharding import PartitionSpec as P

MODEL_WIDTH = 2880
HEAD_SIZE = 64
EXPERTS = 32
ATTEND_WINDOW = 128
NSEQ = 4
PAGE_TOKENS = 16
QUERY_PER_KEY = 8


EPSILON = 1e-05
ROPE_BASE = 150000.0
GLU_ALPHA = 1.702

LANES = 128
MAIN_SLOTS = 8
PIECE = 768
PIECES = 4
EXTRA_AT = 2944
IN_TILE = 1920
FIRST_COPY = 1
DOWN_COPIES = 4
MIB = 1 << 20


def passed_along(array, axis, by):
    peers = lax.axis_size(axis)
    pairs = [(i, i + by) for i in range(peers) if 0 <= i + by < peers]
    return lax.ppermute(array, axis, pairs)


def segment_ends(lengths_ref):
    ends, end = [], 0
    for k in range(NSEQ):
        end = end + lengths_ref[k]
        ends.append(end)
    return ends


def segment_of(index, ends):
    segment = jnp.zeros_like(index)
    for end in ends:
        segment = segment + jnp.where(index >= end, 1, 0)
    return segment


def rope_tables(index, ends):
    start = jnp.zeros_like(index)
    for end in ends:
        start = jnp.where(index >= end, end, start)
    half = HEAD_SIZE // 2
    lane = lax.broadcasted_iota(jnp.int32, index.shape, 1)
    inv_freq = jnp.exp(
        (lane % half).astype(jnp.float32) * (-2.0 * math.log(ROPE_BASE) / HEAD_SIZE)
    )
    angles = (index - start).astype(jnp.float32) * inv_freq
    low = lane % HEAD_SIZE < half
    sin = jnp.sin(angles)
    return jnp.cos(angles), jnp.where(low, -sin, sin), low, lane


def qkv_kernel(step, chips, ids_ref, lengths_ref, own_ref, other_ref, gain_ref, w_ref, *refs):
    q_ref, kv_ref, xn_ref, cos_ref, sin_ref = refs[-5:]
    rows = own_ref.shape[0]
    core, chip, shard = ids_ref[0], (ids_ref[1] + chips - step) % chips, ids_ref[2]

    @pl.when(pl.program_id(0) == 0)
    def _():
        for at, ref in ((core, own_ref), (1 - core, other_ref)):
            wide = ref[...].astype(jnp.float32)
            inv_rms = lax.rsqrt(jnp.mean(wide * wide, axis=-1, keepdims=True) + EPSILON)
            normed = (wide * inv_rms * gain_ref[...][None]).astype(jnp.bfloat16)
            xn_ref[pl.ds(pl.multiple_of(at * rows, 16), rows), :] = normed
        first = (shard * chips + chip) * 2 * rows
        index = first + lax.broadcasted_iota(jnp.int32, cos_ref.shape, 0)
        cos, sin, _, _ = rope_tables(index, segment_ends(lengths_ref))
        cos_ref[...] = cos
        sin_ref[...] = sin

    projected = jnp.dot(xn_ref[...], w_ref[...], preferred_element_type=jnp.float32)
    cos, sin = cos_ref[...], sin_ref[...]
    lane = lax.broadcasted_iota(jnp.int32, cos.shape, 1)
    low = lane % HEAD_SIZE < HEAD_SIZE // 2

    def turned(u):
        return jnp.where(low, pltpu.roll(u, LANES - 32, 1), pltpu.roll(u, 32, 1))

    for b in range(QUERY_PER_KEY // 2):
        u = projected[:, b * LANES : (b + 1) * LANES]
        q_ref[:, b * LANES : (b + 1) * LANES] = (
            (u * cos + turned(u) * sin) * HEAD_SIZE ** (-0.5)
        ).astype(jnp.bfloat16)
    u = projected[:, QUERY_PER_KEY * HEAD_SIZE :]
    rotated = u * cos + turned(u) * sin
    kv_ref[...] = jnp.where(lane < HEAD_SIZE, rotated, u).astype(jnp.bfloat16)


def project(ids, lengths, step, chips, own, other, gain, weight, earlier):
    rows, width = own.shape
    columns = weight.shape[1]
    group = (QUERY_PER_KEY + 2) * HEAD_SIZE
    qs, kvs = QUERY_PER_KEY * HEAD_SIZE, 2 * HEAD_SIZE
    groups = columns // group
    whole = lambda g, ids: (0, 0)
    by_group = lambda g, ids: ((ids[1] + chips - step) % chips, g)
    return pl.pallas_call(
        functools.partial(qkv_kernel, step, chips),
        grid_spec=pltpu.PrefetchScalarGridSpec(
            num_scalar_prefetch=1,
            grid=(groups,),
            in_specs=[
                pl.BlockSpec(memory_space=pltpu.SMEM),
                pl.BlockSpec((rows, width), whole),
                pl.BlockSpec((rows, width), whole),
                pl.BlockSpec((width,), lambda g, ids: (0,)),
                pl.BlockSpec((width, group), lambda g, ids: (0, g)),
            ]
            + [pl.BlockSpec(memory_space=pl.ANY)] * len(earlier),
            out_specs=[
                pl.BlockSpec((2 * rows, qs), by_group),
                pl.BlockSpec((2 * rows, kvs), by_group),
            ],
            scratch_shapes=[
                pltpu.VMEM((2 * rows, width), jnp.bfloat16),
                pltpu.VMEM((2 * rows, LANES), jnp.float32),
                pltpu.VMEM((2 * rows, LANES), jnp.float32),
            ],
        ),
        out_shape=[
            jax.ShapeDtypeStruct((2 * rows * chips, groups * qs), jnp.bfloat16),
            jax.ShapeDtypeStruct((2 * rows * chips, groups * kvs), jnp.bfloat16),
        ],
        input_output_aliases={6: 0, 7: 1} if earlier else {},
        compiler_params=pltpu.CompilerParams(vmem_limit_bytes=60 * MIB),
        cost_estimate=pl.CostEstimate(
            flops=4 * rows * width * columns, bytes_accessed=2 * width * columns, transcendentals=0
        ),
        name="project",
    )(ids, lengths, own, other, gain, weight, *earlier)


def pack_rows(values_ref, pick_ref, packed_ref):
    packed_ref[:, :EXTRA_AT] = jnp.dot(
        pick_ref[0], values_ref[:, :EXTRA_AT], preferred_element_type=jnp.float32
    ).astype(jnp.bfloat16)
    pieces = jnp.zeros((packed_ref.shape[0], packed_ref.shape[1] - EXTRA_AT), jnp.float32)
    for p in range(pick_ref.shape[0] - 1):
        pieces = pieces + jnp.dot(
            pick_ref[1 + p],
            values_ref[:, p * PIECE : (p + 1) * PIECE],
            preferred_element_type=jnp.float32,
        )
    packed_ref[:, EXTRA_AT:] = pieces.astype(jnp.bfloat16)


def resid_kernel(tokens_ref, own_ref, others_ref, gain_ref, resid_ref, moe_ref):
    resid = tokens_ref[...].astype(jnp.float32) + own_ref[...].astype(jnp.float32)
    for k in range(others_ref.shape[0]):
        resid = resid + others_ref[k].astype(jnp.float32)
    resid_ref[...] = resid
    inv_rms = lax.rsqrt(jnp.mean(resid * resid, axis=-1, keepdims=True) + EPSILON)
    moe_ref[...] = (resid * inv_rms * gain_ref[...][None]).astype(jnp.bfloat16)


def pack_kernel(moe_ref, pick_ref, packed_ref, values_ref):
    width = moe_ref.shape[1]
    values_ref[:, width:] = jnp.zeros_like(values_ref[:, width:])
    values_ref[:, :width] = moe_ref[...]
    pack_rows(values_ref, pick_ref, packed_ref)


def packed_width(extras):
    return EXTRA_AT + PIECE if extras else PIECES * PIECE


def finish_attention(tokens, own, others, gain):
    rows, width = tokens.shape
    return pl.pallas_call(
        resid_kernel,
        out_shape=[
            jax.ShapeDtypeStruct((rows, width), jnp.float32),
            jax.ShapeDtypeStruct((rows, width), jnp.bfloat16),
        ],
        compiler_params=pltpu.CompilerParams(vmem_limit_bytes=32 * MIB),
        name="finish_attention",
    )(tokens, own, others, gain)


def pack(moe_in, picks, beside):
    rows, width = moe_in.shape
    kinds, slots, _ = picks.shape
    return pl.pallas_call(
        pack_kernel,
        out_shape=jax.ShapeDtypeStruct((slots, packed_width(kinds > 1)), jnp.bfloat16),
        scratch_shapes=[pltpu.VMEM((rows, PIECES * PIECE), jnp.bfloat16)],
        compiler_params=pltpu.CompilerParams(vmem_limit_bytes=32 * MIB),
        cost_estimate=pl.CostEstimate(
            flops=2 * slots * rows * 2 * width, bytes_accessed=beside, transcendentals=0
        ),
        name="pack",
    )(moe_in, picks)


def piece_of(count, slots, piece):
    t = lax.broadcasted_iota(jnp.int32, (count, slots), 0)
    r = lax.broadcasted_iota(jnp.int32, (count, slots), 1)
    return jnp.where(r == PIECES * t + piece, 1.0, 0.0).astype(jnp.bfloat16)


def fill_rows(packed_ref, x_ref, extras):
    slots, width = packed_ref.shape[0], x_ref.shape[1]
    x_ref[:slots, :] = packed_ref[:, :width]
    if extras:
        further = slots // PIECES
        for p in range(PIECES):
            extent = min(PIECE, width - p * PIECE)
            x_ref[slots:, p * PIECE : p * PIECE + extent] = jnp.dot(
                piece_of(further, slots, p),
                packed_ref[:, EXTRA_AT : EXTRA_AT + extent],
                preferred_element_type=jnp.float32,
            ).astype(jnp.bfloat16)


def activate(gate_up_ref, act_ref):
    rows, ffs = act_ref.shape
    base = ffs // LANES * LANES
    chunk = 32
    for r in range(0, rows, chunk):
        gate = gate_up_ref[r : r + chunk, :ffs]
        up = gate_up_ref[r : r + chunk, base:]
        if ffs > base:
            up = pltpu.roll(up, up.shape[1] - (ffs - base), 1)
        up = up[:, :ffs]
        act_ref[r : r + chunk, :] = (
            (up + 1.0) * gate * jax.nn.sigmoid(GLU_ALPHA * gate)
        ).astype(jnp.bfloat16)


def put_piece(piece, made, out_ref, width, piece_ref):
    slots = out_ref.shape[0]
    extent = made.shape[1]
    if extent < PIECE:
        out_ref[:, piece * PIECE + extent : (piece + 1) * PIECE] = jnp.zeros(
            (slots, PIECE - extent), jnp.bfloat16
        )
        out_ref[:, piece * PIECE : piece * PIECE + extent] = made[:slots]
    else:
        start = piece * PIECE
        start = start if isinstance(piece, int) else pl.multiple_of(start, LANES)
        out_ref[:, pl.ds(start, extent)] = made[:slots]
    if piece_ref is not None:
        further = slots // PIECES
        t = lax.broadcasted_iota(jnp.int32, (slots, further), 1)
        r = lax.broadcasted_iota(jnp.int32, (slots, further), 0)
        spread = jnp.where(r == PIECES * t + piece, 1.0, 0.0).astype(jnp.bfloat16)
        part = jnp.dot(spread, made[slots:], preferred_element_type=jnp.float32).astype(
            jnp.bfloat16
        )
        if isinstance(piece, int):
            if piece == 0:
                piece_ref[...] = part
            else:
                piece_ref[:, :extent] = piece_ref[:, :extent] + part
            if piece == PIECES - 1:
                out_ref[:, EXTRA_AT:] = piece_ref[...]
            return

        @pl.when(piece == 0)
        def _():
            piece_ref[...] = part

        @pl.when(piece > 0)
        def _():
            piece_ref[...] = piece_ref[...] + part

        @pl.when(piece == PIECES - 1)
        def _():
            out_ref[:, EXTRA_AT:] = piece_ref[...]


def expert_kernel(extras, in_tiles, down, *refs):
    packed_ref, w_in_ref = refs[:2]
    scratch = refs[4:] if down else refs[3:]
    x_ref, gate_up_ref = scratch[:2]
    act_ref = scratch[2] if down else refs[2]
    step = pl.program_id(0)
    copies = []
    if down:
        w_down_ref, out_ref = refs[2:4]
        held_ref, total_ref, sems = scratch[3:6]
        piece_ref = scratch[6] if extras else None
        ffs = held_ref.shape[0]
        rows = pl.cdiv(ffs, DOWN_COPIES * LANES) * LANES
        for c in range(pl.cdiv(ffs, rows)):
            part = pl.ds(c * rows, min(rows, ffs - c * rows))
            copies.append(
                pltpu.make_async_copy(w_down_ref.at[0, part], held_ref.at[part], sems.at[c])
            )

    @pl.when(step == 0)
    def _():
        fill_rows(packed_ref, x_ref, extras)

    for c, copy in enumerate(copies):
        pl.when(step == min(c + FIRST_COPY, in_tiles - 1))(copy.start)

    tile = w_in_ref.shape[2]
    made = jnp.dot(x_ref[...], w_in_ref[0], preferred_element_type=jnp.float32)
    if in_tiles == 1:
        gate_up_ref[...] = made
    else:
        gate_up_ref[:, pl.ds(pl.multiple_of(step * tile, LANES), tile)] = made

    @pl.when(step == in_tiles - 1)
    def _():
        activate(gate_up_ref, act_ref)
        if down:
            width = x_ref.shape[1]
            for c, copy in enumerate(copies):
                copy.wait()
                part = slice(c * rows, min((c + 1) * rows, ffs))
                term = jnp.dot(
                    act_ref[:, part], held_ref[part, :], preferred_element_type=jnp.float32
                )
                total_ref[...] = term if c == 0 else total_ref[...] + term
            for piece in range(PIECES):
                extent = min(PIECE, width - piece * PIECE)
                made = total_ref[:, piece * PIECE : piece * PIECE + extent].astype(jnp.bfloat16)
                put_piece(piece, made, out_ref, width, piece_ref)


def down_kernel(extras, width, act_ref, w_down_ref, out_ref, *scratch):
    piece = pl.program_id(0)
    made = jnp.dot(act_ref[...], w_down_ref[0], preferred_element_type=jnp.float32)
    column = lax.broadcasted_iota(jnp.int32, made.shape, 1) + piece * PIECE
    made = jnp.where(column < width, made, 0.0).astype(jnp.bfloat16)
    put_piece(piece, made, out_ref, width, scratch[0] if extras else None)


def expert(packed, w_in, w_down, extras, down=True):
    slots, held = packed.shape
    width = w_in.shape[1]
    ffs = w_down.shape[1]
    rows = slots + (slots // PIECES if extras else 0)
    tile = min(IN_TILE, 2 * ffs)
    in_tiles = pl.cdiv(2 * ffs, tile)
    whole = lambda i: (0, 0)
    in_specs = [
        pl.BlockSpec((slots, held), whole),
        pl.BlockSpec((1, width, tile), lambda i: (0, 0, i)),
    ]
    scratch = [
        pltpu.VMEM((rows, width), jnp.bfloat16),
        pltpu.VMEM((rows, in_tiles * tile), jnp.float32),
    ]
    args = (packed, w_in)
    out = (rows, ffs)
    if down:
        in_specs += [pl.BlockSpec(memory_space=pl.ANY)]
        scratch += [
            pltpu.VMEM((rows, ffs), jnp.bfloat16),
            pltpu.VMEM((ffs, width), jnp.bfloat16),
            pltpu.VMEM((rows, width), jnp.float32),
            pltpu.SemaphoreType.DMA((DOWN_COPIES,)),
        ]
        scratch += [pltpu.VMEM((slots, PIECE), jnp.bfloat16)] if extras else []
        args += (w_down,)
        out = (slots, held)
    parts = 6 if down else 4
    return pl.pallas_call(
        functools.partial(expert_kernel, extras, in_tiles, down),
        grid=(in_tiles,),
        in_specs=in_specs,
        out_specs=pl.BlockSpec(out, whole),
        out_shape=jax.ShapeDtypeStruct(out, jnp.bfloat16),
        scratch_shapes=scratch,
        compiler_params=pltpu.CompilerParams(vmem_limit_bytes=56 * MIB),
        cost_estimate=pl.CostEstimate(
            flops=parts * rows * width * ffs,
            bytes_accessed=parts * width * ffs,
            transcendentals=rows * ffs,
        ),
        name="expert" if down else "expert_up",
    )(*args)


def expert_down(act, w_down, slots, held, extras):
    rows, ffs = act.shape
    width = w_down.shape[2]
    whole = lambda i: (0, 0)
    return pl.pallas_call(
        functools.partial(down_kernel, extras, width),
        grid=(PIECES,),
        in_specs=[
            pl.BlockSpec((rows, ffs), whole),
            pl.BlockSpec((1, ffs, PIECE), lambda i: (0, 0, i)),
        ],
        out_specs=pl.BlockSpec((slots, held), whole),
        out_shape=jax.ShapeDtypeStruct((slots, held), jnp.bfloat16),
        scratch_shapes=[pltpu.VMEM((slots, PIECE), jnp.bfloat16)] if extras else [],
        compiler_params=pltpu.CompilerParams(vmem_limit_bytes=56 * MIB),
        cost_estimate=pl.CostEstimate(
            flops=2 * rows * width * ffs, bytes_accessed=2 * width * ffs, transcendentals=0
        ),
        name="expert_down",
    )(act, w_down)


def weighted_sum(made_ref, weight_ref, total_ref):
    width = total_ref.shape[1]
    for term in range(2):
        made = jnp.dot(
            weight_ref[term, 0], made_ref[:, :width], preferred_element_type=jnp.float32
        )
        total_ref[...] = made if term == 0 else total_ref[...] + made
        for p in range(weight_ref.shape[1] - 1):
            extent = min(PIECE, width - p * PIECE)
            at = slice(p * PIECE, p * PIECE + extent)
            total_ref[:, at] = total_ref[:, at] + jnp.dot(
                weight_ref[term, 1 + p],
                made_ref[:, EXTRA_AT : EXTRA_AT + extent],
                preferred_element_type=jnp.float32,
            )


def partial_kernel(made_ref, weight_ref, out_ref, total_ref):
    weighted_sum(made_ref, weight_ref, total_ref)
    out_ref[...] = total_ref[...].astype(jnp.bfloat16)


def total_kernel(made_ref, weight_ref, resid_ref, far_ref, out_ref, total_ref):
    weighted_sum(made_ref, weight_ref, total_ref)
    out_ref[...] = (
        resid_ref[...] + (total_ref[...] + far_ref[...].astype(jnp.float32))
    ).astype(jnp.bfloat16)


def combine(made, weights, resid=None, far=None):
    rows = weights.shape[2]
    kernel, more = (partial_kernel, ()) if resid is None else (total_kernel, (resid, far))
    return pl.pallas_call(
        kernel,
        out_shape=jax.ShapeDtypeStruct((rows, MODEL_WIDTH), jnp.bfloat16),
        scratch_shapes=[pltpu.VMEM((rows, MODEL_WIDTH), jnp.float32)],
        compiler_params=pltpu.CompilerParams(vmem_limit_bytes=32 * MIB),
        name="combine",
    )(made, weights, *more)


def slots_kernel(extras, far, half, experts, shards, topk, ids_ref, lengths_ref, choice_ref, *out_refs):
    pick_ref, weight_ref = out_refs
    device = ids_ref[3]
    first_expert = device // half * experts
    _, slots, rows = pick_ref.shape
    source = (device + half) % (2 * half) if far else device
    r = lax.broadcasted_iota(jnp.int32, (slots, rows), 0)
    index = source * rows + lax.broadcasted_iota(jnp.int32, (slots, rows), 1)
    slot = r % MAIN_SLOTS
    own_expert = (first_expert + r // (MAIN_SLOTS * shards)).astype(jnp.float32)
    named = jnp.zeros((slots, rows), jnp.float32)
    gate = jnp.zeros((slots, rows), jnp.float32)
    for k in range(topk):
        here = choice_ref[k : k + 1, :] == own_expert
        named = jnp.where(here, 1.0, named)
        gate = gate + jnp.where(here, choice_ref[topk + k : topk + k + 1, :], 0.0)
    named = jnp.where(index < segment_ends(lengths_ref)[-1], named, 0.0)
    i = lax.broadcasted_iota(jnp.int32, (rows, rows), 0)
    j = lax.broadcasted_iota(jnp.int32, (rows, rows), 1)
    earlier = jnp.where(i < j, 1.0, 0.0).astype(jnp.bfloat16)
    same = jnp.where(i == j, 1.0, 0.0).astype(jnp.bfloat16)
    rank = jnp.dot(named.astype(jnp.bfloat16), earlier, preferred_element_type=jnp.float32)
    rank = jnp.where(named > 0.0, rank, -1.0).astype(jnp.int32)
    high = gate.astype(jnp.bfloat16).astype(jnp.float32)

    def put(hit, pick_at, high_at, low_at):
        pick_at[...] = jnp.where(hit, 1.0, 0.0).astype(jnp.bfloat16)
        for values, at in ((high, high_at), (gate - high, low_at)):
            kept = jnp.where(hit, values, 0.0).astype(jnp.bfloat16)
            at[...] = lax.dot_general(
                same, kept, (((1,), (1,)), ((), ())), preferred_element_type=jnp.float32
            ).astype(jnp.bfloat16)

    put(rank == slot, pick_ref.at[0], weight_ref.at[0, 0], weight_ref.at[1, 0])
    if extras:
        for p in range(PIECES):
            hit = jnp.where(slot % PIECES == p, rank, -2) == MAIN_SLOTS + slot // PIECES
            put(hit, pick_ref.at[1 + p], weight_ref.at[0, 1 + p], weight_ref.at[1, 1 + p])


def slot_tables(ids, lengths, choice, far, half, experts, shards, extras):
    topk, rows = choice.shape[0] // 2, choice.shape[1]
    slots = experts * shards * MAIN_SLOTS
    kinds = 1 + PIECES if extras else 1
    shapes = [(kinds, slots, rows), (2, kinds, rows, slots)]
    smem = pl.BlockSpec(memory_space=pltpu.SMEM)
    return pl.pallas_call(
        functools.partial(slots_kernel, extras, far, half, experts, shards, topk),
        in_specs=[smem, smem, pl.BlockSpec(memory_space=pltpu.VMEM)],
        out_shape=[jax.ShapeDtypeStruct(shape, jnp.bfloat16) for shape in shapes],
        compiler_params=pltpu.CompilerParams(vmem_limit_bytes=32 * MIB),
        name="slots",
    )(ids, lengths, choice)


def attend_kernel(row_count, chips, ids_ref, lengths_ref, q_ref, rim_ref, pair_ref, sink_ref, w_ref, kept_ref, sent_ref, attended_ref):
    def attend_block(block):
        window = rim_ref.shape[0]
        rows = slice(block * window, (block + 1) * window)
        groups = pair_ref.shape[1] // LANES
        core = ids_ref[0]
        ends = segment_ends(lengths_ref)
        first = ids_ref[2] * (chips * 2 * row_count) + block * window
        query = first + lax.broadcasted_iota(jnp.int32, (window, 2 * window), 0)
        key = first - window + lax.broadcasted_iota(jnp.int32, (window, 2 * window), 1)
        query_segment = segment_of(query, ends)
        seen = (query_segment == segment_of(key, ends)) & (query_segment < NSEQ)
        seen = seen & (key >= 0) & (query >= key) & (query - key < window)
        lane = lax.broadcasted_iota(jnp.int32, (2 * window, LANES), 1)
        twos = QUERY_PER_KEY // 2
        for g in range(groups):
            at = slice(g * LANES, (g + 1) * LANES)
            before = pair_ref[(block - 1) * window : block * window, at] if block else rim_ref[:, at]
            pairs = jnp.concatenate([before, pair_ref[rows, at]], axis=0).astype(jnp.float32)
            keys = jnp.where(lane < HEAD_SIZE, pairs, 0.0)
            values = jnp.where(lane < HEAD_SIZE, 0.0, pairs)
            keys = [x.astype(jnp.bfloat16) for x in (keys, pltpu.roll(keys, HEAD_SIZE, 1))]
            values = [x.astype(jnp.bfloat16) for x in (pltpu.roll(values, HEAD_SIZE, 1), values)]
            start = g * twos * LANES
            queries = jnp.concatenate(
                [q_ref[rows, start + two * LANES : start + (two + 1) * LANES] for two in range(twos)],
                axis=0,
            )
            made = jnp.zeros((twos * window, LANES), jnp.float32)
            for side in range(2):
                scores = lax.dot_general(
                    queries, keys[side], (((1,), (1,)), ((), ())), preferred_element_type=jnp.float32
                )
                probs = []
                for two in range(twos):
                    sink = sink_ref[g * QUERY_PER_KEY + 2 * two + side]
                    weights = jnp.where(
                        seen, jnp.exp(scores[two * window : (two + 1) * window]), 0.0
                    )
                    totals = jnp.sum(weights, axis=-1, keepdims=True)
                    totals = totals + jnp.exp(jnp.full_like(totals, sink))
                    probs.append((weights * (1.0 / totals)).astype(jnp.bfloat16))
                made = made + jnp.dot(
                    jnp.concatenate(probs, axis=0), values[side], preferred_element_type=jnp.float32
                )
            made = made.astype(jnp.bfloat16)
            for two in range(twos):
                columns = slice(start + two * LANES, start + (two + 1) * LANES)
                for part in range(window // row_count):
                    head = block * (window // row_count) + part
                    place = (head % 2 + core) % 2 * chips + head // 2
                    row = two * window + part * row_count
                    attended_ref[
                        pl.ds(pl.multiple_of(place * row_count, 16), row_count), columns
                    ] = made[row : row + row_count]

    @pl.when(pl.program_id(0) == 0)
    def _():
        window = rim_ref.shape[0]
        for block in range(q_ref.shape[0] // window):
            attend_block(block)

    product = lax.dot_general(
        attended_ref[...],
        w_ref[...],
        (((1,), (1,)), ((), ())),
        preferred_element_type=jnp.float32,
    )
    for chip in range(chips):
        at, then = chip * row_count, (chips + chip) * row_count
        kept_ref[chip] = product[at : at + row_count]
        sent_ref[chip] = product[then : then + row_count].astype(jnp.bfloat16)


def attend(ids, lengths, queries, rim, pairs, sinks, w_out, row_count):
    total, columns = queries.shape
    width = w_out.shape[0]
    chips = total // (2 * row_count)
    tile = 2 * PIECE
    whole = lambda i, ids: (0, 0)
    smem = pl.BlockSpec(memory_space=pltpu.SMEM)
    return pl.pallas_call(
        functools.partial(attend_kernel, row_count, chips),
        grid_spec=pltpu.PrefetchScalarGridSpec(
            num_scalar_prefetch=1,
            grid=(pl.cdiv(width, tile),),
            in_specs=[
                smem,
                pl.BlockSpec(queries.shape, whole),
                pl.BlockSpec(rim.shape, whole),
                pl.BlockSpec(pairs.shape, whole),
                smem,
                pl.BlockSpec((tile, columns), lambda i, ids: (i, 0)),
            ],
            out_specs=[pl.BlockSpec((chips, row_count, tile), lambda i, ids: (0, 0, i))] * 2,
            scratch_shapes=[pltpu.VMEM(queries.shape, jnp.bfloat16)],
        ),
        out_shape=[
            jax.ShapeDtypeStruct((chips, row_count, width), jnp.float32),
            jax.ShapeDtypeStruct((chips, row_count, width), jnp.bfloat16),
        ],
        compiler_params=pltpu.CompilerParams(vmem_limit_bytes=60 * MIB),
        cost_estimate=pl.CostEstimate(
            flops=2 * total * columns * width, bytes_accessed=2 * columns * width, transcendentals=0
        ),
        name="attend",
    )(ids, lengths, queries, rim, pairs, sinks, w_out)


def page_order(page_table, n_tok, pages_dev):
    page_grid = page_table.reshape(n_tok, pages_dev)
    target = page_grid // pages_dev
    page_ids = jnp.arange(pages_dev, dtype=jnp.int32)
    earlier = page_ids[:, None] > page_ids[None, :]
    same_dest = target[:, :, None] == target[:, None, :]
    order_rank = jnp.sum((same_dest & earlier[None]).astype(jnp.int32), axis=2)
    return (target, order_rank, page_grid % pages_dev)


def exchanged_pages(pairs, page_table, tok_id, n_tok):
    rows = pairs.shape[0]
    groups = pairs.shape[1] // (2 * HEAD_SIZE)
    pages_dev = rows // PAGE_TOKENS
    share_count = pages_dev // n_tok
    paged = pairs.reshape(pages_dev, PAGE_TOKENS, groups, 2 * HEAD_SIZE).transpose(0, 2, 1, 3)
    target, order_rank, _ = page_order(page_table, n_tok, pages_dev)
    dest_ids = jnp.arange(n_tok, dtype=jnp.int32)
    share_ids = jnp.arange(share_count, dtype=jnp.int32)
    page_ids = jnp.arange(pages_dev, dtype=jnp.int32)
    matched = (target[tok_id][:, None, None] == dest_ids[None, :, None]) & (
        order_rank[tok_id][:, None, None] == share_ids[None, None, :]
    )
    pick_page = jnp.sum(jnp.where(matched, page_ids[:, None, None], 0), axis=0).reshape(-1)
    sent = paged[pick_page].reshape(n_tok, share_count * groups * PAGE_TOKENS, 2 * HEAD_SIZE)
    return lax.all_to_all(sent, "tok", split_axis=0, concat_axis=0, tiled=True)


def landed_pages(arrived, page_table, tok_id, n_tok, groups):
    share_count = arrived.shape[1] // (groups * PAGE_TOKENS)
    pages_dev = n_tok * share_count
    arrived = arrived.reshape(pages_dev, groups, PAGE_TOKENS, 2 * HEAD_SIZE)
    target, order_rank, slot_grid = page_order(page_table, n_tok, pages_dev)
    share_ids = jnp.arange(share_count, dtype=jnp.int32)
    page_ids = jnp.arange(pages_dev, dtype=jnp.int32)
    to_here = (target == tok_id)[:, :, None] & (order_rank[:, :, None] == share_ids[None, None, :])
    landing = jnp.sum(jnp.where(to_here, slot_grid[:, :, None], 0), axis=1).reshape(-1)
    source = jnp.sum(
        jnp.where(landing[None, :] == page_ids[:, None], page_ids[None, :], 0), axis=1
    )
    return arrived[source].transpose(1, 0, 2, 3)


def per_device(
    tokens,
    lengths,
    norm_gain_attn,
    query_key_value_weight,
    sinks,
    w_out_attn,
    norm_gain_moe,
    routes,
    gates,
    w_in,
    w_down,
    page_table,
):
    n_tok = lax.axis_size("tok")
    n_head = lax.axis_size("head")
    tok_id = lax.axis_index("tok")
    head_id = lax.axis_index("head")
    row_count, width = tokens.shape
    tok_dev = row_count * n_head
    groups = sinks.shape[0] // QUERY_PER_KEY
    n_y = n_head // 2
    y_id, core = head_id // 2, head_id % 2

    def to_core(array):
        return lax.ppermute(array, "head", [(h, h ^ 1) for h in range(n_head)])

    def along_y(array, by):
        return lax.ppermute(
            array, "head", [(h, (h // 2 + by) % n_y * 2 + h % 2) for h in range(n_head)]
        )

    n_dev = n_tok * n_head
    half = n_dev // 2

    def across(array):
        return lax.ppermute(array, ("tok", "head"), [(d, d ^ half) for d in range(n_dev)])

    def in_half(array):
        return lax.all_to_all(
            array,
            ("tok", "head"),
            split_axis=0,
            concat_axis=0,
            tiled=True,
            axis_index_groups=[list(range(half)), list(range(half, n_dev))],
        )

    flat_id = tok_id * n_head + head_id
    ids = jnp.stack([core, y_id, tok_id, flat_id]).astype(jnp.int32)
    choice = jnp.concatenate([routes.T.astype(jnp.float32), gates.T], axis=0)

    capacity = row_count // 8 + 2
    shards = n_dev // EXPERTS
    extras = capacity > MAIN_SLOTS
    tables = functools.partial(slot_tables, ids, lengths)
    sizes = (half, EXPERTS // 2, shards, extras)
    placed, block = [], tokens
    for k in range(n_y):
        if k:
            block, placed, choice = lax.optimization_barrier((along_y(tokens, k), placed, choice))
        placed = project(
            ids,
            lengths,
            k,
            n_y,
            block,
            to_core(block),
            norm_gain_attn,
            query_key_value_weight,
            placed,
        )
    far_choice = across(choice)
    placed, choice, far_choice = lax.optimization_barrier((placed, choice, far_choice))
    query_rows, key_value_pairs = placed
    rim_rows = passed_along(key_value_pairs[tok_dev - ATTEND_WINDOW :], "tok", 1)
    slots = tables(choice, False, *sizes), tables(far_choice, True, *sizes)
    rim_rows, slots = lax.optimization_barrier((rim_rows, slots))
    (own_picks, own_weights), (far_picks, far_weights) = slots
    kept, sent = attend(
        ids, lengths, query_rows, rim_rows, key_value_pairs, sinks, w_out_attn.T, row_count
    )
    sent = to_core(sent)

    def chip_sum(chip):
        here = lax.dynamic_index_in_dim(kept, chip, 0, keepdims=False)
        there = lax.dynamic_index_in_dim(sent, chip, 0, keepdims=False)
        return here + there.astype(jnp.float32)

    own_sum = chip_sum(y_id)
    leaving = [chip_sum((y_id + k) % n_y).astype(jnp.bfloat16) for k in range(1, n_y)]
    leaving, key_value_pairs = lax.optimization_barrier((leaving, key_value_pairs))
    other_sums = jnp.stack([along_y(part, k + 1) for k, part in enumerate(leaving)])
    pages = exchanged_pages(key_value_pairs, page_table, tok_id, n_tok)
    other_sums, pages = lax.optimization_barrier((other_sums, pages))

    resid, moe_in = finish_attention(
        tokens, own_sum, other_sums, norm_gain_moe
    )
    far_moe_in = across(moe_in)
    own_packed = pack(moe_in, own_picks, 64 * MIB)

    def exchanged(packed):
        slots, held = packed.shape
        return in_half(packed.reshape(half, MAIN_SLOTS, held)).reshape(slots, held)

    def exchanged_beside(packed):
        return lax.cond(lengths[0] > 0, exchanged, jnp.zeros_like, packed)

    own_arrived = exchanged_beside(own_packed)
    far_moe_in, own_arrived = lax.optimization_barrier((far_moe_in, own_arrived))
    far_arrived = exchanged(pack(far_moe_in, far_picks, MIB))
    own_act = expert(own_arrived, w_in, w_down, extras, down=False)
    far_arrived, own_act = lax.optimization_barrier((far_arrived, own_act))
    far_made = expert(far_arrived, w_in, w_down, extras)
    far_made, own_act = lax.optimization_barrier((far_made, own_act))
    far_returned = exchanged(far_made)
    own_made = expert_down(own_act, w_down, *own_packed.shape, extras)
    far_returned, own_made = lax.optimization_barrier((far_returned, own_made))
    far_part, own_made = lax.optimization_barrier((combine(far_returned, far_weights), own_made))
    far_sum = across(far_part)
    own_returned = exchanged_beside(own_made)
    hidden_out = combine(own_returned, own_weights, resid, far_sum)
    kv_cache = landed_pages(pages, page_table, tok_id, n_tok, groups)
    return (hidden_out, kv_cache)


def solution(mesh):
    return jax.shard_map(
        per_device,
        mesh=mesh,
        in_specs=(
            P(("tok", "head"), None),
            P(),
            P(),
            P(None, "head"),
            P("head"),
            P("head", None),
            P(),
            P(("tok", "head"), None),
            P(("tok", "head"), None),
            P(("tok", "head"), None, None),
            P(("tok", "head"), None, None),
            P(),
        ),
        out_specs=(P(("tok", "head"), None), P("head", "tok", None, None)),
        check_vma=False,
    )
```

```python
import functools
import math

import jax
import jax.numpy as jnp
from jax import lax
from jax.experimental import pallas as pl
from jax.experimental.pallas import tpu as pltpu
from jax.sharding import PartitionSpec as P

MODEL_WIDTH = 2880
HEAD_SIZE = 64
EXPERTS = 32
ATTEND_WINDOW = 128
NSEQ = 4
PAGE_TOKENS = 16
QUERY_PER_KEY = 8


EPSILON = 1e-05
ROPE_BASE = 150000.0
GLU_ALPHA = 1.702

LANES = 128
MAIN_SLOTS = 8
PIECE = 768
PIECES = 4
EXTRA_AT = 2944
IN_TILE = 1920
FIRST_COPY = 1
DOWN_COPIES = 4
MIB = 1 << 20


def passed_along(array, axis, by):
    peers = lax.axis_size(axis)
    pairs = [(i, i + by) for i in range(peers) if 0 <= i + by < peers]
    return lax.ppermute(array, axis, pairs)


def segment_ends(lengths_ref):
    ends, end = [], 0
    for k in range(NSEQ):
        end = end + lengths_ref[k]
        ends.append(end)
    return ends


def segment_of(index, ends):
    segment = jnp.zeros_like(index)
    for end in ends:
        segment = segment + jnp.where(index >= end, 1, 0)
    return segment


def rope_tables(index, ends):
    start = jnp.zeros_like(index)
    for end in ends:
        start = jnp.where(index >= end, end, start)
    half = HEAD_SIZE // 2
    lane = lax.broadcasted_iota(jnp.int32, index.shape, 1)
    inv_freq = jnp.exp(
        (lane % half).astype(jnp.float32) * (-2.0 * math.log(ROPE_BASE) / HEAD_SIZE)
    )
    angles = (index - start).astype(jnp.float32) * inv_freq
    low = lane % HEAD_SIZE < half
    sin = jnp.sin(angles)
    return jnp.cos(angles), jnp.where(low, -sin, sin), low, lane


def qkv_kernel(step, chips, ids_ref, lengths_ref, own_ref, other_ref, gain_ref, w_ref, *refs):
    q_ref, kv_ref, xn_ref, cos_ref, sin_ref = refs[-5:]
    rows = own_ref.shape[0]
    core, chip, shard = ids_ref[0], (ids_ref[1] + chips - step) % chips, ids_ref[2]

    @pl.when(pl.program_id(0) == 0)
    def _():
        for at, ref in ((core, own_ref), (1 - core, other_ref)):
            wide = ref[...].astype(jnp.float32)
            inv_rms = lax.rsqrt(jnp.mean(wide * wide, axis=-1, keepdims=True) + EPSILON)
            normed = (wide * inv_rms * gain_ref[...][None]).astype(jnp.bfloat16)
            xn_ref[pl.ds(pl.multiple_of(at * rows, 16), rows), :] = normed
        first = (shard * chips + chip) * 2 * rows
        index = first + lax.broadcasted_iota(jnp.int32, cos_ref.shape, 0)
        cos, sin, _, _ = rope_tables(index, segment_ends(lengths_ref))
        cos_ref[...] = cos
        sin_ref[...] = sin

    projected = jnp.dot(xn_ref[...], w_ref[...], preferred_element_type=jnp.float32)
    cos, sin = cos_ref[...], sin_ref[...]
    lane = lax.broadcasted_iota(jnp.int32, cos.shape, 1)
    low = lane % HEAD_SIZE < HEAD_SIZE // 2

    def turned(u):
        return jnp.where(low, pltpu.roll(u, LANES - 32, 1), pltpu.roll(u, 32, 1))

    for b in range(QUERY_PER_KEY // 2):
        u = projected[:, b * LANES : (b + 1) * LANES]
        q_ref[:, b * LANES : (b + 1) * LANES] = (
            (u * cos + turned(u) * sin) * HEAD_SIZE ** (-0.5)
        ).astype(jnp.bfloat16)
    u = projected[:, QUERY_PER_KEY * HEAD_SIZE :]
    rotated = u * cos + turned(u) * sin
    kv_ref[...] = jnp.where(lane < HEAD_SIZE, rotated, u).astype(jnp.bfloat16)


def project(ids, lengths, step, chips, own, other, gain, weight, earlier):
    rows, width = own.shape
    columns = weight.shape[1]
    group = (QUERY_PER_KEY + 2) * HEAD_SIZE
    qs, kvs = QUERY_PER_KEY * HEAD_SIZE, 2 * HEAD_SIZE
    groups = columns // group
    whole = lambda g, ids: (0, 0)
    by_group = lambda g, ids: ((ids[1] + chips - step) % chips, g)
    return pl.pallas_call(
        functools.partial(qkv_kernel, step, chips),
        grid_spec=pltpu.PrefetchScalarGridSpec(
            num_scalar_prefetch=1,
            grid=(groups,),
            in_specs=[
                pl.BlockSpec(memory_space=pltpu.SMEM),
                pl.BlockSpec((rows, width), whole),
                pl.BlockSpec((rows, width), whole),
                pl.BlockSpec((width,), lambda g, ids: (0,)),
                pl.BlockSpec((width, group), lambda g, ids: (0, g)),
            ]
            + [pl.BlockSpec(memory_space=pl.ANY)] * len(earlier),
            out_specs=[
                pl.BlockSpec((2 * rows, qs), by_group),
                pl.BlockSpec((2 * rows, kvs), by_group),
            ],
            scratch_shapes=[
                pltpu.VMEM((2 * rows, width), jnp.bfloat16),
                pltpu.VMEM((2 * rows, LANES), jnp.float32),
                pltpu.VMEM((2 * rows, LANES), jnp.float32),
            ],
        ),
        out_shape=[
            jax.ShapeDtypeStruct((2 * rows * chips, groups * qs), jnp.bfloat16),
            jax.ShapeDtypeStruct((2 * rows * chips, groups * kvs), jnp.bfloat16),
        ],
        input_output_aliases={6: 0, 7: 1} if earlier else {},
        compiler_params=pltpu.CompilerParams(vmem_limit_bytes=60 * MIB),
        cost_estimate=pl.CostEstimate(
            flops=4 * rows * width * columns, bytes_accessed=2 * width * columns, transcendentals=0
        ),
        name="project",
    )(ids, lengths, own, other, gain, weight, *earlier)


def pack_rows(values_ref, pick_ref, packed_ref):
    packed_ref[:, :EXTRA_AT] = jnp.dot(
        pick_ref[0], values_ref[:, :EXTRA_AT], preferred_element_type=jnp.float32
    ).astype(jnp.bfloat16)
    pieces = jnp.zeros((packed_ref.shape[0], packed_ref.shape[1] - EXTRA_AT), jnp.float32)
    for p in range(pick_ref.shape[0] - 1):
        pieces = pieces + jnp.dot(
            pick_ref[1 + p],
            values_ref[:, p * PIECE : (p + 1) * PIECE],
            preferred_element_type=jnp.float32,
        )
    packed_ref[:, EXTRA_AT:] = pieces.astype(jnp.bfloat16)


def resid_kernel(tokens_ref, own_ref, others_ref, gain_ref, resid_ref, moe_ref):
    resid = tokens_ref[...].astype(jnp.float32) + own_ref[...].astype(jnp.float32)
    for k in range(others_ref.shape[0]):
        resid = resid + others_ref[k].astype(jnp.float32)
    resid_ref[...] = resid
    inv_rms = lax.rsqrt(jnp.mean(resid * resid, axis=-1, keepdims=True) + EPSILON)
    moe_ref[...] = (resid * inv_rms * gain_ref[...][None]).astype(jnp.bfloat16)


def pack_kernel(moe_ref, pick_ref, packed_ref, values_ref):
    width = moe_ref.shape[1]
    values_ref[:, width:] = jnp.zeros_like(values_ref[:, width:])
    values_ref[:, :width] = moe_ref[...]
    pack_rows(values_ref, pick_ref, packed_ref)


def packed_width(extras):
    return EXTRA_AT + PIECE if extras else PIECES * PIECE


def finish_attention(tokens, own, others, gain):
    rows, width = tokens.shape
    return pl.pallas_call(
        resid_kernel,
        out_shape=[
            jax.ShapeDtypeStruct((rows, width), jnp.float32),
            jax.ShapeDtypeStruct((rows, width), jnp.bfloat16),
        ],
        compiler_params=pltpu.CompilerParams(vmem_limit_bytes=32 * MIB),
        name="finish_attention",
    )(tokens, own, others, gain)


def pack(moe_in, picks, beside):
    rows, width = moe_in.shape
    kinds, slots, _ = picks.shape
    return pl.pallas_call(
        pack_kernel,
        out_shape=jax.ShapeDtypeStruct((slots, packed_width(kinds > 1)), jnp.bfloat16),
        scratch_shapes=[pltpu.VMEM((rows, PIECES * PIECE), jnp.bfloat16)],
        compiler_params=pltpu.CompilerParams(vmem_limit_bytes=32 * MIB),
        cost_estimate=pl.CostEstimate(
            flops=2 * slots * rows * 2 * width, bytes_accessed=beside, transcendentals=0
        ),
        name="pack",
    )(moe_in, picks)


def piece_of(count, slots, piece):
    t = lax.broadcasted_iota(jnp.int32, (count, slots), 0)
    r = lax.broadcasted_iota(jnp.int32, (count, slots), 1)
    return jnp.where(r == PIECES * t + piece, 1.0, 0.0).astype(jnp.bfloat16)


def fill_rows(packed_ref, x_ref, extras):
    slots, width = packed_ref.shape[0], x_ref.shape[1]
    x_ref[:slots, :] = packed_ref[:, :width]
    if extras:
        further = slots // PIECES
        for p in range(PIECES):
            extent = min(PIECE, width - p * PIECE)
            x_ref[slots:, p * PIECE : p * PIECE + extent] = jnp.dot(
                piece_of(further, slots, p),
                packed_ref[:, EXTRA_AT : EXTRA_AT + extent],
                preferred_element_type=jnp.float32,
            ).astype(jnp.bfloat16)


def activate(gate_up_ref, act_ref):
    rows, ffs = act_ref.shape
    base = ffs // LANES * LANES
    chunk = 32
    for r in range(0, rows, chunk):
        gate = gate_up_ref[r : r + chunk, :ffs]
        up = gate_up_ref[r : r + chunk, base:]
        if ffs > base:
            up = pltpu.roll(up, up.shape[1] - (ffs - base), 1)
        up = up[:, :ffs]
        act_ref[r : r + chunk, :] = (
            (up + 1.0) * gate * jax.nn.sigmoid(GLU_ALPHA * gate)
        ).astype(jnp.bfloat16)


def put_piece(piece, made, out_ref, width, piece_ref):
    slots = out_ref.shape[0]
    extent = made.shape[1]
    if extent < PIECE:
        out_ref[:, piece * PIECE + extent : (piece + 1) * PIECE] = jnp.zeros(
            (slots, PIECE - extent), jnp.bfloat16
        )
        out_ref[:, piece * PIECE : piece * PIECE + extent] = made[:slots]
    else:
        start = piece * PIECE
        start = start if isinstance(piece, int) else pl.multiple_of(start, LANES)
        out_ref[:, pl.ds(start, extent)] = made[:slots]
    if piece_ref is not None:
        further = slots // PIECES
        t = lax.broadcasted_iota(jnp.int32, (slots, further), 1)
        r = lax.broadcasted_iota(jnp.int32, (slots, further), 0)
        spread = jnp.where(r == PIECES * t + piece, 1.0, 0.0).astype(jnp.bfloat16)
        part = jnp.dot(spread, made[slots:], preferred_element_type=jnp.float32).astype(
            jnp.bfloat16
        )
        if isinstance(piece, int):
            if piece == 0:
                piece_ref[...] = part
            else:
                piece_ref[:, :extent] = piece_ref[:, :extent] + part
            if piece == PIECES - 1:
                out_ref[:, EXTRA_AT:] = piece_ref[...]
            return

        @pl.when(piece == 0)
        def _():
            piece_ref[...] = part

        @pl.when(piece > 0)
        def _():
            piece_ref[...] = piece_ref[...] + part

        @pl.when(piece == PIECES - 1)
        def _():
            out_ref[:, EXTRA_AT:] = piece_ref[...]


def expert_kernel(extras, in_tiles, down, *refs):
    packed_ref, w_in_ref = refs[:2]
    scratch = refs[4:] if down else refs[3:]
    x_ref, gate_up_ref = scratch[:2]
    act_ref = scratch[2] if down else refs[2]
    step = pl.program_id(0)
    copies = []
    if down:
        w_down_ref, out_ref = refs[2:4]
        held_ref, total_ref, sems = scratch[3:6]
        piece_ref = scratch[6] if extras else None
        ffs = held_ref.shape[0]
        rows = pl.cdiv(ffs, DOWN_COPIES * LANES) * LANES
        for c in range(pl.cdiv(ffs, rows)):
            part = pl.ds(c * rows, min(rows, ffs - c * rows))
            copies.append(
                pltpu.make_async_copy(w_down_ref.at[0, part], held_ref.at[part], sems.at[c])
            )

    @pl.when(step == 0)
    def _():
        fill_rows(packed_ref, x_ref, extras)

    for c, copy in enumerate(copies):
        pl.when(step == min(c + FIRST_COPY, in_tiles - 1))(copy.start)

    tile = w_in_ref.shape[2]
    made = jnp.dot(x_ref[...], w_in_ref[0], preferred_element_type=jnp.float32)
    if in_tiles == 1:
        gate_up_ref[...] = made
    else:
        gate_up_ref[:, pl.ds(pl.multiple_of(step * tile, LANES), tile)] = made

    @pl.when(step == in_tiles - 1)
    def _():
        activate(gate_up_ref, act_ref)
        if down:
            width = x_ref.shape[1]
            for c, copy in enumerate(copies):
                copy.wait()
                part = slice(c * rows, min((c + 1) * rows, ffs))
                term = jnp.dot(
                    act_ref[:, part], held_ref[part, :], preferred_element_type=jnp.float32
                )
                total_ref[...] = term if c == 0 else total_ref[...] + term
            for piece in range(PIECES):
                extent = min(PIECE, width - piece * PIECE)
                made = total_ref[:, piece * PIECE : piece * PIECE + extent].astype(jnp.bfloat16)
                put_piece(piece, made, out_ref, width, piece_ref)


def down_kernel(extras, width, act_ref, w_down_ref, out_ref, *scratch):
    piece = pl.program_id(0)
    made = jnp.dot(act_ref[...], w_down_ref[0], preferred_element_type=jnp.float32)
    column = lax.broadcasted_iota(jnp.int32, made.shape, 1) + piece * PIECE
    made = jnp.where(column < width, made, 0.0).astype(jnp.bfloat16)
    put_piece(piece, made, out_ref, width, scratch[0] if extras else None)


def expert(packed, w_in, w_down, extras, down=True):
    slots, held = packed.shape
    width = w_in.shape[1]
    ffs = w_down.shape[1]
    rows = slots + (slots // PIECES if extras else 0)
    tile = min(IN_TILE, 2 * ffs)
    in_tiles = pl.cdiv(2 * ffs, tile)
    whole = lambda i: (0, 0)
    in_specs = [
        pl.BlockSpec((slots, held), whole),
        pl.BlockSpec((1, width, tile), lambda i: (0, 0, i)),
    ]
    scratch = [
        pltpu.VMEM((rows, width), jnp.bfloat16),
        pltpu.VMEM((rows, in_tiles * tile), jnp.float32),
    ]
    args = (packed, w_in)
    out = (rows, ffs)
    if down:
        in_specs += [pl.BlockSpec(memory_space=pl.ANY)]
        scratch += [
            pltpu.VMEM((rows, ffs), jnp.bfloat16),
            pltpu.VMEM((ffs, width), jnp.bfloat16),
            pltpu.VMEM((rows, width), jnp.float32),
            pltpu.SemaphoreType.DMA((DOWN_COPIES,)),
        ]
        scratch += [pltpu.VMEM((slots, PIECE), jnp.bfloat16)] if extras else []
        args += (w_down,)
        out = (slots, held)
    parts = 6 if down else 4
    return pl.pallas_call(
        functools.partial(expert_kernel, extras, in_tiles, down),
        grid=(in_tiles,),
        in_specs=in_specs,
        out_specs=pl.BlockSpec(out, whole),
        out_shape=jax.ShapeDtypeStruct(out, jnp.bfloat16),
        scratch_shapes=scratch,
        compiler_params=pltpu.CompilerParams(vmem_limit_bytes=56 * MIB),
        cost_estimate=pl.CostEstimate(
            flops=parts * rows * width * ffs,
            bytes_accessed=parts * width * ffs,
            transcendentals=rows * ffs,
        ),
        name="expert" if down else "expert_up",
    )(*args)


def expert_down(act, w_down, slots, held, extras):
    rows, ffs = act.shape
    width = w_down.shape[2]
    whole = lambda i: (0, 0)
    return pl.pallas_call(
        functools.partial(down_kernel, extras, width),
        grid=(PIECES,),
        in_specs=[
            pl.BlockSpec((rows, ffs), whole),
            pl.BlockSpec((1, ffs, PIECE), lambda i: (0, 0, i)),
        ],
        out_specs=pl.BlockSpec((slots, held), whole),
        out_shape=jax.ShapeDtypeStruct((slots, held), jnp.bfloat16),
        scratch_shapes=[pltpu.VMEM((slots, PIECE), jnp.bfloat16)] if extras else [],
        compiler_params=pltpu.CompilerParams(vmem_limit_bytes=56 * MIB),
        cost_estimate=pl.CostEstimate(
            flops=2 * rows * width * ffs, bytes_accessed=2 * width * ffs, transcendentals=0
        ),
        name="expert_down",
    )(act, w_down)


def weighted_sum(made_ref, weight_ref, total_ref):
    width = total_ref.shape[1]
    for term in range(2):
        made = jnp.dot(
            weight_ref[term, 0], made_ref[:, :width], preferred_element_type=jnp.float32
        )
        total_ref[...] = made if term == 0 else total_ref[...] + made
        for p in range(weight_ref.shape[1] - 1):
            extent = min(PIECE, width - p * PIECE)
            at = slice(p * PIECE, p * PIECE + extent)
            total_ref[:, at] = total_ref[:, at] + jnp.dot(
                weight_ref[term, 1 + p],
                made_ref[:, EXTRA_AT : EXTRA_AT + extent],
                preferred_element_type=jnp.float32,
            )


def partial_kernel(made_ref, weight_ref, out_ref, total_ref):
    weighted_sum(made_ref, weight_ref, total_ref)
    out_ref[...] = total_ref[...].astype(jnp.bfloat16)


def total_kernel(made_ref, weight_ref, resid_ref, far_ref, out_ref, total_ref):
    weighted_sum(made_ref, weight_ref, total_ref)
    out_ref[...] = (
        resid_ref[...] + (total_ref[...] + far_ref[...].astype(jnp.float32))
    ).astype(jnp.bfloat16)


def combine(made, weights, resid=None, far=None):
    rows = weights.shape[2]
    kernel, more = (partial_kernel, ()) if resid is None else (total_kernel, (resid, far))
    return pl.pallas_call(
        kernel,
        out_shape=jax.ShapeDtypeStruct((rows, MODEL_WIDTH), jnp.bfloat16),
        scratch_shapes=[pltpu.VMEM((rows, MODEL_WIDTH), jnp.float32)],
        compiler_params=pltpu.CompilerParams(vmem_limit_bytes=32 * MIB),
        name="combine",
    )(made, weights, *more)


def slots_kernel(extras, far, half, experts, shards, topk, ids_ref, lengths_ref, choice_ref, *out_refs):
    pick_ref, weight_ref = out_refs
    device = ids_ref[3]
    first_expert = device // half * experts
    _, slots, rows = pick_ref.shape
    source = (device + half) % (2 * half) if far else device
    r = lax.broadcasted_iota(jnp.int32, (slots, rows), 0)
    index = source * rows + lax.broadcasted_iota(jnp.int32, (slots, rows), 1)
    slot = r % MAIN_SLOTS
    own_expert = (first_expert + r // (MAIN_SLOTS * shards)).astype(jnp.float32)
    named = jnp.zeros((slots, rows), jnp.float32)
    gate = jnp.zeros((slots, rows), jnp.float32)
    for k in range(topk):
        here = choice_ref[k : k + 1, :] == own_expert
        named = jnp.where(here, 1.0, named)
        gate = gate + jnp.where(here, choice_ref[topk + k : topk + k + 1, :], 0.0)
    named = jnp.where(index < segment_ends(lengths_ref)[-1], named, 0.0)
    i = lax.broadcasted_iota(jnp.int32, (rows, rows), 0)
    j = lax.broadcasted_iota(jnp.int32, (rows, rows), 1)
    earlier = jnp.where(i < j, 1.0, 0.0).astype(jnp.bfloat16)
    same = jnp.where(i == j, 1.0, 0.0).astype(jnp.bfloat16)
    rank = jnp.dot(named.astype(jnp.bfloat16), earlier, preferred_element_type=jnp.float32)
    rank = jnp.where(named > 0.0, rank, -1.0).astype(jnp.int32)
    high = gate.astype(jnp.bfloat16).astype(jnp.float32)

    def put(hit, pick_at, high_at, low_at):
        pick_at[...] = jnp.where(hit, 1.0, 0.0).astype(jnp.bfloat16)
        for values, at in ((high, high_at), (gate - high, low_at)):
            kept = jnp.where(hit, values, 0.0).astype(jnp.bfloat16)
            at[...] = lax.dot_general(
                same, kept, (((1,), (1,)), ((), ())), preferred_element_type=jnp.float32
            ).astype(jnp.bfloat16)

    put(rank == slot, pick_ref.at[0], weight_ref.at[0, 0], weight_ref.at[1, 0])
    if extras:
        for p in range(PIECES):
            hit = jnp.where(slot % PIECES == p, rank, -2) == MAIN_SLOTS + slot // PIECES
            put(hit, pick_ref.at[1 + p], weight_ref.at[0, 1 + p], weight_ref.at[1, 1 + p])


def slot_tables(ids, lengths, choice, far, half, experts, shards, extras):
    topk, rows = choice.shape[0] // 2, choice.shape[1]
    slots = experts * shards * MAIN_SLOTS
    kinds = 1 + PIECES if extras else 1
    shapes = [(kinds, slots, rows), (2, kinds, rows, slots)]
    smem = pl.BlockSpec(memory_space=pltpu.SMEM)
    return pl.pallas_call(
        functools.partial(slots_kernel, extras, far, half, experts, shards, topk),
        in_specs=[smem, smem, pl.BlockSpec(memory_space=pltpu.VMEM)],
        out_shape=[jax.ShapeDtypeStruct(shape, jnp.bfloat16) for shape in shapes],
        compiler_params=pltpu.CompilerParams(vmem_limit_bytes=32 * MIB),
        name="slots",
    )(ids, lengths, choice)


def attend_kernel(row_count, chips, ids_ref, lengths_ref, q_ref, rim_ref, pair_ref, sink_ref, w_ref, kept_ref, sent_ref, attended_ref):
    def attend_block(block):
        window = rim_ref.shape[0]
        rows = slice(block * window, (block + 1) * window)
        groups = pair_ref.shape[1] // LANES
        core = ids_ref[0]
        ends = segment_ends(lengths_ref)
        first = ids_ref[2] * (chips * 2 * row_count) + block * window
        query = first + lax.broadcasted_iota(jnp.int32, (window, 2 * window), 0)
        key = first - window + lax.broadcasted_iota(jnp.int32, (window, 2 * window), 1)
        query_segment = segment_of(query, ends)
        seen = (query_segment == segment_of(key, ends)) & (query_segment < NSEQ)
        seen = seen & (key >= 0) & (query >= key) & (query - key < window)
        lane = lax.broadcasted_iota(jnp.int32, (2 * window, LANES), 1)
        twos = QUERY_PER_KEY // 2
        for g in range(groups):
            at = slice(g * LANES, (g + 1) * LANES)
            before = pair_ref[(block - 1) * window : block * window, at] if block else rim_ref[:, at]
            pairs = jnp.concatenate([before, pair_ref[rows, at]], axis=0).astype(jnp.float32)
            keys = jnp.where(lane < HEAD_SIZE, pairs, 0.0)
            values = jnp.where(lane < HEAD_SIZE, 0.0, pairs)
            keys = [x.astype(jnp.bfloat16) for x in (keys, pltpu.roll(keys, HEAD_SIZE, 1))]
            values = [x.astype(jnp.bfloat16) for x in (pltpu.roll(values, HEAD_SIZE, 1), values)]
            start = g * twos * LANES
            queries = jnp.concatenate(
                [q_ref[rows, start + two * LANES : start + (two + 1) * LANES] for two in range(twos)],
                axis=0,
            )
            made = jnp.zeros((twos * window, LANES), jnp.float32)
            for side in range(2):
                scores = lax.dot_general(
                    queries, keys[side], (((1,), (1,)), ((), ())), preferred_element_type=jnp.float32
                )
                probs = []
                for two in range(twos):
                    sink = sink_ref[g * QUERY_PER_KEY + 2 * two + side]
                    weights = jnp.where(
                        seen, jnp.exp(scores[two * window : (two + 1) * window]), 0.0
                    )
                    totals = jnp.sum(weights, axis=-1, keepdims=True)
                    totals = totals + jnp.exp(jnp.full_like(totals, sink))
                    probs.append((weights * (1.0 / totals)).astype(jnp.bfloat16))
                made = made + jnp.dot(
                    jnp.concatenate(probs, axis=0), values[side], preferred_element_type=jnp.float32
                )
            made = made.astype(jnp.bfloat16)
            for two in range(twos):
                columns = slice(start + two * LANES, start + (two + 1) * LANES)
                for part in range(window // row_count):
                    head = block * (window // row_count) + part
                    place = (head % 2 + core) % 2 * chips + head // 2
                    row = two * window + part * row_count
                    attended_ref[
                        pl.ds(pl.multiple_of(place * row_count, 16), row_count), columns
                    ] = made[row : row + row_count]

    @pl.when(pl.program_id(0) == 0)
    def _():
        window = rim_ref.shape[0]
        for block in range(q_ref.shape[0] // window):
            attend_block(block)

    product = lax.dot_general(
        attended_ref[...],
        w_ref[...],
        (((1,), (1,)), ((), ())),
        preferred_element_type=jnp.float32,
    )
    for chip in range(chips):
        at, then = chip * row_count, (chips + chip) * row_count
        kept_ref[chip] = product[at : at + row_count]
        sent_ref[chip] = product[then : then + row_count].astype(jnp.bfloat16)


def attend(ids, lengths, queries, rim, pairs, sinks, w_out, row_count):
    total, columns = queries.shape
    width = w_out.shape[0]
    chips = total // (2 * row_count)
    tile = 2 * PIECE
    whole = lambda i, ids: (0, 0)
    smem = pl.BlockSpec(memory_space=pltpu.SMEM)
    return pl.pallas_call(
        functools.partial(attend_kernel, row_count, chips),
        grid_spec=pltpu.PrefetchScalarGridSpec(
            num_scalar_prefetch=1,
            grid=(pl.cdiv(width, tile),),
            in_specs=[
                smem,
                pl.BlockSpec(queries.shape, whole),
                pl.BlockSpec(rim.shape, whole),
                pl.BlockSpec(pairs.shape, whole),
                smem,
                pl.BlockSpec((tile, columns), lambda i, ids: (i, 0)),
            ],
            out_specs=[pl.BlockSpec((chips, row_count, tile), lambda i, ids: (0, 0, i))] * 2,
            scratch_shapes=[pltpu.VMEM(queries.shape, jnp.bfloat16)],
        ),
        out_shape=[
            jax.ShapeDtypeStruct((chips, row_count, width), jnp.float32),
            jax.ShapeDtypeStruct((chips, row_count, width), jnp.bfloat16),
        ],
        compiler_params=pltpu.CompilerParams(vmem_limit_bytes=60 * MIB),
        cost_estimate=pl.CostEstimate(
            flops=2 * total * columns * width, bytes_accessed=2 * columns * width, transcendentals=0
        ),
        name="attend",
    )(ids, lengths, queries, rim, pairs, sinks, w_out)


def page_order(page_table, n_tok, pages_dev):
    page_grid = page_table.reshape(n_tok, pages_dev)
    target = page_grid // pages_dev
    page_ids = jnp.arange(pages_dev, dtype=jnp.int32)
    earlier = page_ids[:, None] > page_ids[None, :]
    same_dest = target[:, :, None] == target[:, None, :]
    order_rank = jnp.sum((same_dest & earlier[None]).astype(jnp.int32), axis=2)
    return (target, order_rank, page_grid % pages_dev)


def leaving_pages(pairs, page_table, tok_id, n_tok):
    rows = pairs.shape[0]
    groups = pairs.shape[1] // (2 * HEAD_SIZE)
    pages_dev = rows // PAGE_TOKENS
    share_count = pages_dev // n_tok
    paged = pairs.reshape(pages_dev, PAGE_TOKENS, groups, 2 * HEAD_SIZE).transpose(0, 2, 1, 3)
    target, order_rank, _ = page_order(page_table, n_tok, pages_dev)
    dest_ids = jnp.arange(n_tok, dtype=jnp.int32)
    share_ids = jnp.arange(share_count, dtype=jnp.int32)
    page_ids = jnp.arange(pages_dev, dtype=jnp.int32)
    matched = (target[tok_id][:, None, None] == dest_ids[None, :, None]) & (
        order_rank[tok_id][:, None, None] == share_ids[None, None, :]
    )
    pick_page = jnp.sum(jnp.where(matched, page_ids[:, None, None], 0), axis=0).reshape(-1)
    return paged[pick_page].reshape(n_tok, share_count * groups * PAGE_TOKENS, 2 * HEAD_SIZE)


def landed_pages(arrived, page_table, tok_id, n_tok, groups):
    share_count = arrived.shape[1] // (groups * PAGE_TOKENS)
    pages_dev = n_tok * share_count
    arrived = arrived.reshape(pages_dev, groups, PAGE_TOKENS, 2 * HEAD_SIZE)
    target, order_rank, slot_grid = page_order(page_table, n_tok, pages_dev)
    share_ids = jnp.arange(share_count, dtype=jnp.int32)
    page_ids = jnp.arange(pages_dev, dtype=jnp.int32)
    to_here = (target == tok_id)[:, :, None] & (order_rank[:, :, None] == share_ids[None, None, :])
    landing = jnp.sum(jnp.where(to_here, slot_grid[:, :, None], 0), axis=1).reshape(-1)
    source = jnp.sum(
        jnp.where(landing[None, :] == page_ids[:, None], page_ids[None, :], 0), axis=1
    )
    return arrived[source].transpose(1, 0, 2, 3)


def per_device(
    tokens,
    lengths,
    norm_gain_attn,
    query_key_value_weight,
    sinks,
    w_out_attn,
    norm_gain_moe,
    routes,
    gates,
    w_in,
    w_down,
    page_table,
):
    n_tok = lax.axis_size("tok")
    n_head = lax.axis_size("head")
    tok_id = lax.axis_index("tok")
    head_id = lax.axis_index("head")
    row_count, width = tokens.shape
    tok_dev = row_count * n_head
    groups = sinks.shape[0] // QUERY_PER_KEY
    n_y = n_head // 2
    y_id, core = head_id // 2, head_id % 2

    def to_core(array):
        return lax.ppermute(array, "head", [(h, h ^ 1) for h in range(n_head)])

    def along_y(array, by):
        return lax.ppermute(
            array, "head", [(h, (h // 2 + by) % n_y * 2 + h % 2) for h in range(n_head)]
        )

    n_dev = n_tok * n_head
    half = n_dev // 2

    def across(array):
        return lax.ppermute(array, ("tok", "head"), [(d, d ^ half) for d in range(n_dev)])

    def in_half(array):
        return lax.all_to_all(
            array,
            ("tok", "head"),
            split_axis=0,
            concat_axis=0,
            tiled=True,
            axis_index_groups=[list(range(half)), list(range(half, n_dev))],
        )

    flat_id = tok_id * n_head + head_id
    ids = jnp.stack([core, y_id, tok_id, flat_id]).astype(jnp.int32)
    choice = jnp.concatenate([routes.T.astype(jnp.float32), gates.T], axis=0)

    capacity = row_count // 8 + 2
    shards = n_dev // EXPERTS
    extras = capacity > MAIN_SLOTS
    tables = functools.partial(slot_tables, ids, lengths)
    sizes = (half, EXPERTS // 2, shards, extras)
    placed, block = [], tokens
    for k in range(n_y):
        if k:
            block, placed, choice = lax.optimization_barrier((along_y(tokens, k), placed, choice))
        placed = project(
            ids,
            lengths,
            k,
            n_y,
            block,
            to_core(block),
            norm_gain_attn,
            query_key_value_weight,
            placed,
        )
    far_choice = across(choice)
    placed, choice, far_choice = lax.optimization_barrier((placed, choice, far_choice))
    query_rows, key_value_pairs = placed
    rim_rows = passed_along(key_value_pairs[tok_dev - ATTEND_WINDOW :], "tok", 1)
    slots = tables(choice, False, *sizes), tables(far_choice, True, *sizes)
    pages = leaving_pages(key_value_pairs, page_table, tok_id, n_tok)
    rim_rows, slots, pages = lax.optimization_barrier((rim_rows, slots, pages))
    (own_picks, own_weights), (far_picks, far_weights) = slots
    kept, sent = attend(
        ids, lengths, query_rows, rim_rows, key_value_pairs, sinks, w_out_attn.T, row_count
    )
    sent = to_core(sent)

    def chip_sum(kept, sent, chip):
        here = lax.dynamic_index_in_dim(kept, chip, 0, keepdims=False)
        there = lax.dynamic_index_in_dim(sent, chip, 0, keepdims=False)
        return here + there.astype(jnp.float32)

    leaving = [chip_sum(kept, sent, (y_id + k) % n_y).astype(jnp.bfloat16) for k in range(1, n_y)]
    leaving, pages, kept, sent = lax.optimization_barrier((leaving, pages, kept, sent))
    other_sums = jnp.stack([along_y(part, k + 1) for k, part in enumerate(leaving)])
    pages = lax.all_to_all(pages, "tok", split_axis=0, concat_axis=0, tiled=True)
    own_sum = chip_sum(kept, sent, y_id)
    other_sums, pages = lax.optimization_barrier((other_sums, pages))

    resid, moe_in = finish_attention(
        tokens, own_sum, other_sums, norm_gain_moe
    )
    far_moe_in = across(moe_in)
    own_packed = pack(moe_in, own_picks, 64 * MIB)

    def exchanged(packed):
        slots, held = packed.shape
        return in_half(packed.reshape(half, MAIN_SLOTS, held)).reshape(slots, held)

    def exchanged_beside(packed):
        return lax.cond(lengths[0] > 0, exchanged, jnp.zeros_like, packed)

    own_arrived = exchanged_beside(own_packed)
    far_moe_in, own_arrived = lax.optimization_barrier((far_moe_in, own_arrived))
    far_arrived = exchanged(pack(far_moe_in, far_picks, MIB))
    own_act = expert(own_arrived, w_in, w_down, extras, down=False)
    far_arrived, own_act = lax.optimization_barrier((far_arrived, own_act))
    far_made = expert(far_arrived, w_in, w_down, extras)
    far_made, own_act = lax.optimization_barrier((far_made, own_act))
    far_returned = exchanged(far_made)
    own_made = expert_down(own_act, w_down, *own_packed.shape, extras)
    far_returned, own_made = lax.optimization_barrier((far_returned, own_made))
    far_part, own_made = lax.optimization_barrier((combine(far_returned, far_weights), own_made))
    far_sum = across(far_part)
    own_returned = exchanged_beside(own_made)
    hidden_out = combine(own_returned, own_weights, resid, far_sum)
    kv_cache = landed_pages(pages, page_table, tok_id, n_tok, groups)
    return (hidden_out, kv_cache)


def solution(mesh):
    return jax.shard_map(
        per_device,
        mesh=mesh,
        in_specs=(
            P(("tok", "head"), None),
            P(),
            P(),
            P(None, "head"),
            P("head"),
            P("head", None),
            P(),
            P(("tok", "head"), None),
            P(("tok", "head"), None),
            P(("tok", "head"), None, None),
            P(("tok", "head"), None, None),
            P(),
        ),
        out_specs=(P(("tok", "head"), None), P("head", "tok", None, None)),
        check_vma=False,
    )
```

```python
import functools
import math

import jax
import jax.numpy as jnp
from jax import lax
from jax.experimental import pallas as pl
from jax.experimental.pallas import tpu as pltpu
from jax.sharding import PartitionSpec as P

MODEL_WIDTH = 2880
HEAD_SIZE = 64
EXPERTS = 32
ATTEND_WINDOW = 128
NSEQ = 4
PAGE_TOKENS = 16
QUERY_PER_KEY = 8


EPSILON = 1e-05
ROPE_BASE = 150000.0
GLU_ALPHA = 1.702

LANES = 128
MAIN_SLOTS = 8
PIECE = 768
PIECES = 4
EXTRA_AT = 2944
IN_TILE = 1920
FIRST_COPY = 1
DOWN_COPIES = 4
MIB = 1 << 20


def passed_along(array, axis, by):
    peers = lax.axis_size(axis)
    pairs = [(i, i + by) for i in range(peers) if 0 <= i + by < peers]
    return lax.ppermute(array, axis, pairs)


def segment_ends(lengths_ref):
    ends, end = [], 0
    for k in range(NSEQ):
        end = end + lengths_ref[k]
        ends.append(end)
    return ends


def segment_of(index, ends):
    segment = jnp.zeros_like(index)
    for end in ends:
        segment = segment + jnp.where(index >= end, 1, 0)
    return segment


def rope_tables(index, ends):
    start = jnp.zeros_like(index)
    for end in ends:
        start = jnp.where(index >= end, end, start)
    half = HEAD_SIZE // 2
    lane = lax.broadcasted_iota(jnp.int32, index.shape, 1)
    inv_freq = jnp.exp(
        (lane % half).astype(jnp.float32) * (-2.0 * math.log(ROPE_BASE) / HEAD_SIZE)
    )
    angles = (index - start).astype(jnp.float32) * inv_freq
    low = lane % HEAD_SIZE < half
    sin = jnp.sin(angles)
    return jnp.cos(angles), jnp.where(low, -sin, sin), low, lane


def qkv_kernel(step, chips, ids_ref, lengths_ref, own_ref, other_ref, gain_ref, w_ref, *refs):
    q_ref, kv_ref, xn_ref, cos_ref, sin_ref = refs[-5:]
    rows = own_ref.shape[0]
    core, chip, shard = ids_ref[0], (ids_ref[1] + chips - step) % chips, ids_ref[2]

    @pl.when(pl.program_id(0) == 0)
    def _():
        for at, ref in ((core, own_ref), (1 - core, other_ref)):
            wide = ref[...].astype(jnp.float32)
            inv_rms = lax.rsqrt(jnp.mean(wide * wide, axis=-1, keepdims=True) + EPSILON)
            normed = (wide * inv_rms * gain_ref[...][None]).astype(jnp.bfloat16)
            xn_ref[pl.ds(pl.multiple_of(at * rows, 16), rows), :] = normed
        first = (shard * chips + chip) * 2 * rows
        index = first + lax.broadcasted_iota(jnp.int32, cos_ref.shape, 0)
        cos, sin, _, _ = rope_tables(index, segment_ends(lengths_ref))
        cos_ref[...] = cos
        sin_ref[...] = sin

    projected = jnp.dot(xn_ref[...], w_ref[...], preferred_element_type=jnp.float32)
    cos, sin = cos_ref[...], sin_ref[...]
    lane = lax.broadcasted_iota(jnp.int32, cos.shape, 1)
    low = lane % HEAD_SIZE < HEAD_SIZE // 2

    def turned(u):
        return jnp.where(low, pltpu.roll(u, LANES - 32, 1), pltpu.roll(u, 32, 1))

    for b in range(QUERY_PER_KEY // 2):
        u = projected[:, b * LANES : (b + 1) * LANES]
        q_ref[:, b * LANES : (b + 1) * LANES] = (
            (u * cos + turned(u) * sin) * HEAD_SIZE ** (-0.5)
        ).astype(jnp.bfloat16)
    u = projected[:, QUERY_PER_KEY * HEAD_SIZE :]
    rotated = u * cos + turned(u) * sin
    kv_ref[...] = jnp.where(lane < HEAD_SIZE, rotated, u).astype(jnp.bfloat16)


def project(ids, lengths, step, chips, own, other, gain, weight, earlier):
    rows, width = own.shape
    columns = weight.shape[1]
    group = (QUERY_PER_KEY + 2) * HEAD_SIZE
    qs, kvs = QUERY_PER_KEY * HEAD_SIZE, 2 * HEAD_SIZE
    groups = columns // group
    whole = lambda g, ids: (0, 0)
    by_group = lambda g, ids: ((ids[1] + chips - step) % chips, g)
    return pl.pallas_call(
        functools.partial(qkv_kernel, step, chips),
        grid_spec=pltpu.PrefetchScalarGridSpec(
            num_scalar_prefetch=1,
            grid=(groups,),
            in_specs=[
                pl.BlockSpec(memory_space=pltpu.SMEM),
                pl.BlockSpec((rows, width), whole),
                pl.BlockSpec((rows, width), whole),
                pl.BlockSpec((width,), lambda g, ids: (0,)),
                pl.BlockSpec((width, group), lambda g, ids: (0, g)),
            ]
            + [pl.BlockSpec(memory_space=pl.ANY)] * len(earlier),
            out_specs=[
                pl.BlockSpec((2 * rows, qs), by_group),
                pl.BlockSpec((2 * rows, kvs), by_group),
            ],
            scratch_shapes=[
                pltpu.VMEM((2 * rows, width), jnp.bfloat16),
                pltpu.VMEM((2 * rows, LANES), jnp.float32),
                pltpu.VMEM((2 * rows, LANES), jnp.float32),
            ],
        ),
        out_shape=[
            jax.ShapeDtypeStruct((2 * rows * chips, groups * qs), jnp.bfloat16),
            jax.ShapeDtypeStruct((2 * rows * chips, groups * kvs), jnp.bfloat16),
        ],
        input_output_aliases={6: 0, 7: 1} if earlier else {},
        compiler_params=pltpu.CompilerParams(vmem_limit_bytes=60 * MIB),
        cost_estimate=pl.CostEstimate(
            flops=4 * rows * width * columns, bytes_accessed=2 * width * columns, transcendentals=0
        ),
        name="project",
    )(ids, lengths, own, other, gain, weight, *earlier)


def pack_rows(values_ref, pick_ref, packed_ref):
    packed_ref[:, :EXTRA_AT] = jnp.dot(
        pick_ref[0], values_ref[:, :EXTRA_AT], preferred_element_type=jnp.float32
    ).astype(jnp.bfloat16)
    pieces = jnp.zeros((packed_ref.shape[0], packed_ref.shape[1] - EXTRA_AT), jnp.float32)
    for p in range(pick_ref.shape[0] - 1):
        pieces = pieces + jnp.dot(
            pick_ref[1 + p],
            values_ref[:, p * PIECE : (p + 1) * PIECE],
            preferred_element_type=jnp.float32,
        )
    packed_ref[:, EXTRA_AT:] = pieces.astype(jnp.bfloat16)


def resid_kernel(tokens_ref, own_ref, others_ref, gain_ref, resid_ref, moe_ref):
    resid = tokens_ref[...].astype(jnp.float32) + own_ref[...].astype(jnp.float32)
    for k in range(others_ref.shape[0]):
        resid = resid + others_ref[k].astype(jnp.float32)
    resid_ref[...] = resid
    inv_rms = lax.rsqrt(jnp.mean(resid * resid, axis=-1, keepdims=True) + EPSILON)
    moe_ref[...] = (resid * inv_rms * gain_ref[...][None]).astype(jnp.bfloat16)


def pack_kernel(moe_ref, pick_ref, packed_ref, values_ref):
    width = moe_ref.shape[1]
    values_ref[:, width:] = jnp.zeros_like(values_ref[:, width:])
    values_ref[:, :width] = moe_ref[...]
    pack_rows(values_ref, pick_ref, packed_ref)


def packed_width(extras):
    return EXTRA_AT + PIECE if extras else PIECES * PIECE


def finish_attention(tokens, own, others, gain):
    rows, width = tokens.shape
    return pl.pallas_call(
        resid_kernel,
        out_shape=[
            jax.ShapeDtypeStruct((rows, width), jnp.float32),
            jax.ShapeDtypeStruct((rows, width), jnp.bfloat16),
        ],
        compiler_params=pltpu.CompilerParams(vmem_limit_bytes=32 * MIB),
        name="finish_attention",
    )(tokens, own, others, gain)


def pack(moe_in, picks, beside):
    rows, width = moe_in.shape
    kinds, slots, _ = picks.shape
    return pl.pallas_call(
        pack_kernel,
        out_shape=jax.ShapeDtypeStruct((slots, packed_width(kinds > 1)), jnp.bfloat16),
        scratch_shapes=[pltpu.VMEM((rows, PIECES * PIECE), jnp.bfloat16)],
        compiler_params=pltpu.CompilerParams(vmem_limit_bytes=32 * MIB),
        cost_estimate=pl.CostEstimate(
            flops=2 * slots * rows * 2 * width, bytes_accessed=beside, transcendentals=0
        ),
        name="pack",
    )(moe_in, picks)


def piece_of(count, slots, piece):
    t = lax.broadcasted_iota(jnp.int32, (count, slots), 0)
    r = lax.broadcasted_iota(jnp.int32, (count, slots), 1)
    return jnp.where(r == PIECES * t + piece, 1.0, 0.0).astype(jnp.bfloat16)


def fill_rows(packed_ref, x_ref, extras):
    slots, width = packed_ref.shape[0], x_ref.shape[1]
    x_ref[:slots, :] = packed_ref[:, :width]
    if extras:
        further = slots // PIECES
        for p in range(PIECES):
            extent = min(PIECE, width - p * PIECE)
            x_ref[slots:, p * PIECE : p * PIECE + extent] = jnp.dot(
                piece_of(further, slots, p),
                packed_ref[:, EXTRA_AT : EXTRA_AT + extent],
                preferred_element_type=jnp.float32,
            ).astype(jnp.bfloat16)


def activate(gate_up_ref, act_ref):
    rows, ffs = act_ref.shape
    base = ffs // LANES * LANES
    chunk = 32
    for r in range(0, rows, chunk):
        gate = gate_up_ref[r : r + chunk, :ffs]
        up = gate_up_ref[r : r + chunk, base:]
        if ffs > base:
            up = pltpu.roll(up, up.shape[1] - (ffs - base), 1)
        up = up[:, :ffs]
        act_ref[r : r + chunk, :] = (
            (up + 1.0) * gate * jax.nn.sigmoid(GLU_ALPHA * gate)
        ).astype(jnp.bfloat16)


def put_piece(piece, made, out_ref, width, piece_ref):
    slots = out_ref.shape[0]
    extent = made.shape[1]
    if extent < PIECE:
        out_ref[:, piece * PIECE + extent : (piece + 1) * PIECE] = jnp.zeros(
            (slots, PIECE - extent), jnp.bfloat16
        )
        out_ref[:, piece * PIECE : piece * PIECE + extent] = made[:slots]
    else:
        start = piece * PIECE
        start = start if isinstance(piece, int) else pl.multiple_of(start, LANES)
        out_ref[:, pl.ds(start, extent)] = made[:slots]
    if piece_ref is not None:
        further = slots // PIECES
        t = lax.broadcasted_iota(jnp.int32, (slots, further), 1)
        r = lax.broadcasted_iota(jnp.int32, (slots, further), 0)
        spread = jnp.where(r == PIECES * t + piece, 1.0, 0.0).astype(jnp.bfloat16)
        part = jnp.dot(spread, made[slots:], preferred_element_type=jnp.float32).astype(
            jnp.bfloat16
        )
        if isinstance(piece, int):
            if piece == 0:
                piece_ref[...] = part
            else:
                piece_ref[:, :extent] = piece_ref[:, :extent] + part
            if piece == PIECES - 1:
                out_ref[:, EXTRA_AT:] = piece_ref[...]
            return

        @pl.when(piece == 0)
        def _():
            piece_ref[...] = part

        @pl.when(piece > 0)
        def _():
            piece_ref[...] = piece_ref[...] + part

        @pl.when(piece == PIECES - 1)
        def _():
            out_ref[:, EXTRA_AT:] = piece_ref[...]


def expert_kernel(extras, in_tiles, down, *refs):
    packed_ref, w_in_ref = refs[:2]
    scratch = refs[4:] if down else refs[3:]
    x_ref, gate_up_ref = scratch[:2]
    act_ref = scratch[2] if down else refs[2]
    step = pl.program_id(0)
    copies = []
    if down:
        w_down_ref, out_ref = refs[2:4]
        held_ref, total_ref, sems = scratch[3:6]
        piece_ref = scratch[6] if extras else None
        ffs = held_ref.shape[0]
        rows = pl.cdiv(ffs, DOWN_COPIES * LANES) * LANES
        for c in range(pl.cdiv(ffs, rows)):
            part = pl.ds(c * rows, min(rows, ffs - c * rows))
            copies.append(
                pltpu.make_async_copy(w_down_ref.at[0, part], held_ref.at[part], sems.at[c])
            )

    @pl.when(step == 0)
    def _():
        fill_rows(packed_ref, x_ref, extras)

    for c, copy in enumerate(copies):
        pl.when(step == min(c + FIRST_COPY, in_tiles - 1))(copy.start)

    tile = w_in_ref.shape[2]
    made = jnp.dot(x_ref[...], w_in_ref[0], preferred_element_type=jnp.float32)
    if in_tiles == 1:
        gate_up_ref[...] = made
    else:
        gate_up_ref[:, pl.ds(pl.multiple_of(step * tile, LANES), tile)] = made

    @pl.when(step == in_tiles - 1)
    def _():
        activate(gate_up_ref, act_ref)
        if down:
            width = x_ref.shape[1]
            for c, copy in enumerate(copies):
                copy.wait()
                part = slice(c * rows, min((c + 1) * rows, ffs))
                term = jnp.dot(
                    act_ref[:, part], held_ref[part, :], preferred_element_type=jnp.float32
                )
                total_ref[...] = term if c == 0 else total_ref[...] + term
            for piece in range(PIECES):
                extent = min(PIECE, width - piece * PIECE)
                made = total_ref[:, piece * PIECE : piece * PIECE + extent].astype(jnp.bfloat16)
                put_piece(piece, made, out_ref, width, piece_ref)


def down_kernel(extras, width, act_ref, w_down_ref, out_ref, *scratch):
    piece = pl.program_id(0)
    made = jnp.dot(act_ref[...], w_down_ref[0], preferred_element_type=jnp.float32)
    column = lax.broadcasted_iota(jnp.int32, made.shape, 1) + piece * PIECE
    made = jnp.where(column < width, made, 0.0).astype(jnp.bfloat16)
    put_piece(piece, made, out_ref, width, scratch[0] if extras else None)


def expert(packed, w_in, w_down, extras, down=True):
    slots, held = packed.shape
    width = w_in.shape[1]
    ffs = w_down.shape[1]
    rows = slots + (slots // PIECES if extras else 0)
    tile = min(IN_TILE, 2 * ffs)
    in_tiles = pl.cdiv(2 * ffs, tile)
    whole = lambda i: (0, 0)
    in_specs = [
        pl.BlockSpec((slots, held), whole),
        pl.BlockSpec((1, width, tile), lambda i: (0, 0, i)),
    ]
    scratch = [
        pltpu.VMEM((rows, width), jnp.bfloat16),
        pltpu.VMEM((rows, in_tiles * tile), jnp.float32),
    ]
    args = (packed, w_in)
    out = (rows, ffs)
    if down:
        in_specs += [pl.BlockSpec(memory_space=pl.ANY)]
        scratch += [
            pltpu.VMEM((rows, ffs), jnp.bfloat16),
            pltpu.VMEM((ffs, width), jnp.bfloat16),
            pltpu.VMEM((rows, width), jnp.float32),
            pltpu.SemaphoreType.DMA((DOWN_COPIES,)),
        ]
        scratch += [pltpu.VMEM((slots, PIECE), jnp.bfloat16)] if extras else []
        args += (w_down,)
        out = (slots, held)
    parts = 6 if down else 4
    return pl.pallas_call(
        functools.partial(expert_kernel, extras, in_tiles, down),
        grid=(in_tiles,),
        in_specs=in_specs,
        out_specs=pl.BlockSpec(out, whole),
        out_shape=jax.ShapeDtypeStruct(out, jnp.bfloat16),
        scratch_shapes=scratch,
        compiler_params=pltpu.CompilerParams(vmem_limit_bytes=56 * MIB),
        cost_estimate=pl.CostEstimate(
            flops=parts * rows * width * ffs,
            bytes_accessed=parts * width * ffs,
            transcendentals=rows * ffs,
        ),
        name="expert" if down else "expert_up",
    )(*args)


def expert_down(act, w_down, slots, held, extras):
    rows, ffs = act.shape
    width = w_down.shape[2]
    whole = lambda i: (0, 0)
    return pl.pallas_call(
        functools.partial(down_kernel, extras, width),
        grid=(PIECES,),
        in_specs=[
            pl.BlockSpec((rows, ffs), whole),
            pl.BlockSpec((1, ffs, PIECE), lambda i: (0, 0, i)),
        ],
        out_specs=pl.BlockSpec((slots, held), whole),
        out_shape=jax.ShapeDtypeStruct((slots, held), jnp.bfloat16),
        scratch_shapes=[pltpu.VMEM((slots, PIECE), jnp.bfloat16)] if extras else [],
        compiler_params=pltpu.CompilerParams(vmem_limit_bytes=56 * MIB),
        cost_estimate=pl.CostEstimate(
            flops=2 * rows * width * ffs, bytes_accessed=2 * width * ffs, transcendentals=0
        ),
        name="expert_down",
    )(act, w_down)


def weighted_sum(made_ref, weight_ref, total_ref):
    width = total_ref.shape[1]
    for term in range(2):
        made = jnp.dot(
            weight_ref[term, 0], made_ref[:, :width], preferred_element_type=jnp.float32
        )
        total_ref[...] = made if term == 0 else total_ref[...] + made
        for p in range(weight_ref.shape[1] - 1):
            extent = min(PIECE, width - p * PIECE)
            at = slice(p * PIECE, p * PIECE + extent)
            total_ref[:, at] = total_ref[:, at] + jnp.dot(
                weight_ref[term, 1 + p],
                made_ref[:, EXTRA_AT : EXTRA_AT + extent],
                preferred_element_type=jnp.float32,
            )


def partial_kernel(made_ref, weight_ref, out_ref, total_ref):
    weighted_sum(made_ref, weight_ref, total_ref)
    out_ref[...] = total_ref[...].astype(jnp.bfloat16)


def total_kernel(made_ref, weight_ref, resid_ref, far_ref, out_ref, total_ref):
    weighted_sum(made_ref, weight_ref, total_ref)
    out_ref[...] = (
        resid_ref[...] + (total_ref[...] + far_ref[...].astype(jnp.float32))
    ).astype(jnp.bfloat16)


def combine(made, weights, resid=None, far=None):
    rows = weights.shape[2]
    kernel, more = (partial_kernel, ()) if resid is None else (total_kernel, (resid, far))
    return pl.pallas_call(
        kernel,
        out_shape=jax.ShapeDtypeStruct((rows, MODEL_WIDTH), jnp.bfloat16),
        scratch_shapes=[pltpu.VMEM((rows, MODEL_WIDTH), jnp.float32)],
        compiler_params=pltpu.CompilerParams(vmem_limit_bytes=32 * MIB),
        name="combine",
    )(made, weights, *more)


def slots_kernel(extras, far, half, experts, shards, topk, ids_ref, lengths_ref, choice_ref, *out_refs):
    pick_ref, weight_ref = out_refs
    device = ids_ref[3]
    first_expert = device // half * experts
    _, slots, rows = pick_ref.shape
    source = (device + half) % (2 * half) if far else device
    r = lax.broadcasted_iota(jnp.int32, (slots, rows), 0)
    index = source * rows + lax.broadcasted_iota(jnp.int32, (slots, rows), 1)
    slot = r % MAIN_SLOTS
    own_expert = (first_expert + r // (MAIN_SLOTS * shards)).astype(jnp.float32)
    named = jnp.zeros((slots, rows), jnp.float32)
    gate = jnp.zeros((slots, rows), jnp.float32)
    for k in range(topk):
        here = choice_ref[k : k + 1, :] == own_expert
        named = jnp.where(here, 1.0, named)
        gate = gate + jnp.where(here, choice_ref[topk + k : topk + k + 1, :], 0.0)
    named = jnp.where(index < segment_ends(lengths_ref)[-1], named, 0.0)
    i = lax.broadcasted_iota(jnp.int32, (rows, rows), 0)
    j = lax.broadcasted_iota(jnp.int32, (rows, rows), 1)
    earlier = jnp.where(i < j, 1.0, 0.0).astype(jnp.bfloat16)
    same = jnp.where(i == j, 1.0, 0.0).astype(jnp.bfloat16)
    rank = jnp.dot(named.astype(jnp.bfloat16), earlier, preferred_element_type=jnp.float32)
    rank = jnp.where(named > 0.0, rank, -1.0).astype(jnp.int32)
    high = gate.astype(jnp.bfloat16).astype(jnp.float32)

    def put(hit, pick_at, high_at, low_at):
        pick_at[...] = jnp.where(hit, 1.0, 0.0).astype(jnp.bfloat16)
        for values, at in ((high, high_at), (gate - high, low_at)):
            kept = jnp.where(hit, values, 0.0).astype(jnp.bfloat16)
            at[...] = lax.dot_general(
                same, kept, (((1,), (1,)), ((), ())), preferred_element_type=jnp.float32
            ).astype(jnp.bfloat16)

    put(rank == slot, pick_ref.at[0], weight_ref.at[0, 0], weight_ref.at[1, 0])
    if extras:
        for p in range(PIECES):
            hit = jnp.where(slot % PIECES == p, rank, -2) == MAIN_SLOTS + slot // PIECES
            put(hit, pick_ref.at[1 + p], weight_ref.at[0, 1 + p], weight_ref.at[1, 1 + p])


def slot_tables(ids, lengths, choice, far, half, experts, shards, extras):
    topk, rows = choice.shape[0] // 2, choice.shape[1]
    slots = experts * shards * MAIN_SLOTS
    kinds = 1 + PIECES if extras else 1
    shapes = [(kinds, slots, rows), (2, kinds, rows, slots)]
    smem = pl.BlockSpec(memory_space=pltpu.SMEM)
    return pl.pallas_call(
        functools.partial(slots_kernel, extras, far, half, experts, shards, topk),
        in_specs=[smem, smem, pl.BlockSpec(memory_space=pltpu.VMEM)],
        out_shape=[jax.ShapeDtypeStruct(shape, jnp.bfloat16) for shape in shapes],
        compiler_params=pltpu.CompilerParams(vmem_limit_bytes=32 * MIB),
        name="slots",
    )(ids, lengths, choice)


def attend_kernel(row_count, chips, ids_ref, lengths_ref, q_ref, rim_ref, pair_ref, sink_ref, w_ref, kept_ref, sent_ref, attended_ref):
    def attend_block(block):
        window = rim_ref.shape[0]
        rows = slice(block * window, (block + 1) * window)
        groups = pair_ref.shape[1] // LANES
        core = ids_ref[0]
        ends = segment_ends(lengths_ref)
        first = ids_ref[2] * (chips * 2 * row_count) + block * window
        query = first + lax.broadcasted_iota(jnp.int32, (window, 2 * window), 0)
        key = first - window + lax.broadcasted_iota(jnp.int32, (window, 2 * window), 1)
        query_segment = segment_of(query, ends)
        seen = (query_segment == segment_of(key, ends)) & (query_segment < NSEQ)
        seen = seen & (key >= 0) & (query >= key) & (query - key < window)
        lane = lax.broadcasted_iota(jnp.int32, (2 * window, LANES), 1)
        twos = QUERY_PER_KEY // 2
        for g in range(groups):
            at = slice(g * LANES, (g + 1) * LANES)
            before = pair_ref[(block - 1) * window : block * window, at] if block else rim_ref[:, at]
            pairs = jnp.concatenate([before, pair_ref[rows, at]], axis=0).astype(jnp.float32)
            keys = jnp.where(lane < HEAD_SIZE, pairs, 0.0)
            values = jnp.where(lane < HEAD_SIZE, 0.0, pairs)
            keys = [x.astype(jnp.bfloat16) for x in (keys, pltpu.roll(keys, HEAD_SIZE, 1))]
            values = [x.astype(jnp.bfloat16) for x in (pltpu.roll(values, HEAD_SIZE, 1), values)]
            start = g * twos * LANES
            queries = jnp.concatenate(
                [q_ref[rows, start + two * LANES : start + (two + 1) * LANES] for two in range(twos)],
                axis=0,
            )
            made = jnp.zeros((twos * window, LANES), jnp.float32)
            for side in range(2):
                scores = lax.dot_general(
                    queries, keys[side], (((1,), (1,)), ((), ())), preferred_element_type=jnp.float32
                )
                probs = []
                for two in range(twos):
                    sink = sink_ref[g * QUERY_PER_KEY + 2 * two + side]
                    weights = jnp.where(
                        seen, jnp.exp(scores[two * window : (two + 1) * window]), 0.0
                    )
                    totals = jnp.sum(weights, axis=-1, keepdims=True)
                    totals = totals + jnp.exp(jnp.full_like(totals, sink))
                    probs.append((weights * (1.0 / totals)).astype(jnp.bfloat16))
                made = made + jnp.dot(
                    jnp.concatenate(probs, axis=0), values[side], preferred_element_type=jnp.float32
                )
            made = made.astype(jnp.bfloat16)
            for two in range(twos):
                columns = slice(start + two * LANES, start + (two + 1) * LANES)
                for part in range(window // row_count):
                    head = block * (window // row_count) + part
                    place = (head % 2 + core) % 2 * chips + head // 2
                    row = two * window + part * row_count
                    attended_ref[
                        pl.ds(pl.multiple_of(place * row_count, 16), row_count), columns
                    ] = made[row : row + row_count]

    @pl.when(pl.program_id(0) == 0)
    def _():
        window = rim_ref.shape[0]
        for block in range(q_ref.shape[0] // window):
            attend_block(block)

    product = lax.dot_general(
        attended_ref[...],
        w_ref[...],
        (((1,), (1,)), ((), ())),
        preferred_element_type=jnp.float32,
    )
    for chip in range(chips):
        at, then = chip * row_count, (chips + chip) * row_count
        kept_ref[chip] = product[at : at + row_count].astype(jnp.bfloat16)
        sent_ref[chip] = product[then : then + row_count].astype(jnp.bfloat16)


def attend(ids, lengths, queries, rim, pairs, sinks, w_out, row_count):
    total, columns = queries.shape
    width = w_out.shape[0]
    chips = total // (2 * row_count)
    tile = 2 * PIECE
    whole = lambda i, ids: (0, 0)
    smem = pl.BlockSpec(memory_space=pltpu.SMEM)
    return pl.pallas_call(
        functools.partial(attend_kernel, row_count, chips),
        grid_spec=pltpu.PrefetchScalarGridSpec(
            num_scalar_prefetch=1,
            grid=(pl.cdiv(width, tile),),
            in_specs=[
                smem,
                pl.BlockSpec(queries.shape, whole),
                pl.BlockSpec(rim.shape, whole),
                pl.BlockSpec(pairs.shape, whole),
                smem,
                pl.BlockSpec((tile, columns), lambda i, ids: (i, 0)),
            ],
            out_specs=[pl.BlockSpec((chips, row_count, tile), lambda i, ids: (0, 0, i))] * 2,
            scratch_shapes=[pltpu.VMEM(queries.shape, jnp.bfloat16)],
        ),
        out_shape=[
            jax.ShapeDtypeStruct((chips, row_count, width), jnp.bfloat16),
            jax.ShapeDtypeStruct((chips, row_count, width), jnp.bfloat16),
        ],
        compiler_params=pltpu.CompilerParams(vmem_limit_bytes=60 * MIB),
        cost_estimate=pl.CostEstimate(
            flops=2 * total * columns * width, bytes_accessed=2 * columns * width, transcendentals=0
        ),
        name="attend",
    )(ids, lengths, queries, rim, pairs, sinks, w_out)


def page_order(page_table, n_tok, pages_dev):
    page_grid = page_table.reshape(n_tok, pages_dev)
    target = page_grid // pages_dev
    page_ids = jnp.arange(pages_dev, dtype=jnp.int32)
    earlier = page_ids[:, None] > page_ids[None, :]
    same_dest = target[:, :, None] == target[:, None, :]
    order_rank = jnp.sum((same_dest & earlier[None]).astype(jnp.int32), axis=2)
    return (target, order_rank, page_grid % pages_dev)


def leaving_pages(pairs, page_table, tok_id, n_tok):
    rows = pairs.shape[0]
    groups = pairs.shape[1] // (2 * HEAD_SIZE)
    pages_dev = rows // PAGE_TOKENS
    share_count = pages_dev // n_tok
    paged = pairs.reshape(pages_dev, PAGE_TOKENS, groups, 2 * HEAD_SIZE).transpose(0, 2, 1, 3)
    target, order_rank, _ = page_order(page_table, n_tok, pages_dev)
    dest_ids = jnp.arange(n_tok, dtype=jnp.int32)
    share_ids = jnp.arange(share_count, dtype=jnp.int32)
    page_ids = jnp.arange(pages_dev, dtype=jnp.int32)
    matched = (target[tok_id][:, None, None] == dest_ids[None, :, None]) & (
        order_rank[tok_id][:, None, None] == share_ids[None, None, :]
    )
    pick_page = jnp.sum(jnp.where(matched, page_ids[:, None, None], 0), axis=0).reshape(-1)
    return paged[pick_page].reshape(n_tok, share_count * groups * PAGE_TOKENS, 2 * HEAD_SIZE)


def landed_pages(arrived, page_table, tok_id, n_tok, groups):
    share_count = arrived.shape[1] // (groups * PAGE_TOKENS)
    pages_dev = n_tok * share_count
    arrived = arrived.reshape(pages_dev, groups, PAGE_TOKENS, 2 * HEAD_SIZE)
    target, order_rank, slot_grid = page_order(page_table, n_tok, pages_dev)
    share_ids = jnp.arange(share_count, dtype=jnp.int32)
    page_ids = jnp.arange(pages_dev, dtype=jnp.int32)
    to_here = (target == tok_id)[:, :, None] & (order_rank[:, :, None] == share_ids[None, None, :])
    landing = jnp.sum(jnp.where(to_here, slot_grid[:, :, None], 0), axis=1).reshape(-1)
    source = jnp.sum(
        jnp.where(landing[None, :] == page_ids[:, None], page_ids[None, :], 0), axis=1
    )
    return arrived[source].transpose(1, 0, 2, 3)


def per_device(
    tokens,
    lengths,
    norm_gain_attn,
    query_key_value_weight,
    sinks,
    w_out_attn,
    norm_gain_moe,
    routes,
    gates,
    w_in,
    w_down,
    page_table,
):
    n_tok = lax.axis_size("tok")
    n_head = lax.axis_size("head")
    tok_id = lax.axis_index("tok")
    head_id = lax.axis_index("head")
    row_count, width = tokens.shape
    tok_dev = row_count * n_head
    groups = sinks.shape[0] // QUERY_PER_KEY
    n_y = n_head // 2
    y_id, core = head_id // 2, head_id % 2

    def to_core(array):
        return lax.ppermute(array, "head", [(h, h ^ 1) for h in range(n_head)])

    def along_y(array, by):
        return lax.ppermute(
            array, "head", [(h, (h // 2 + by) % n_y * 2 + h % 2) for h in range(n_head)]
        )

    n_dev = n_tok * n_head
    half = n_dev // 2

    def across(array):
        return lax.ppermute(array, ("tok", "head"), [(d, d ^ half) for d in range(n_dev)])

    def in_half(array):
        return lax.all_to_all(
            array,
            ("tok", "head"),
            split_axis=0,
            concat_axis=0,
            tiled=True,
            axis_index_groups=[list(range(half)), list(range(half, n_dev))],
        )

    flat_id = tok_id * n_head + head_id
    ids = jnp.stack([core, y_id, tok_id, flat_id]).astype(jnp.int32)
    choice = jnp.concatenate([routes.T.astype(jnp.float32), gates.T], axis=0)

    capacity = row_count // 8 + 2
    shards = n_dev // EXPERTS
    extras = capacity > MAIN_SLOTS
    tables = functools.partial(slot_tables, ids, lengths)
    sizes = (half, EXPERTS // 2, shards, extras)
    placed, block = [], tokens
    for k in range(n_y):
        if k:
            block, placed, choice = lax.optimization_barrier((along_y(tokens, k), placed, choice))
        placed = project(
            ids,
            lengths,
            k,
            n_y,
            block,
            to_core(block),
            norm_gain_attn,
            query_key_value_weight,
            placed,
        )
    far_choice = across(choice)
    placed, choice, far_choice = lax.optimization_barrier((placed, choice, far_choice))
    query_rows, key_value_pairs = placed
    rim_rows = passed_along(key_value_pairs[tok_dev - ATTEND_WINDOW :], "tok", 1)
    slots = tables(choice, False, *sizes), tables(far_choice, True, *sizes)
    pages = leaving_pages(key_value_pairs, page_table, tok_id, n_tok)
    rim_rows, slots, pages = lax.optimization_barrier((rim_rows, slots, pages))
    (own_picks, own_weights), (far_picks, far_weights) = slots
    kept, sent = attend(
        ids, lengths, query_rows, rim_rows, key_value_pairs, sinks, w_out_attn.T, row_count
    )
    sent = to_core(sent)

    def chip_sum(kept, sent, chip):
        here = lax.dynamic_index_in_dim(kept, chip, 0, keepdims=False)
        there = lax.dynamic_index_in_dim(sent, chip, 0, keepdims=False)
        return here.astype(jnp.float32) + there.astype(jnp.float32)

    leaving = [chip_sum(kept, sent, (y_id + k) % n_y).astype(jnp.bfloat16) for k in range(1, n_y)]
    leaving, pages, kept, sent = lax.optimization_barrier((leaving, pages, kept, sent))
    other_sums = jnp.stack([along_y(part, k + 1) for k, part in enumerate(leaving)])
    pages = lax.all_to_all(pages, "tok", split_axis=0, concat_axis=0, tiled=True)
    own_sum = chip_sum(kept, sent, y_id)
    other_sums, pages = lax.optimization_barrier((other_sums, pages))

    resid, moe_in = finish_attention(
        tokens, own_sum, other_sums, norm_gain_moe
    )
    far_moe_in = across(moe_in)
    own_packed = pack(moe_in, own_picks, 64 * MIB)

    def exchanged(packed):
        slots, held = packed.shape
        return in_half(packed.reshape(half, MAIN_SLOTS, held)).reshape(slots, held)

    def exchanged_beside(packed):
        return lax.cond(lengths[0] > 0, exchanged, jnp.zeros_like, packed)

    own_arrived = exchanged_beside(own_packed)
    far_moe_in, own_arrived = lax.optimization_barrier((far_moe_in, own_arrived))
    far_arrived = exchanged(pack(far_moe_in, far_picks, MIB))
    own_act = expert(own_arrived, w_in, w_down, extras, down=False)
    far_arrived, own_act = lax.optimization_barrier((far_arrived, own_act))
    far_made = expert(far_arrived, w_in, w_down, extras)
    far_made, own_act = lax.optimization_barrier((far_made, own_act))
    far_returned = exchanged(far_made)
    own_made = expert_down(own_act, w_down, *own_packed.shape, extras)
    far_returned, own_made = lax.optimization_barrier((far_returned, own_made))
    far_part, own_made = lax.optimization_barrier((combine(far_returned, far_weights), own_made))
    far_sum = across(far_part)
    own_returned = exchanged_beside(own_made)
    hidden_out = combine(own_returned, own_weights, resid, far_sum)
    kv_cache = landed_pages(pages, page_table, tok_id, n_tok, groups)
    return (hidden_out, kv_cache)


def solution(mesh):
    return jax.shard_map(
        per_device,
        mesh=mesh,
        in_specs=(
            P(("tok", "head"), None),
            P(),
            P(),
            P(None, "head"),
            P("head"),
            P("head", None),
            P(),
            P(("tok", "head"), None),
            P(("tok", "head"), None),
            P(("tok", "head"), None, None),
            P(("tok", "head"), None, None),
            P(),
        ),
        out_specs=(P(("tok", "head"), None), P("head", "tok", None, None)),
        check_vma=False,
    )
```
